32 devices in a mesh: section: 2 (over y), fsdp: 16 (over z, x, core).
Axes of the slice: x: 2, y: 2, z: 4, core: 2. Of those that a mesh axis runs over, the one named last changes fastest.
Arguments:
- tokens: bfloat16 [32, 128, 1280], P('fsdp'), may hold values from -6 to 6
- cotangent: bfloat16 [32, 128, 1280], P('fsdp'), may hold values from -6 to 6
- lengths: int32 [32], P('fsdp'), may hold values from 32 to 128, as said below
- qkv_weight: float32 [2, 1280, 3840], P('section', 'fsdp'), may hold values from -0.15625 to 0.15625
- out_weight: float32 [2, 1280, 1280], P('section', 'fsdp'), may hold values from -1 to 1
- up_weight: float32 [2, 1280, 1280], P('section', 'fsdp'), may hold values from -0.15625 to 0.15625
- down_weight: float32 [2, 1280, 1280], P('section', 'fsdp'), may hold values from -0.15625 to 0.15625
- norm_gains: float32 [2, 1280, 2], P('section', 'fsdp'), may hold values from 0.5 to 1.5
- query_gain: float32 [2, 80], P('section'), may hold values from -1 to 1
Outputs:
- output: bfloat16 [32, 128, 1280], P('fsdp', None, 'section')
- d_tokens: bfloat16 [32, 128, 1280], P('fsdp', None, 'section')
- d_qkv_weight: float32 [2, 1280, 3840], P('section', 'fsdp')
- d_out_weight: float32 [2, 1280, 1280], P('section', 'fsdp')
- d_up_weight: float32 [2, 1280, 1280], P('section', 'fsdp')
- d_down_weight: float32 [2, 1280, 1280], P('section', 'fsdp')
- d_norm_gains: float32 [2, 1280, 2], P('section', 'fsdp')
- d_query_gain: float32 [2, 80], P('section')
The draws below stay inside these ranges and needn't reach their ends.
Inputs may be any that keep to these rules, and one draw needn't show every extreme that they name: `lengths`: live tokens of each sequence, counted from its start; the first sequence is always full (128).
All inputs are finite; a program needn't handle non-finite values.
Results may differ from the reference program's by a relative error of at most 0.019.
Values may be sent and summed in bfloat16 or wider, within the bound.
A program may use at most 192 MiB of HBM per device.

```python
import math
import jax
import jax.numpy as jnp
from jax import lax

D = 1280
H = 16
HD = 80
FF = 1280
SLOT = 128
MINLEN = 32
SEQS = 32
N_SECTION = 2


def draw_lengths(key, part):
    key = jax.random.fold_in(key, 11)
    key_full, key_value = jax.random.split(key)
    full_flag = jax.random.randint(key_full, (SEQS,), 0, 2)
    values = jax.random.randint(key_value, (SEQS,), MINLEN, SLOT + 1)
    picked = jnp.where(full_flag == 1, SLOT, values)
    first = jnp.arange(SEQS) == 0
    return jnp.where(first, SLOT, picked).astype(jnp.int32)


def shard_levels(stream_key, dims, cuts, low, top_value):
    loudness = 1.0
    for dim, parts in cuts:
        heights = jax.random.uniform(jax.random.fold_in(jax.random.fold_in(stream_key, 6), dim), (parts,), jnp.float32, low / len(cuts), top_value / len(cuts))
        loudness = loudness * jnp.repeat(jnp.exp(heights), dims[dim] // parts).reshape((-1,) + (1,) * (len(dims) - 1 - dim))
    return loudness


def scatter_about(key, extent, spread, bound, cuts=(), kind=jnp.bfloat16):
    gain = shard_levels(key, extent, cuts, -0.22, 0.18) if cuts else 1.0
    array = jax.random.normal(key, extent, jnp.float32) * spread * gain
    return jnp.minimum(jnp.maximum(array, -bound), bound).astype(kind)


def setup_inputs(seed: int = 0) -> dict:
    arg_keys = jax.random.split(jax.random.key(seed), 10)
    tokens = scatter_about(arg_keys[0], (SEQS, SLOT, D), 1.0, 6.0, ((0, 16),))
    cotangent = scatter_about(arg_keys[1], (SEQS, SLOT, D), 1.0, 6.0, ((0, 16),))
    lengths = draw_lengths(jax.random.fold_in(arg_keys[9], 71), 0)
    qkv_weight = scatter_about(arg_keys[3], (N_SECTION, D, 3 * D), D ** -0.5, 0.15625, ((0, 2), (1, 16)), jnp.float32)
    out_weight = scatter_about(arg_keys[4], (N_SECTION, D, D), (D // 32) ** -0.5, 1.0, ((0, 2), (1, 16)), jnp.float32)
    up_weight = scatter_about(arg_keys[5], (N_SECTION, D, FF), D ** -0.5, 0.15625, ((0, 2), (1, 16)), jnp.float32)
    down_weight = scatter_about(arg_keys[6], (N_SECTION, FF, D), FF ** -0.5, 0.15625, ((0, 2), (1, 16)), jnp.float32)
    norm_gains = jnp.clip(1.0 + 0.1 * jax.random.normal(arg_keys[7], (N_SECTION, D, 2), jnp.float32), 0.5, 1.5)
    query_gain = jnp.clip(jax.random.uniform(arg_keys[8], (N_SECTION, HD), jnp.float32, -1.0, 1.0) * shard_levels(arg_keys[8], (N_SECTION, HD), ((0, 2),), -0.4, 0.0), -1.0, 1.0)
    return {"tokens": tokens, "cotangent": cotangent, "lengths": lengths, "qkv_weight": qkv_weight, "out_weight": out_weight, "up_weight": up_weight, "down_weight": down_weight, "norm_gains": norm_gains, "query_gain": query_gain}


NORM_EPS = 1e-06
NEG_FILL = -1e+30
LOG_BASE = 1.442695041

@jax.custom_vjp
def low(v):
    return lax.optimization_barrier(v.astype(jnp.bfloat16)).astype(jnp.float32)

@jax.custom_vjp
def low_back(v):
    return v

def low_keep(v):
    return (low(v), None)

def low_pass(kept, grad):
    return (grad,)

def back_keep(v):
    return (v, None)

def back_low(kept, grad):
    return (low(grad),)
low.defvjp(low_keep, low_pass)
low_back.defvjp(back_keep, back_low)

def layer_sequence(hidden_in, length, qkv_w, out_w, up_w, down_w, gain_pair, gain_param):
    high = lax.Precision.HIGHEST
    qkv_w = low(qkv_w)
    out_w = low(out_w)
    up_w = low(up_w)
    down_w = low(down_w)
    gain_pair = low(gain_pair)
    query_scale = jax.nn.softplus(gain_param) * (LOG_BASE / math.sqrt(HD))
    recip_one = lax.rsqrt(lax.optimization_barrier(jnp.mean(hidden_in * hidden_in, -1, keepdims=True)) + NORM_EPS)
    normed = low(hidden_in * recip_one * gain_pair[:, 0])
    proj = jnp.dot(normed, qkv_w, precision=high, preferred_element_type=jnp.float32)
    query = low_back(proj[:, :D]).reshape(SLOT, H, HD)
    query_b = low(query * query_scale)
    keys_b = low(low_back(proj[:, D:2 * D])).reshape(SLOT, H, HD)
    values_b = low(low_back(proj[:, 2 * D:])).reshape(SLOT, H, HD)
    scores = low_back(jnp.einsum('qhd,khd->hqk', query_b, keys_b, precision=high))
    row_ids = lax.broadcasted_iota(jnp.int32, (SLOT, SLOT), 0)
    col_ids = lax.broadcasted_iota(jnp.int32, (SLOT, SLOT), 1)
    allowed = (col_ids <= row_ids) & (col_ids < length)
    scores = jnp.where(allowed[None], scores, NEG_FILL)
    row_peak = lax.optimization_barrier(jnp.max(scores, -1, keepdims=True))
    expd = jnp.exp(scores - row_peak)
    probs = expd / lax.optimization_barrier(jnp.sum(expd, -1, keepdims=True))
    attended = jnp.einsum('hqk,khd->qhd', low(probs), values_b, precision=high).reshape(SLOT, D)
    attended = low(low_back(attended))
    middle = hidden_in + low_back(jnp.dot(attended, out_w, precision=high, preferred_element_type=jnp.float32))
    recip_two = lax.rsqrt(lax.optimization_barrier(jnp.mean(middle * middle, -1, keepdims=True)) + NORM_EPS)
    normed_two = low(middle * recip_two * gain_pair[:, 1])
    upper = low_back(jnp.dot(normed_two, up_w, precision=high, preferred_element_type=jnp.float32))
    hidden = low(jax.nn.silu(upper))
    return middle + low_back(jnp.dot(hidden, down_w, precision=high, preferred_element_type=jnp.float32))

def both_layers(token_group, length_group, param_set):
    hidden_state = token_group
    for layer_index in range(N_SECTION):
        layer_params = tuple((item[layer_index] for item in param_set))
        result = jax.vmap(layer_sequence, in_axes=(0, 0, None, None, None, None, None, None))(hidden_state, length_group, *layer_params)
        if layer_index + 1 < N_SECTION:
            hidden_state = low(low_back(result))
        else:
            hidden_state = result
    return hidden_state

def reference(tokens, cotangent, lengths, qkv_weight, out_weight, up_weight, down_weight, norm_gains, query_gain):
    group_size = math.gcd(SEQS, max(1, 4096 // SLOT))
    group_count = SEQS // group_size
    params = (qkv_weight, out_weight, up_weight, down_weight, norm_gains, query_gain)
    row_ids = jnp.arange(SLOT, dtype=jnp.int32)

    def one_group(carry, item):
        token_group, cot_group, length_group = item
        live_rows = (row_ids[None, :] < length_group[:, None]).astype(jnp.float32)[..., None]

        def forward_fn(token_arg, param_arg):
            return both_layers(token_arg, length_group, param_arg)
        result, pull = jax.vjp(forward_fn, token_group.astype(jnp.float32), params)
        d_group, d_params = pull(cot_group.astype(jnp.float32) * live_rows)
        carry = jax.tree.map(jnp.add, carry, d_params)
        return (carry, (result.astype(jnp.bfloat16), d_group.astype(jnp.bfloat16)))
    zeros = jax.tree.map(jnp.zeros_like, params)
    items = (tokens.reshape(group_count, group_size, SLOT, D), cotangent.reshape(group_count, group_size, SLOT, D), lengths.reshape(group_count, group_size))
    totals, (outputs, d_groups) = lax.scan(one_group, zeros, items)
    return (outputs.reshape(SEQS, SLOT, D), d_groups.reshape(SEQS, SLOT, D), totals[0], totals[1], totals[2], totals[3], totals[4], totals[5])
```

```python
import math

import jax
import jax.numpy as jnp
from jax import lax
from jax.experimental import pallas as pl
from jax.experimental.pallas import tpu as pltpu
from jax.sharding import PartitionSpec as P

H = 16
HD = 80


NORM_EPS = 1e-06
NEG_FILL = -1e30
LOG_BASE = 1.442695041


MESH_ID = pl.DeviceIdType.MESH
BF16 = jnp.bfloat16
F32 = jnp.float32
NZ = 4
FIRST = 0


def place():
    s, f = lax.axis_index("section"), lax.axis_index("fsdp")
    return s, f // 4, (f // 2) % 2, f % 2


def device(s, z, x, c):
    return (s, z * 4 + x * 2 + c)


def piece_rows(z, x, c, n):
    return pl.ds(pl.multiple_of((z * 4 + x * 2 + c) * n, 16), n)


def inside(z):
    return (z >= 0) & (z < NZ)


def neighbour_barrier(s, z, x, c):
    barrier = pltpu.get_barrier_semaphore()

    def tell(target):
        pl.semaphore_signal(barrier, inc=1, device_id=target, device_id_type=MESH_ID)

    tell(device(s, z, x, 1 - c))
    tell(device(s, z, 1 - x, c))
    pl.when(z > 0)(lambda: tell(device(s, z - 1, x, c)))
    pl.when(z < NZ - 1)(lambda: tell(device(s, z + 1, x, c)))
    pl.semaphore_wait(barrier, 2 + (z > 0).astype(jnp.int32) + (z < NZ - 1).astype(jnp.int32))


def gather_engine(s, z, x, c, n, held, send_sem, recv_sem, core_send, core_recv):
    sent = []

    def copy(p, zz, xx, target, sem_s, sem_r, cc=c):
        rows = piece_rows(zz, xx, cc, n)
        return pltpu.make_async_remote_copy(
            held.at[p, rows], held.at[p, rows], sem_s, sem_r, device_id=target, device_id_type=MESH_ID
        )

    def ship(p, zz, xx, way, cond=None):
        i = zz * 2 + xx
        target = (
            device(s, jnp.minimum(z + 1, NZ - 1), x, c),
            device(s, jnp.maximum(z - 1, 0), x, c),
            device(s, z, 1 - x, c),
            device(s, z, x, 1 - c),
        )[way]
        if way < 3:
            cp = copy(p, zz, xx, target, send_sem.at[p, i, way], recv_sem.at[p, i])
        else:
            cp = copy(p, zz, xx, target, core_send.at[p, i], core_recv.at[p, i])
        if cond is None:
            cp.start()
        else:
            pl.when(cond)(cp.start)
        sent.append((cp, cond))

    def arrived(p, zz, xx):
        copy(p, zz, xx, device(s, z, 1 - x, c), send_sem.at[p, 0, 0], recv_sem.at[p, zz * 2 + xx]).wait_recv()

    def own(p):
        for way, cond in ((0, z < NZ - 1), (1, z > 0), (2, None), (3, None)):
            ship(p, z, x, way, cond)

    def relay(p, cols):
        for d in range(1, NZ):
            for sign, way in ((-1, 0), (1, 1)):
                zz = z + sign * d
                here = inside(zz)
                zc = jnp.clip(zz, 0, NZ - 1)
                for xx in cols:
                    pl.when(here)(lambda xx=xx: arrived(p, zc, xx))
                    ship(p, zc, xx, way, here & inside(z - sign))
                    if len(cols) == 1:
                        ship(p, zc, xx, 2, here)
                    ship(p, zc, xx, 3, here)

    def across_first(p):
        arrived(p, z, 1 - x)
        ship(p, z, 1 - x, 0, z < NZ - 1)
        ship(p, z, 1 - x, 1, z > 0)
        ship(p, z, 1 - x, 3)

    def across(p):
        for d in range(NZ):
            for sign in (-1, 1) if d else (1,):
                zz = z + sign * d
                here = inside(zz)
                zc = jnp.clip(zz, 0, NZ - 1)
                pl.when(here)(lambda: arrived(p, zc, 1 - x))
                ship(p, zc, 1 - x, 3, here)

    def finish(p):
        for zz in range(NZ):
            for xx in range(2):
                copy(p, zz, xx, device(s, z, x, 1 - c), core_send.at[p, 0], core_recv.at[p, zz * 2 + xx], 1 - c).wait_recv()

    def drain():
        for cp, cond in sent:
            if cond is None:
                cp.wait_send()
            else:
                pl.when(cond)(cp.wait_send)

    return own, relay, across_first, across, finish, drain


def gather_kernel(n, wq, wo, wu, wd, held, send_sem, recv_sem, core_send, core_recv):
    s, z, x, c = place()
    width = wo.shape[-1]
    mine = piece_rows(z, x, c, n)
    for k in range(3):
        held[k, mine] = wq[:, k * width : (k + 1) * width].astype(BF16)
    for k, ref in enumerate((wo, wu, wd)):
        held[3 + k, mine] = ref[...].astype(BF16)
    neighbour_barrier(s, z, x, c)
    own, relay, across_first, across, finish, drain = gather_engine(
        s, z, x, c, n, held, send_sem, recv_sem, core_send, core_recv
    )
    own(0)
    for p in range(6):
        if p + 1 < 6:
            own(p + 1)
        if p == FIRST:
            across_first(p)
            relay(p, (x, 1 - x))
        else:
            relay(p, (x,))
        if p > 0 and p - 1 != FIRST:
            across(p - 1)
    if FIRST != 5:
        across(5)
    for p in range(6):
        finish(p)
    drain()


def gather_pieces(wq, wo, wu, wd):
    n, width = wo.shape
    dma = pltpu.SemaphoreType.DMA
    return pl.pallas_call(
        lambda *refs: gather_kernel(n, *refs),
        out_shape=jax.ShapeDtypeStruct((6, n * 16, width), BF16),
        in_specs=[pl.BlockSpec(memory_space=pltpu.VMEM)] * 4,
        out_specs=pl.BlockSpec(memory_space=pltpu.VMEM),
        scratch_shapes=[dma((6, 8, 3)), dma((6, 8)), dma((6, 8)), dma((6, 8))],
        compiler_params=pltpu.CompilerParams(collective_id=1, has_side_effects=True, vmem_limit_bytes=40 << 20),
        name="gather_weights",
    )(wq, wo, wu, wd)


def add_block(dst, src):
    n = dst.shape[0]

    @pl.loop(0, n // 16)
    def _(k):
        r = pl.ds(pl.multiple_of(k * 16, 16), 16)
        dst[r] = (dst[r].astype(F32) + src[r].astype(F32)).astype(BF16)


def scatter_engine(s, z, x, c, n, part, got_core, got_x, got_z, got_zz, out_store, sems):
    core_s, core_r, x_s, x_r, z_s, z_r = sems
    sent = []

    def begin(cp, cond=None):
        if cond is None:
            cp.start()
        else:
            pl.when(cond)(cp.start)
        sent.append((cp, cond))

    def remote(src, dst, a, b, target):
        return pltpu.make_async_remote_copy(src, dst, a, b, device_id=target, device_id_type=MESH_ID)

    other = device(s, z, x, 1 - c)
    side = device(s, z, 1 - x, c)

    def core_copy(p, i):
        rows = piece_rows(i // 2, i % 2, 1 - c, n)
        return remote(part.at[p, rows], got_core.at[p, i], core_s.at[p, i], core_r.at[p, i], other)

    def core_send(p):
        for i in range(8):
            begin(core_copy(p, i))

    def core_add(p):
        for i in range(8):
            core_copy(p, i).wait_recv()
            add_block(part.at[p, piece_rows(i // 2, i % 2, c, n)], got_core.at[p, i])

    def walk(fn):
        for d in range(NZ - 1, 0, -1):
            for sign in (1, -1):
                zz = z + sign * d
                fn(jnp.clip(zz, 0, NZ - 1), inside(zz), sign)

    def x_copy(p, zz):
        return remote(
            part.at[p, piece_rows(zz, 1 - x, c, n)], got_x.at[p, zz], x_s.at[p, zz], x_r.at[p, zz], side
        )

    def x_send(p):
        walk(lambda zz, here, sign: begin(x_copy(p, zz), here))
        begin(x_copy(p, z))

    def x_add(p, zz):
        x_copy(p, zz).wait_recv()
        add_block(part.at[p, piece_rows(zz, x, c, n)], got_x.at[p, zz])

    def z_copy(p, zz, xx, sign, slot, buf):
        target = device(s, jnp.clip(z + sign, 0, NZ - 1), x, c)
        return remote(
            part.at[p, piece_rows(zz, xx, c, n)], buf(slot, xx), z_s.at[p, xx, zz], z_r.at[p, xx, slot], target
        )

    def buffer(p):
        if p == FIRST:
            return lambda slot, xx: got_zz.at[xx, slot]
        return lambda slot, xx: got_z.at[p, slot]

    def slot_there(zz, sign):
        return jnp.where((sign < 0) & (z + sign == zz), NZ, zz)

    def z_chain(p, cols, before=None):
        buf = buffer(p)

        def step(zz, here, sign):
            def go():
                if before is not None:
                    before(zz)
                for xx in cols:
                    def take(xx=xx):
                        z_copy(p, zz, xx, sign, zz, buf).wait_recv()
                        add_block(part.at[p, piece_rows(zz, xx, c, n)], buf(zz, xx))

                    pl.when(inside(z - sign))(take)
                    z_copy(p, zz, xx, sign, slot_there(zz, sign), buf).start()

            pl.when(here)(go)
            for xx in cols:
                sent.append((z_copy(p, zz, xx, sign, slot_there(zz, sign), buf), here))

        walk(step)

    def z_last(p, xx):
        buf = buffer(p)
        mine = part.at[p, piece_rows(z, xx, c, n)]

        def take(slot):
            z_copy(p, z, xx, 1, slot, buf).wait_recv()
            add_block(mine, buf(slot, xx))

        pl.when(z > 0)(lambda: take(z))
        pl.when(z < NZ - 1)(lambda: take(NZ))

    def total(p, pieces):
        @pl.loop(0, n // 16)
        def _(k):
            r = pl.ds(pl.multiple_of(k * 16, 16), 16)
            value = part[p, piece_rows(z, x, c, n)] if False else part.at[p, piece_rows(z, x, c, n)][r].astype(F32)
            out_store(p, r, value)

    def serve(p):
        if p == FIRST:
            z_chain(p, (x, 1 - x))
            z_last(p, 1 - x)
            begin(x_copy(p, z))
            z_last(p, x)
            x_add(p, z)
        else:
            z_chain(p, (x,), before=lambda zz: x_add(p, zz))
            x_add(p, z)
            z_last(p, x)
        total(p, None)

    def drain():
        for cp, cond in sent:
            if cond is None:
                cp.wait_send()
            else:
                pl.when(cond)(cp.wait_send)

    return core_send, core_add, x_send, serve, drain


def scatter_kernel(n, grads, dq, do, du, dd, part, got_core, got_x, got_z, got_zz, load_sem, *sems):
    s, z, x, c = place()
    width = do.shape[-1]
    loads = [pltpu.make_async_copy(grads.at[p], part.at[p], load_sem.at[p]) for p in range(6)]
    for ld in loads:
        ld.start()

    def out_store(p, r, value):
        if p < 3:
            dq[r, p * width : (p + 1) * width] = value
        else:
            (do, du, dd)[p - 3][r] = value

    neighbour_barrier(s, z, x, c)
    core_send, core_add, x_send, serve, drain = scatter_engine(
        s, z, x, c, n, part, got_core, got_x, got_z, got_zz, out_store, sems
    )
    order = [FIRST] + [p for p in range(6) if p != FIRST]
    for k in range(2):
        loads[order[k]].wait()
        core_send(order[k])
    for k, p in enumerate(order):
        if k + 2 < 6:
            loads[order[k + 2]].wait()
            core_send(order[k + 2])
        core_add(p)
        if p != FIRST:
            x_send(p)
        if k > 0:
            serve(order[k - 1])
    serve(order[5])
    drain()


def scatter_pieces(grads):
    rows, width = grads.shape[1:]
    n = rows // 16
    dma = pltpu.SemaphoreType.DMA
    block = (n, width)
    return pl.pallas_call(
        lambda *refs: scatter_kernel(n, *refs),
        out_shape=(
            jax.ShapeDtypeStruct((n, 3 * width), F32),
            jax.ShapeDtypeStruct(block, F32),
            jax.ShapeDtypeStruct(block, F32),
            jax.ShapeDtypeStruct(block, F32),
        ),
        in_specs=[pl.BlockSpec(memory_space=pl.ANY)],
        out_specs=(pl.BlockSpec(memory_space=pltpu.VMEM),) * 4,
        scratch_shapes=[
            pltpu.VMEM((6, rows, width), BF16),
            pltpu.VMEM((6, 8) + block, BF16),
            pltpu.VMEM((6, 4) + block, BF16),
            pltpu.VMEM((6, 5) + block, BF16),
            pltpu.VMEM((2, 5) + block, BF16),
            dma((6,)),
            dma((6, 8)),
            dma((6, 8)),
            dma((6, 4)),
            dma((6, 4)),
            dma((6, 2, 4)),
            dma((6, 2, 5)),
        ],
        compiler_params=pltpu.CompilerParams(collective_id=2, has_side_effects=True, vmem_limit_bytes=56 << 20),
        name="scatter_gradients",
    )(grads)


def swapped(value, axis, bit):
    return lax.ppermute(value, axis, [(i, i ^ 1 << bit) for i in range(lax.axis_size(axis))])


def causal_allowed(row_count, length):
    row_ids = lax.broadcasted_iota(jnp.int32, (row_count, row_count), 0)
    col_ids = lax.broadcasted_iota(jnp.int32, (row_count, row_count), 1)
    return (col_ids <= row_ids) & (col_ids < length)


def contract_rows(left, right):
    return lax.dot_general(
        left, right, (((0,), (0,)), ((), ())), preferred_element_type=jnp.float32
    )


def contract_cols(left, right):
    return lax.dot_general(
        left, right, (((1,), (1,)), ((), ())), preferred_element_type=jnp.float32
    )


def norm_back(source, recip, grad_flat):
    return recip * grad_flat - source * recip**3 * jnp.mean(grad_flat * source, -1, keepdims=True)


def layer_forward(layer_input, length, weights, query_scale):
    qkv_w, out_w, up_w, down_w, gain_pair = weights
    row_count, width = layer_input.shape
    gain_one = gain_pair[:, 0].astype(jnp.float32)
    gain_two = gain_pair[:, 1].astype(jnp.float32)
    recip_one = lax.rsqrt(jnp.mean(layer_input * layer_input, -1, keepdims=True) + NORM_EPS)
    normed = (layer_input * recip_one * gain_one).astype(jnp.bfloat16)
    proj = jnp.dot(normed, qkv_w, preferred_element_type=jnp.float32)
    query = proj[:, :width].reshape(row_count, H, HD)
    query_b = (query * query_scale).astype(jnp.bfloat16)
    keys_b = proj[:, width : 2 * width].astype(jnp.bfloat16).reshape(row_count, H, HD)
    values_b = proj[:, 2 * width :].astype(jnp.bfloat16).reshape(row_count, H, HD)
    scores = jnp.einsum("qhd,khd->hqk", query_b, keys_b, preferred_element_type=jnp.float32)
    scores = jnp.where(causal_allowed(row_count, length)[None], scores, NEG_FILL)
    row_peak = jnp.max(scores, -1, keepdims=True)
    expd = jnp.exp(scores - row_peak)
    row_total = jnp.sum(expd, -1, keepdims=True)
    probs = expd / row_total
    logsum = (row_peak + jnp.log(row_total))[..., 0]
    attended = (
        jnp.einsum(
            "hqk,khd->qhd", probs.astype(jnp.bfloat16), values_b, preferred_element_type=jnp.float32
        )
        .reshape(row_count, width)
        .astype(jnp.bfloat16)
    )
    middle = layer_input + jnp.dot(attended, out_w, preferred_element_type=jnp.float32)
    recip_two = lax.rsqrt(jnp.mean(middle * middle, -1, keepdims=True) + NORM_EPS)
    normed_two = (middle * recip_two * gain_two).astype(jnp.bfloat16)
    upper = jnp.dot(normed_two, up_w, preferred_element_type=jnp.float32)
    hidden = jax.nn.silu(upper).astype(jnp.bfloat16)
    layer_output = middle + jnp.dot(hidden, down_w, preferred_element_type=jnp.float32)
    saved = (
        layer_input,
        normed,
        query,
        query_b,
        keys_b,
        values_b,
        logsum,
        attended,
        middle,
        normed_two,
        upper,
        hidden,
        recip_one,
        recip_two,
    )
    return (layer_output, saved)


def layer_backward(saved, length, weights, query_scale, grad_output):
    qkv_w, out_w, up_w, down_w, gain_pair = weights
    (
        layer_input,
        normed,
        query,
        query_b,
        keys_b,
        values_b,
        logsum,
        attended,
        middle,
        normed_two,
        upper,
        hidden,
        recip_one,
        recip_two,
    ) = saved
    row_count, width = layer_input.shape
    gain_one = gain_pair[:, 0].astype(jnp.float32)
    gain_two = gain_pair[:, 1].astype(jnp.float32)
    grad_low = grad_output.astype(jnp.bfloat16)
    d_down = contract_rows(hidden, grad_low)
    d_hidden = contract_cols(grad_low, down_w)
    sigmoid_up = jax.nn.sigmoid(upper)
    d_upper = (d_hidden * sigmoid_up * (1.0 + upper * (1.0 - sigmoid_up))).astype(jnp.bfloat16)
    d_up = contract_rows(normed_two, d_upper)
    d_normed_two = contract_cols(d_upper, up_w)
    d_gain_two = jnp.sum(d_normed_two * middle * recip_two, 0)
    d_middle = grad_output + norm_back(middle, recip_two, d_normed_two * gain_two)
    middle_low = d_middle.astype(jnp.bfloat16)
    d_out = contract_rows(attended, middle_low)
    d_attended = contract_cols(middle_low, out_w).astype(jnp.bfloat16).reshape(row_count, H, HD)
    scores = jnp.einsum("qhd,khd->hqk", query_b, keys_b, preferred_element_type=jnp.float32)
    scores = jnp.where(causal_allowed(row_count, length)[None], scores, NEG_FILL)
    probs = jnp.exp(scores - logsum[..., None])
    d_probs = jnp.einsum("qhd,khd->hqk", d_attended, values_b, preferred_element_type=jnp.float32)
    d_values = jnp.einsum(
        "hqk,qhd->khd", probs.astype(jnp.bfloat16), d_attended, preferred_element_type=jnp.float32
    ).astype(jnp.bfloat16)
    d_scores = (probs * (d_probs - jnp.sum(probs * d_probs, -1, keepdims=True))).astype(
        jnp.bfloat16
    )
    d_query_s = jnp.einsum("hqk,khd->qhd", d_scores, keys_b, preferred_element_type=jnp.float32)
    d_keys = jnp.einsum(
        "hqk,qhd->khd", d_scores, query_b, preferred_element_type=jnp.float32
    ).astype(jnp.bfloat16)
    d_scale = jnp.sum(d_query_s * query, (0, 1))
    d_query = (d_query_s * query_scale).astype(jnp.bfloat16)
    d_proj = jnp.concatenate(
        [
            d_query.reshape(row_count, width),
            d_keys.reshape(row_count, width),
            d_values.reshape(row_count, width),
        ],
        -1,
    )
    d_qkv = contract_rows(normed, d_proj)
    d_normed = contract_cols(d_proj, qkv_w)
    d_gain_one = jnp.sum(d_normed * layer_input * recip_one, 0)
    d_input = d_middle + norm_back(layer_input, recip_one, d_normed * gain_one)
    d_gains = jnp.stack([d_gain_one, d_gain_two], -1)
    return (d_input, (d_qkv, d_out, d_up, d_down, d_gains), d_scale)


def shards(
    tokens,
    cotangent,
    lengths,
    qkv_weight,
    out_weight,
    up_weight,
    down_weight,
    norm_gains,
    query_gain,
):
    near = lax.axis_size("fsdp") == 16
    section_index = lax.axis_index("section")
    micro_count, slot_rows, width = tokens.shape
    half_width = width // 2
    scale_factor = LOG_BASE / math.sqrt(HD)
    query_scale = jax.nn.softplus(query_gain[0]) * scale_factor

    def gather_weights():
        pieces = (
            lax.all_gather(qkv_weight.astype(jnp.bfloat16), "fsdp", axis=1, tiled=True),
            lax.all_gather(out_weight.astype(jnp.bfloat16), "fsdp", axis=1, tiled=True),
            lax.all_gather(up_weight.astype(jnp.bfloat16), "fsdp", axis=1, tiled=True),
            lax.all_gather(down_weight.astype(jnp.bfloat16), "fsdp", axis=1, tiled=True),
            lax.all_gather(norm_gains.astype(jnp.bfloat16), "fsdp", axis=1, tiled=True),
        )
        return tuple((piece[0] for piece in pieces))

    def handoff(value):
        return swapped(value, "section", 0)

    gains = lax.all_gather(norm_gains.astype(jnp.bfloat16), "fsdp", axis=1, tiled=True)[0]
    if near:
        held = gather_pieces(qkv_weight[0], out_weight[0], up_weight[0], down_weight[0])
        weights = (jnp.concatenate([held[0], held[1], held[2]], -1), held[3], held[4], held[5], gains)
    else:
        weights = gather_weights()
    received = jnp.zeros((slot_rows, width), jnp.bfloat16)
    kept = []
    result_parts = []
    for tick_index in range(micro_count + 1):
        first_input = tokens[min(tick_index, micro_count - 1)].astype(jnp.float32)
        layer_input = jnp.where(section_index == 0, first_input, received.astype(jnp.float32))
        micro_index = jnp.clip(tick_index - section_index, 0, micro_count - 1)
        length = lengths[micro_index]
        layer_output, saved = layer_forward(layer_input, length, weights, query_scale)
        sent = layer_output.astype(jnp.bfloat16)
        received = handoff(sent)
        kept.append(saved)
        if tick_index >= 1:
            finished = jnp.where(section_index == 1, sent, received)
            result_parts.append(
                lax.dynamic_slice_in_dim(finished, section_index * half_width, half_width, 1)
            )
    output = jnp.stack(result_parts)
    row_ids = lax.iota(jnp.int32, slot_rows)
    grad_received = jnp.zeros((slot_rows, width), jnp.bfloat16)
    grad_parts = []
    grad_totals = None
    scale_total = jnp.zeros((HD,), jnp.float32)
    for tick_index in range(micro_count + 1):
        offset = tick_index - 1 + section_index
        micro_index = jnp.clip(offset, 0, micro_count - 1)
        length = lengths[micro_index]
        live_tick = ((offset >= 0) & (offset < micro_count)).astype(jnp.float32)
        live_rows = (row_ids < length).astype(jnp.float32)[:, None]
        top_grad = cotangent[min(tick_index, micro_count - 1)].astype(jnp.float32) * live_rows
        grad_output = jnp.where(section_index == 1, top_grad, grad_received.astype(jnp.float32))
        saved = jax.tree.map(
            lambda early, late: jnp.where(section_index == 0, early, late),
            kept[max(tick_index - 1, 0)],
            kept[min(tick_index + 1, micro_count)],
        )
        d_input, weight_grads, scale_grad = layer_backward(
            saved, length, weights, query_scale, grad_output
        )
        weight_grads = tuple((item * live_tick for item in weight_grads))
        scale_total = scale_total + scale_grad * live_tick
        sent = d_input.astype(jnp.bfloat16)
        grad_received = handoff(sent)
        if tick_index >= 1:
            finished = jnp.where(section_index == 0, sent, grad_received)
            grad_parts.append(
                lax.dynamic_slice_in_dim(finished, section_index * half_width, half_width, 1)
            )
        if grad_totals is None:
            grad_totals = weight_grads
        else:
            grad_totals = tuple((total + piece for total, piece in zip(grad_totals, weight_grads)))
    d_tokens = jnp.stack(grad_parts)
    if near:
        d_qkv = grad_totals[0]
        parts = [d_qkv[:, k * width : (k + 1) * width] for k in range(3)] + list(grad_totals[1:4])
        scattered = scatter_pieces(jnp.stack([item.astype(BF16) for item in parts]))
        scattered = scattered + (
            lax.psum_scatter(grad_totals[4], "fsdp", scatter_dimension=0, tiled=True),
        )
    else:
        scattered = (
        lax.psum_scatter(grad_totals[0], "fsdp", scatter_dimension=0, tiled=True),
        lax.psum_scatter(grad_totals[1], "fsdp", scatter_dimension=0, tiled=True),
        lax.psum_scatter(grad_totals[2], "fsdp", scatter_dimension=0, tiled=True),
        lax.psum_scatter(grad_totals[3], "fsdp", scatter_dimension=0, tiled=True),
        lax.psum_scatter(grad_totals[4], "fsdp", scatter_dimension=0, tiled=True),
    )
    owned = tuple((item[None] for item in scattered))
    scale_sum = lax.psum(scale_total, "fsdp")
    d_query_gain = (scale_sum * jax.nn.sigmoid(query_gain[0]) * scale_factor)[None]
    return (output, d_tokens, owned[0], owned[1], owned[2], owned[3], owned[4], d_query_gain)


def solution(mesh):
    in_specs = (
        P("fsdp", None, None),
        P("fsdp", None, None),
        P("fsdp"),
        P("section", "fsdp", None),
        P("section", "fsdp", None),
        P("section", "fsdp", None),
        P("section", "fsdp", None),
        P("section", "fsdp", None),
        P("section", None),
    )
    out_specs = (
        P("fsdp", None, "section"),
        P("fsdp", None, "section"),
        P("section", "fsdp", None),
        P("section", "fsdp", None),
        P("section", "fsdp", None),
        P("section", "fsdp", None),
        P("section", "fsdp", None),
        P("section", None),
    )
    return jax.shard_map(shards, mesh=mesh, in_specs=in_specs, out_specs=out_specs, check_vma=False)
```

```python
import math

import jax
import jax.numpy as jnp
from jax import lax
from jax.experimental import pallas as pl
from jax.experimental.pallas import tpu as pltpu
from jax.sharding import PartitionSpec as P

H = 16
HD = 80


NORM_EPS = 1e-06
NEG_FILL = -1e30
LOG_BASE = 1.442695041


MESH_ID = pl.DeviceIdType.MESH
BF16 = jnp.bfloat16
F32 = jnp.float32
NZ = 4
TILE = 256
PIECES = 6
GAINS = 6
FIRST_IN = 0
FIRST_OUT = 5


def place():
    s, f = lax.axis_index("section"), lax.axis_index("fsdp")
    return s, f // 4, (f // 2) % 2, f % 2


def device(s, z, x, c):
    return (s, z * 4 + x * 2 + c)


def inside(z):
    return (z >= 0) & (z < NZ)


def clipped(z):
    return jnp.clip(z, 0, NZ - 1)


def neighbour_barrier(s, z, x, c):
    barrier = pltpu.get_barrier_semaphore()

    def tell(target):
        pl.semaphore_signal(barrier, inc=1, device_id=target, device_id_type=MESH_ID)

    tell(device(s, z, x, 1 - c))
    tell(device(s, z, 1 - x, c))
    tell(device(1 - s, z, x, c))
    tell(device(s, (z + 2) % NZ, x, c))
    pl.when(z > 0)(lambda: tell(device(s, z - 1, x, c)))
    pl.when(z < NZ - 1)(lambda: tell(device(s, z + 1, x, c)))
    pl.semaphore_wait(barrier, 4 + (z > 0).astype(jnp.int32) + (z < NZ - 1).astype(jnp.int32))


def remote(src, dst, send_sem, recv_sem, target):
    return pltpu.make_async_remote_copy(
        src, dst, send_sem, recv_sem, device_id=target, device_id_type=MESH_ID
    )


class Gather:
    def __init__(self, where, view, sems):
        self.where, self.view = where, view
        self.send_sem, self.recv_sem, self.core_send, self.core_recv = sems

    def ship(self, p, zz, xx, way, cond, wait):
        s, z, x, c = self.where
        i = zz * 2 + xx
        block = self.view(p, zz, xx, c)
        if way < 3:
            target = (
                device(s, clipped(z + 1), x, c),
                device(s, clipped(z - 1), x, c),
                device(s, z, 1 - x, c),
            )[way]
            cp = remote(block, block, self.send_sem.at[p, i, way], self.recv_sem.at[p, i], target)
        else:
            cp = remote(block, block, self.core_send.at[p, i], self.core_recv.at[p, i], device(s, z, x, 1 - c))
        act = cp.wait_send if wait else cp.start
        if cond is None:
            act()
        else:
            pl.when(cond)(act)

    def arrived(self, p, zz, xx):
        s, z, x, c = self.where
        block = self.view(p, zz, xx, c)
        i = zz * 2 + xx
        remote(block, block, self.send_sem.at[p, i, 0], self.recv_sem.at[p, i], device(s, z, 1 - x, c)).wait_recv()

    def own(self, p, wait=False):
        s, z, x, c = self.where
        for way, cond in ((0, z < NZ - 1), (1, z > 0), (2, None), (3, None)):
            self.ship(p, z, x, way, cond, wait)

    def relay(self, p, wait=False):
        s, z, x, c = self.where
        cols = (x, 1 - x) if p == FIRST_IN else (x,)
        if p == FIRST_IN:
            if not wait:
                self.arrived(p, z, 1 - x)
            self.ship(p, z, 1 - x, 0, z < NZ - 1, wait)
            self.ship(p, z, 1 - x, 1, z > 0, wait)
            self.ship(p, z, 1 - x, 3, None, wait)
        for d in range(1, NZ):
            for sign, way in ((-1, 0), (1, 1)):
                zz = clipped(z + sign * d)
                here = inside(z + sign * d)
                for xx in cols:
                    if not wait:
                        pl.when(here)(lambda zz=zz, xx=xx: self.arrived(p, zz, xx))
                    self.ship(p, zz, xx, way, here & inside(z - sign), wait)
                    if p != FIRST_IN:
                        self.ship(p, zz, xx, 2, here, wait)
                    self.ship(p, zz, xx, 3, here, wait)

    def across(self, p, wait=False):
        s, z, x, c = self.where
        if p == FIRST_IN:
            return
        for d in range(NZ):
            for sign in (-1, 1) if d else (1,):
                zz = clipped(z + sign * d)
                here = inside(z + sign * d)
                if not wait:
                    pl.when(here)(lambda zz=zz: self.arrived(p, zz, 1 - x))
                self.ship(p, zz, 1 - x, 3, here, wait)

    def finish(self, p):
        s, z, x, c = self.where
        for zz in range(NZ):
            for xx in range(2):
                block = self.view(p, zz, xx, 1 - c)
                i = zz * 2 + xx
                remote(block, block, self.core_send.at[p, i], self.core_recv.at[p, i], device(s, z, x, 1 - c)).wait_recv()

    def drain(self, p):
        self.own(p, True)
        self.relay(p, True)
        self.across(p, True)


def add_block(dst, src):
    @pl.loop(0, dst.shape[0] // 16)
    def _(k):
        r = pl.ds(pl.multiple_of(k * 16, 16), 16)
        dst[r] = (dst[r].astype(F32) + src[r].astype(F32)).astype(BF16)


class Scatter:
    def __init__(self, where, view, bufs, sems, store):
        self.where, self.view, self.store = where, view, store
        self.got_core, self.got_x, self.got_z, self.got_zz = bufs
        self.core_s, self.core_r, self.x_s, self.x_r, self.z_s, self.z_r = sems

    def core_copy(self, p, i):
        s, z, x, c = self.where
        return remote(
            self.view(p, i // 2, i % 2, 1 - c),
            self.got_core.at[p, i],
            self.core_s.at[p, i],
            self.core_r.at[p, i],
            device(s, z, x, 1 - c),
        )

    def core_send(self, p):
        for i in range(2 * NZ):
            self.core_copy(p, i).start()

    def core_add(self, p):
        c = self.where[3]

        @pl.loop(0, 2 * NZ)
        def _(i):
            self.core_copy(p, i).wait_recv()
            add_block(self.view(p, i // 2, i % 2, c), self.got_core.at[p, i])

    def x_copy(self, p, zz):
        s, z, x, c = self.where
        return remote(
            self.view(p, zz, 1 - x, c),
            self.got_x.at[p, zz],
            self.x_s.at[p, zz],
            self.x_r.at[p, zz],
            device(s, z, 1 - x, c),
        )

    def steps(self):
        z = self.where[1]
        for d in range(NZ - 1, 0, -1):
            for sign in (1, -1):
                yield d, clipped(z + sign * d), inside(z + sign * d), sign

    def x_send(self, p):
        for _, zz, here, _ in self.steps():
            pl.when(here)(lambda zz=zz: self.x_copy(p, zz).start())
        self.x_copy(p, self.where[1]).start()

    def x_add(self, p, zz):
        s, z, x, c = self.where
        self.x_copy(p, zz).wait_recv()
        add_block(self.view(p, zz, x, c), self.got_x.at[p, zz])

    def slot(self, p, k, xx):
        return self.got_zz.at[xx, k] if p == FIRST_OUT else self.got_z.at[p, k]

    def z_copy(self, p, zz, xx, sign, k):
        s, z, x, c = self.where
        return remote(
            self.view(p, zz, xx, c),
            self.slot(p, k, xx),
            self.z_s.at[p, xx, zz],
            self.z_r.at[p, xx, k],
            device(s, clipped(z + sign), x, c),
        )

    def z_out(self, p, zz, xx, sign):
        k = jnp.where((sign < 0) & (self.where[1] + sign == zz), NZ, zz)
        return self.z_copy(p, zz, xx, sign, k)

    def cols(self, p):
        x = self.where[2]
        return (x, 1 - x) if p == FIRST_OUT else (x,)

    def z_take(self, p, zz, xx, k):
        self.z_copy(p, zz, xx, 1, k).wait_recv()
        add_block(self.view(p, zz, xx, self.where[3]), self.slot(p, k, xx))

    def z_step(self, p, distance):
        z = self.where[1]
        for d, zz, here, sign in self.steps():
            if d != distance:
                continue

            @pl.when(here)
            def _(zz=zz, sign=sign):
                if p != FIRST_OUT:
                    self.x_add(p, zz)
                for xx in self.cols(p):
                    pl.when(inside(z - sign))(lambda xx=xx: self.z_take(p, zz, xx, zz))
                    self.z_out(p, zz, xx, sign).start()

    def z_last(self, p, xx):
        z = self.where[1]
        pl.when(z > 0)(lambda: self.z_take(p, z, xx, z))
        pl.when(z < NZ - 1)(lambda: self.z_take(p, z, xx, NZ))

    def close(self, p):
        s, z, x, c = self.where
        if p == FIRST_OUT:
            self.z_last(p, 1 - x)
            self.x_copy(p, z).start()
            self.z_last(p, x)
            self.x_add(p, z)
        else:
            self.x_add(p, z)
            self.z_last(p, x)
        self.store(p, self.view(p, z, x, c))

    def serve(self, p):
        for d in range(NZ - 1, 0, -1):
            self.z_step(p, d)
        self.close(p)

    def drain(self, p):
        for i in range(2 * NZ):
            self.core_copy(p, i).wait_send()
        for _, zz, here, sign in self.steps():
            if p != FIRST_OUT:
                pl.when(here)(lambda zz=zz: self.x_copy(p, zz).wait_send())
            for xx in self.cols(p):
                pl.when(here)(lambda zz=zz, xx=xx, sign=sign: self.z_out(p, zz, xx, sign).wait_send())
        self.x_copy(p, self.where[1]).wait_send()


def head_windows():
    for k in range(8):
        start = HD * k // 128 * 128
        offset = HD * k - start
        span = 128 if offset + HD <= 128 else 256
        yield k, start, offset, span


def layers_kernel(
    n,
    tokens,
    cotangent,
    lengths,
    gain_block,
    scale,
    wq,
    wo,
    wu,
    wd,
    out_half,
    token_half,
    d_q,
    d_o,
    d_u,
    d_d,
    small_out,
    held,
    gain_all,
    gain_rows,
    hb,
    a1,
    qf,
    qb,
    kb,
    vb,
    prob,
    ob,
    mid,
    a2,
    up,
    hid,
    grad,
    dup,
    dmid,
    low,
    give,
    sums,
    swap,
    got_core,
    got_x,
    got_z,
    got_zz,
    *sems,
):
    where = s, z, x, c = place()
    dob = dup
    rows, width = hb.shape
    slots = cotangent.shape[1]
    half = width // 2
    group = 8 * HD
    g_sems, r_sems = sems[:4], sems[4:10]
    swap_s, swap_r, hand_s, hand_r, back_s, back_r, end_s, end_r = sems[10:]
    across_y = device(1 - s, z, x, c)

    def weight_view(p, zz, xx, cc):
        return held.at[p, pl.ds(pl.multiple_of((zz * 4 + xx * 2 + cc) * n, 16), n)]

    def view(p, zz, xx, cc):
        if p == GAINS:
            return gain_all.at[zz * 4 + xx * 2 + cc]
        return weight_view(p, zz, xx, cc)

    def store(p, block):
        @pl.loop(0, n // 16)
        def _(k):
            r = pl.ds(pl.multiple_of(k * 16, 16), 16)
            value = block[r].astype(F32)
            if p < 3:
                d_q[r, p * width : (p + 1) * width] = value
            else:
                (d_o, d_u, d_d)[p - 3][r] = value

    gather = Gather(where, view, g_sems)
    scatter = Scatter(where, weight_view, (got_core, got_x, got_z, got_zz), r_sems, store)


    def row_loop(fn):
        @pl.loop(0, rows // 32)
        def _(k):
            fn(pl.ds(pl.multiple_of(k * 32, 32), 32))

    def project(p, a, emit):
        @pl.loop(0, width // TILE)
        def _(k):
            lanes = pl.ds(pl.multiple_of(k * TILE, TILE), TILE)
            emit(lanes, jnp.dot(a[...], held[p, :, lanes], preferred_element_type=F32))

    def project_back(pieces, emit):
        @pl.loop(0, width // TILE)
        def _(k):
            lanes = pl.ds(pl.multiple_of(k * TILE, TILE), TILE)
            total = None
            for p, a in pieces:
                term = contract_cols(a[...], held[p, lanes, :])
                total = term if total is None else total + term
            emit(lanes, total)

    def weight_grad(p, a, g):
        @pl.loop(0, width // TILE)
        def _(k):
            lanes = pl.ds(pl.multiple_of(k * TILE, TILE), TILE)
            flipped = a[:, lanes].T
            for j in range(width // TILE):
                cols = slice(j * TILE, (j + 1) * TILE)
                held[p, lanes, cols] = jnp.dot(flipped, g[:, cols], preferred_element_type=F32).astype(BF16)

    def recip_of(value):
        return lax.rsqrt(jnp.mean(value * value, -1, keepdims=True) + NORM_EPS)

    def norm(src, row, dst):
        def part(r):
            value = src[r].astype(F32)
            dst[r] = (value * recip_of(value) * gain_rows[row : row + 1]).astype(BF16)

        row_loop(part)

    def put(ref):
        def emit(lanes, value):
            ref[:, lanes] = value.astype(ref.dtype)

        return emit

    def emit_query(lanes, value):
        qf[:, lanes] = value
        qb[:, lanes] = (value * scale[0:1, lanes]).astype(BF16)

    def emit_up(lanes, value):
        up[:, lanes] = value
        hid[:, lanes] = (value / (1.0 + jnp.exp(-value))).astype(BF16)

    def emit_mid(lanes, value):
        mid[:, lanes] = hb[:, lanes].astype(F32) + value

    def emit_out(lanes, value):
        give[:, lanes] = (mid[:, lanes] + value).astype(BF16)

    def lane_mask(offset, span):
        lane = lax.broadcasted_iota(jnp.int32, (1, span), 1)
        return ((lane >= offset) & (lane < offset + HD)).astype(F32).astype(BF16)

    def attention(body):
        @pl.loop(0, rows // slots * 2)
        def _(it):
            seq, g = it // 2, it % 2
            r = pl.ds(pl.multiple_of(seq * slots, slots), slots)

            def window(ref, start, span):
                return ref[r, pl.ds(pl.multiple_of(g * group + start, 128), span)]

            body(it, seq, r, g, window)

    def spread(total, start, span, value):
        for j in range(span // 128):
            k = start // 128 + j
            term = value[:, j * 128 : (j + 1) * 128]
            total[k] = term if total[k] is None else total[k] + term

    def attend(it, seq, r, g, window):
        allowed = causal_allowed(slots, lengths[seq])
        total = [None] * (group // 128)
        for k, start, offset, span in head_windows():
            only = lane_mask(offset, span)
            scores = contract_cols(window(qb, start, span) * only, window(kb, start, span))
            scores = jnp.where(allowed, scores, NEG_FILL)
            expd = jnp.exp(scores - jnp.max(scores, -1, keepdims=True))
            probs = expd / jnp.sum(expd, -1, keepdims=True)
            prob[it, k] = probs
            value = jnp.dot(probs.astype(BF16), window(vb, start, span) * only, preferred_element_type=F32)
            spread(total, start, span, value)
        for k, value in enumerate(total):
            ob[r, pl.ds(pl.multiple_of(g * group + k * 128, 128), 128)] = value.astype(BF16)

    def attend_back(it, seq, r, g, window):
        count = group // 128
        t_q, t_k, t_v = [None] * count, [None] * count, [None] * count
        for k, start, offset, span in head_windows():
            only = lane_mask(offset, span)
            d_o_part = window(dob, start, span) * only
            probs = prob[it, k]
            d_probs = contract_cols(d_o_part, window(vb, start, span))
            spread(t_v, start, span, contract_rows(probs.astype(BF16), d_o_part))
            d_scores = probs * (d_probs - jnp.sum(probs * d_probs, -1, keepdims=True))
            d_scores = d_scores.astype(BF16)
            spread(t_q, start, span, jnp.dot(d_scores, window(kb, start, span) * only, preferred_element_type=F32))
            spread(t_k, start, span, contract_rows(d_scores, window(qb, start, span) * only))
        for k in range(count):
            lanes = pl.ds(pl.multiple_of(g * group + k * 128, 128), 128)
            products = t_q[k] * qf[r, lanes]
            sums[2, :, lanes] += jnp.sum(products.reshape(slots // 8, 8, 128), 0)
            qb[r, lanes] = (t_q[k] * scale[0:1, lanes]).astype(BF16)
            kb[r, lanes] = t_k[k].astype(BF16)
            vb[r, lanes] = t_v[k].astype(BF16)

    def emit_dup(lanes, value):
        u = up[:, lanes]
        sig = 1.0 / (1.0 + jnp.exp(-u))
        dup[:, lanes] = (value * sig * (1.0 + u * (1.0 - sig))).astype(BF16)

    def norm_grad(row, src, base, emit):
        def part(r):
            value, d_normed = src[r].astype(F32), up[r]
            recip = recip_of(value)
            sums[row] += jnp.sum((d_normed * value * recip).reshape(4, 8, width), 0)
            emit(r, base[r].astype(F32) + norm_back(value, recip, d_normed * gain_rows[row : row + 1]))

        row_loop(part)

    def emit_dmid(r, value):
        dmid[r] = value
        low[r] = value.astype(BF16)

    def emit_give(r, value):
        give[r] = value.astype(BF16)

    def spread_gains():
        gain_rows[...] = jnp.zeros_like(gain_rows)
        for f in range(4 * NZ):
            start = min(n * f // 128 * 128, width - 256)
            block = jnp.concatenate([gain_all[f], jnp.zeros((8, 128), F32)], -1)
            block = pltpu.roll(block, n * f - start, 1) if n * f > start else block
            gain_rows[:, start : start + 256] += block

    def forward_stage(p):
        if p == 0:
            spread_gains()
            norm(hb, 0, a1)
            project(0, a1, emit_query)
        elif p == 1:
            project(1, a1, put(kb))
        elif p == 2:
            project(2, a1, put(vb))
            attention(attend)
        elif p == 3:
            project(3, ob, emit_mid)
            norm(mid, 1, a2)
        elif p == 4:
            project(4, a2, emit_up)
        else:
            project(5, hid, emit_out)


    def hand(k):
        r = pl.ds(k * slots, slots)
        return remote(give.at[r], hb.at[r], hand_s.at[k], hand_r.at[k], across_y)

    def back(k):
        r = pl.ds(k * slots, slots)
        return remote(give.at[r], grad.at[r], back_s.at[k], back_r.at[k], across_y)

    def end(which):
        dst, col = ((out_half, 0), (token_half, half))[which]
        return remote(give.at[:, col : col + half], dst, end_s.at[which], end_r.at[which], across_y)


    mine = pl.ds(pl.multiple_of((z * 4 + x * 2 + c) * n, 16), n)
    for k in range(3):
        held[k, mine] = wq[:, k * width : (k + 1) * width].astype(BF16)
    for k, ref in enumerate((wo, wu, wd)):
        held[3 + k, mine] = ref[...].astype(BF16)
    gain_all[z * 4 + x * 2 + c] = gain_block[...]
    sums[...] = jnp.zeros_like(sums)
    neighbour_barrier(s, z, x, c)

    @pl.when(s == 0)
    def _():
        for k in range(rows // slots):
            hb[k * slots : (k + 1) * slots] = tokens[k]

    order_in = [GAINS] + list(range(PIECES))

    @pl.loop(0, 2)
    def _(phase):
        @pl.when(phase == 0)
        def _():
            gather.own(order_in[0])
            gather.own(order_in[1])

        @pl.when((phase == 1) & (s == 1))
        def _():
            for k in range(rows // slots):
                hand(k).wait_recv()

        count = len(order_in)
        for t in range(count + 2):

            @pl.when(phase == 0)
            def _():
                if t + 2 < count:
                    gather.own(order_in[t + 2])
                if t < count:
                    gather.relay(order_in[t])
                if 0 <= t - 1 < count:
                    gather.across(order_in[t - 1])
                if 0 <= t - 2:
                    gather.finish(order_in[t - 2])

            if t - 2 >= 1:
                pl.when(phase == s)(lambda: forward_stage(order_in[t - 2]))

        @pl.when((phase == 0) & (s == 0))
        def _():
            for k in range(rows // slots):
                hand(k).start()

    for p in order_in:
        gather.drain(p)

    @pl.when(s == 0)
    def _():
        for k in range(rows // slots):
            hand(k).wait_send()
            back(k).wait_recv()

    @pl.when(s == 1)
    def _():
        end(0).start()
        out_half[...] = give[:, half:]
        for k in range(rows // slots):
            row = lax.broadcasted_iota(jnp.int32, (slots, 1), 0)
            live = (row < lengths[k]).astype(F32)
            grad[k * slots : (k + 1) * slots] = (cotangent[k].astype(F32) * live).astype(BF16)

    project_back([(5, grad)], emit_dup)
    weight_grad(5, hid, grad)
    scatter.core_send(5)
    project_back([(4, dup)], put(up))
    weight_grad(4, a2, dup)
    scatter.core_send(4)
    scatter.core_add(5)
    scatter.z_step(5, 3)
    norm_grad(1, mid, grad, emit_dmid)
    project_back([(3, low)], put(dob))
    weight_grad(3, ob, low)
    scatter.core_send(3)
    scatter.core_add(4)
    scatter.x_send(4)
    attention(attend_back)
    project_back([(0, qb), (1, kb), (2, vb)], put(up))

    @pl.when(s == 1)
    def _():
        end(0).wait_send()

    norm_grad(0, hb, dmid, emit_give)

    @pl.when(s == 1)
    def _():
        for k in range(rows // slots):
            back(k).start()

    @pl.when(s == 0)
    def _():
        end(1).start()
        token_half[...] = give[:, :half]

    scatter.core_add(3)
    scatter.x_send(3)
    for p, ref in enumerate((qb, kb, vb)):
        weight_grad(p, a1, ref)
        scatter.core_send(p)

    totals = [jnp.sum(sums[k], 0, keepdims=True) for k in range(3)]
    swap[0, 0] = jnp.concatenate(totals + [jnp.zeros((5, width), F32)], 0)
    partners = (
        device(s, z, x, 1 - c),
        device(s, z, 1 - x, c),
        device(s, z + 1 - 2 * (z % 2), x, c),
        device(s, (z + 2) % NZ, x, c),
    )

    def exchange(k):
        return remote(swap.at[k, 0], swap.at[k, 1], swap_s.at[k], swap_r.at[k], partners[k])

    exchange(0).start()
    for d in (2, 1):
        scatter.z_step(5, d)
    scatter.close(5)
    order_out = [4, 3, 0, 1, 2]
    for k, p in enumerate(order_out):
        if k + 2 < len(order_out):
            scatter.core_add(order_out[k + 2])
            scatter.x_send(order_out[k + 2])
        if k < 4:
            exchange(k).wait_recv()
            if k < 3:
                swap[k + 1, 0] = swap[k, 0] + swap[k, 1]
                exchange(k + 1).start()
            else:
                small_out[...] = swap[k, 0] + swap[k, 1]
        scatter.serve(p)
    for p in range(PIECES):
        scatter.drain(p)
    for k in range(4):
        exchange(k).wait_send()

    @pl.when(s == 0)
    def _():
        end(1).wait_send()
        end(0).wait_recv()

    @pl.when(s == 1)
    def _():
        for k in range(rows // slots):
            back(k).wait_send()
        end(1).wait_recv()


def near_shards(
    tokens, cotangent, lengths, qkv_weight, out_weight, up_weight, down_weight, norm_gains, query_gain
):
    n, width = out_weight.shape
    count, slots, _ = tokens.shape
    rows = count * slots
    factor = LOG_BASE / math.sqrt(HD)
    scale = jnp.tile(jax.nn.softplus(query_gain) * factor, (8, H))
    gains = norm_gains.astype(BF16).astype(F32).T
    gain_block = jnp.pad(gains, ((0, 6), (0, 128 - n)))
    dma = pltpu.SemaphoreType.DMA
    whole = pl.BlockSpec(memory_space=pltpu.VMEM)
    block = (n, width)
    low_rows = pltpu.VMEM((rows, width), BF16)
    wide_rows = pltpu.VMEM((rows, width), F32)
    scratch = dict(
        held=pltpu.VMEM((PIECES, 4 * NZ * n, width), BF16),
        gain_all=pltpu.VMEM((4 * NZ, 8, 128), F32),
        gain_rows=pltpu.VMEM((8, width), F32),
        hb=low_rows,
        a1=low_rows,
        qf=wide_rows,
        qb=low_rows,
        kb=low_rows,
        vb=low_rows,
        prob=pltpu.VMEM((2 * count, 8, slots, slots), F32),
        ob=low_rows,
        mid=wide_rows,
        a2=low_rows,
        up=wide_rows,
        hid=low_rows,
        grad=low_rows,
        dup=low_rows,
        dmid=wide_rows,
        low=low_rows,
        give=low_rows,
        sums=pltpu.VMEM((3, 8, width), F32),
        swap=pltpu.VMEM((4, 2, 8, width), F32),
        got_core=pltpu.VMEM((PIECES, 2 * NZ) + block, BF16),
        got_x=pltpu.VMEM((PIECES, NZ) + block, BF16),
        got_z=pltpu.VMEM((PIECES - 1, NZ + 1) + block, BF16),
        got_zz=pltpu.VMEM((2, NZ + 1) + block, BF16),
    )
    semaphores = [
        dma((PIECES + 1, 2 * NZ, 3)),
        dma((PIECES + 1, 2 * NZ)),
        dma((PIECES + 1, 2 * NZ)),
        dma((PIECES + 1, 2 * NZ)),
        dma((PIECES, 2 * NZ)),
        dma((PIECES, 2 * NZ)),
        dma((PIECES, NZ)),
        dma((PIECES, NZ)),
        dma((PIECES, 2, NZ)),
        dma((PIECES, 2, NZ + 1)),
        dma((4,)),
        dma((4,)),
        dma((count,)),
        dma((count,)),
        dma((count,)),
        dma((count,)),
        dma((2,)),
        dma((2,)),
    ]
    half = jax.ShapeDtypeStruct((rows, width // 2), BF16)
    out, d_tokens, d_q, d_o, d_u, d_d, small = pl.pallas_call(
        lambda *refs: layers_kernel(n, *refs),
        out_shape=(
            half,
            half,
            jax.ShapeDtypeStruct((n, 3 * width), F32),
            jax.ShapeDtypeStruct(block, F32),
            jax.ShapeDtypeStruct(block, F32),
            jax.ShapeDtypeStruct(block, F32),
            jax.ShapeDtypeStruct((8, width), F32),
        ),
        in_specs=[whole, whole, pl.BlockSpec(memory_space=pltpu.SMEM)] + [whole] * 6,
        out_specs=(whole,) * 7,
        scratch_shapes=list(scratch.values()) + semaphores,
        compiler_params=pltpu.CompilerParams(
            collective_id=1, has_side_effects=True, vmem_limit_bytes=63 << 20
        ),
        name="two_layers",
    )(tokens, cotangent, lengths, gain_block, scale, qkv_weight, out_weight, up_weight, down_weight)
    own = lax.dynamic_slice_in_dim(small[:2], lax.axis_index("fsdp") * n, n, 1).T
    d_scale = jnp.sum(small[2].reshape(H, HD), 0)
    d_query_gain = (d_scale * jax.nn.sigmoid(query_gain[0]) * factor)[None]
    shape = (count, slots, width // 2)
    return (
        out.reshape(shape),
        d_tokens.reshape(shape),
        d_q[None],
        d_o[None],
        d_u[None],
        d_d[None],
        own[None],
        d_query_gain,
    )


def swapped(value, axis, bit):
    return lax.ppermute(value, axis, [(i, i ^ 1 << bit) for i in range(lax.axis_size(axis))])


def causal_allowed(row_count, length):
    row_ids = lax.broadcasted_iota(jnp.int32, (row_count, row_count), 0)
    col_ids = lax.broadcasted_iota(jnp.int32, (row_count, row_count), 1)
    return (col_ids <= row_ids) & (col_ids < length)


def contract_rows(left, right):
    return lax.dot_general(
        left, right, (((0,), (0,)), ((), ())), preferred_element_type=jnp.float32
    )


def contract_cols(left, right):
    return lax.dot_general(
        left, right, (((1,), (1,)), ((), ())), preferred_element_type=jnp.float32
    )


def norm_back(source, recip, grad_flat):
    return recip * grad_flat - source * recip**3 * jnp.mean(grad_flat * source, -1, keepdims=True)


def layer_forward(layer_input, length, weights, query_scale):
    qkv_w, out_w, up_w, down_w, gain_pair = weights
    row_count, width = layer_input.shape
    gain_one = gain_pair[:, 0].astype(jnp.float32)
    gain_two = gain_pair[:, 1].astype(jnp.float32)
    recip_one = lax.rsqrt(jnp.mean(layer_input * layer_input, -1, keepdims=True) + NORM_EPS)
    normed = (layer_input * recip_one * gain_one).astype(jnp.bfloat16)
    proj = jnp.dot(normed, qkv_w, preferred_element_type=jnp.float32)
    query = proj[:, :width].reshape(row_count, H, HD)
    query_b = (query * query_scale).astype(jnp.bfloat16)
    keys_b = proj[:, width : 2 * width].astype(jnp.bfloat16).reshape(row_count, H, HD)
    values_b = proj[:, 2 * width :].astype(jnp.bfloat16).reshape(row_count, H, HD)
    scores = jnp.einsum("qhd,khd->hqk", query_b, keys_b, preferred_element_type=jnp.float32)
    scores = jnp.where(causal_allowed(row_count, length)[None], scores, NEG_FILL)
    row_peak = jnp.max(scores, -1, keepdims=True)
    expd = jnp.exp(scores - row_peak)
    row_total = jnp.sum(expd, -1, keepdims=True)
    probs = expd / row_total
    logsum = (row_peak + jnp.log(row_total))[..., 0]
    attended = (
        jnp.einsum(
            "hqk,khd->qhd", probs.astype(jnp.bfloat16), values_b, preferred_element_type=jnp.float32
        )
        .reshape(row_count, width)
        .astype(jnp.bfloat16)
    )
    middle = layer_input + jnp.dot(attended, out_w, preferred_element_type=jnp.float32)
    recip_two = lax.rsqrt(jnp.mean(middle * middle, -1, keepdims=True) + NORM_EPS)
    normed_two = (middle * recip_two * gain_two).astype(jnp.bfloat16)
    upper = jnp.dot(normed_two, up_w, preferred_element_type=jnp.float32)
    hidden = jax.nn.silu(upper).astype(jnp.bfloat16)
    layer_output = middle + jnp.dot(hidden, down_w, preferred_element_type=jnp.float32)
    saved = (
        layer_input,
        normed,
        query,
        query_b,
        keys_b,
        values_b,
        logsum,
        attended,
        middle,
        normed_two,
        upper,
        hidden,
        recip_one,
        recip_two,
    )
    return (layer_output, saved)


def layer_backward(saved, length, weights, query_scale, grad_output):
    qkv_w, out_w, up_w, down_w, gain_pair = weights
    (
        layer_input,
        normed,
        query,
        query_b,
        keys_b,
        values_b,
        logsum,
        attended,
        middle,
        normed_two,
        upper,
        hidden,
        recip_one,
        recip_two,
    ) = saved
    row_count, width = layer_input.shape
    gain_one = gain_pair[:, 0].astype(jnp.float32)
    gain_two = gain_pair[:, 1].astype(jnp.float32)
    grad_low = grad_output.astype(jnp.bfloat16)
    d_down = contract_rows(hidden, grad_low)
    d_hidden = contract_cols(grad_low, down_w)
    sigmoid_up = jax.nn.sigmoid(upper)
    d_upper = (d_hidden * sigmoid_up * (1.0 + upper * (1.0 - sigmoid_up))).astype(jnp.bfloat16)
    d_up = contract_rows(normed_two, d_upper)
    d_normed_two = contract_cols(d_upper, up_w)
    d_gain_two = jnp.sum(d_normed_two * middle * recip_two, 0)
    d_middle = grad_output + norm_back(middle, recip_two, d_normed_two * gain_two)
    middle_low = d_middle.astype(jnp.bfloat16)
    d_out = contract_rows(attended, middle_low)
    d_attended = contract_cols(middle_low, out_w).astype(jnp.bfloat16).reshape(row_count, H, HD)
    scores = jnp.einsum("qhd,khd->hqk", query_b, keys_b, preferred_element_type=jnp.float32)
    scores = jnp.where(causal_allowed(row_count, length)[None], scores, NEG_FILL)
    probs = jnp.exp(scores - logsum[..., None])
    d_probs = jnp.einsum("qhd,khd->hqk", d_attended, values_b, preferred_element_type=jnp.float32)
    d_values = jnp.einsum(
        "hqk,qhd->khd", probs.astype(jnp.bfloat16), d_attended, preferred_element_type=jnp.float32
    ).astype(jnp.bfloat16)
    d_scores = (probs * (d_probs - jnp.sum(probs * d_probs, -1, keepdims=True))).astype(
        jnp.bfloat16
    )
    d_query_s = jnp.einsum("hqk,khd->qhd", d_scores, keys_b, preferred_element_type=jnp.float32)
    d_keys = jnp.einsum(
        "hqk,qhd->khd", d_scores, query_b, preferred_element_type=jnp.float32
    ).astype(jnp.bfloat16)
    d_scale = jnp.sum(d_query_s * query, (0, 1))
    d_query = (d_query_s * query_scale).astype(jnp.bfloat16)
    d_proj = jnp.concatenate(
        [
            d_query.reshape(row_count, width),
            d_keys.reshape(row_count, width),
            d_values.reshape(row_count, width),
        ],
        -1,
    )
    d_qkv = contract_rows(normed, d_proj)
    d_normed = contract_cols(d_proj, qkv_w)
    d_gain_one = jnp.sum(d_normed * layer_input * recip_one, 0)
    d_input = d_middle + norm_back(layer_input, recip_one, d_normed * gain_one)
    d_gains = jnp.stack([d_gain_one, d_gain_two], -1)
    return (d_input, (d_qkv, d_out, d_up, d_down, d_gains), d_scale)


def shards(
    tokens,
    cotangent,
    lengths,
    qkv_weight,
    out_weight,
    up_weight,
    down_weight,
    norm_gains,
    query_gain,
):
    if lax.axis_size("fsdp") == 4 * NZ:
        return near_shards(
            tokens,
            cotangent,
            lengths,
            qkv_weight[0],
            out_weight[0],
            up_weight[0],
            down_weight[0],
            norm_gains[0],
            query_gain,
        )
    section_index = lax.axis_index("section")
    micro_count, slot_rows, width = tokens.shape
    half_width = width // 2
    scale_factor = LOG_BASE / math.sqrt(HD)
    query_scale = jax.nn.softplus(query_gain[0]) * scale_factor

    def gather_weights():
        pieces = (
            lax.all_gather(qkv_weight.astype(jnp.bfloat16), "fsdp", axis=1, tiled=True),
            lax.all_gather(out_weight.astype(jnp.bfloat16), "fsdp", axis=1, tiled=True),
            lax.all_gather(up_weight.astype(jnp.bfloat16), "fsdp", axis=1, tiled=True),
            lax.all_gather(down_weight.astype(jnp.bfloat16), "fsdp", axis=1, tiled=True),
            lax.all_gather(norm_gains.astype(jnp.bfloat16), "fsdp", axis=1, tiled=True),
        )
        return tuple((piece[0] for piece in pieces))

    def handoff(value):
        return swapped(value, "section", 0)

    weights = gather_weights()
    received = jnp.zeros((slot_rows, width), jnp.bfloat16)
    kept = []
    result_parts = []
    for tick_index in range(micro_count + 1):
        first_input = tokens[min(tick_index, micro_count - 1)].astype(jnp.float32)
        layer_input = jnp.where(section_index == 0, first_input, received.astype(jnp.float32))
        micro_index = jnp.clip(tick_index - section_index, 0, micro_count - 1)
        length = lengths[micro_index]
        layer_output, saved = layer_forward(layer_input, length, weights, query_scale)
        sent = layer_output.astype(jnp.bfloat16)
        received = handoff(sent)
        kept.append(saved)
        if tick_index >= 1:
            finished = jnp.where(section_index == 1, sent, received)
            result_parts.append(
                lax.dynamic_slice_in_dim(finished, section_index * half_width, half_width, 1)
            )
    output = jnp.stack(result_parts)
    weights = gather_weights()
    row_ids = lax.iota(jnp.int32, slot_rows)
    grad_received = jnp.zeros((slot_rows, width), jnp.bfloat16)
    grad_parts = []
    grad_totals = None
    scale_total = jnp.zeros((HD,), jnp.float32)
    for tick_index in range(micro_count + 1):
        offset = tick_index - 1 + section_index
        micro_index = jnp.clip(offset, 0, micro_count - 1)
        length = lengths[micro_index]
        live_tick = ((offset >= 0) & (offset < micro_count)).astype(jnp.float32)
        live_rows = (row_ids < length).astype(jnp.float32)[:, None]
        top_grad = cotangent[min(tick_index, micro_count - 1)].astype(jnp.float32) * live_rows
        grad_output = jnp.where(section_index == 1, top_grad, grad_received.astype(jnp.float32))
        saved = jax.tree.map(
            lambda early, late: jnp.where(section_index == 0, early, late),
            kept[max(tick_index - 1, 0)],
            kept[min(tick_index + 1, micro_count)],
        )
        d_input, weight_grads, scale_grad = layer_backward(
            saved, length, weights, query_scale, grad_output
        )
        weight_grads = tuple((item * live_tick for item in weight_grads))
        scale_total = scale_total + scale_grad * live_tick
        sent = d_input.astype(jnp.bfloat16)
        grad_received = handoff(sent)
        if tick_index >= 1:
            finished = jnp.where(section_index == 0, sent, grad_received)
            grad_parts.append(
                lax.dynamic_slice_in_dim(finished, section_index * half_width, half_width, 1)
            )
        if grad_totals is None:
            grad_totals = weight_grads
        else:
            grad_totals = tuple((total + piece for total, piece in zip(grad_totals, weight_grads)))
    d_tokens = jnp.stack(grad_parts)
    scattered = (
        lax.psum_scatter(grad_totals[0], "fsdp", scatter_dimension=0, tiled=True),
        lax.psum_scatter(grad_totals[1], "fsdp", scatter_dimension=0, tiled=True),
        lax.psum_scatter(grad_totals[2], "fsdp", scatter_dimension=0, tiled=True),
        lax.psum_scatter(grad_totals[3], "fsdp", scatter_dimension=0, tiled=True),
        lax.psum_scatter(grad_totals[4], "fsdp", scatter_dimension=0, tiled=True),
    )
    owned = tuple((item[None] for item in scattered))
    scale_sum = lax.psum(scale_total, "fsdp")
    d_query_gain = (scale_sum * jax.nn.sigmoid(query_gain[0]) * scale_factor)[None]
    return (output, d_tokens, owned[0], owned[1], owned[2], owned[3], owned[4], d_query_gain)


def solution(mesh):
    in_specs = (
        P("fsdp", None, None),
        P("fsdp", None, None),
        P("fsdp"),
        P("section", "fsdp", None),
        P("section", "fsdp", None),
        P("section", "fsdp", None),
        P("section", "fsdp", None),
        P("section", "fsdp", None),
        P("section", None),
    )
    out_specs = (
        P("fsdp", None, "section"),
        P("fsdp", None, "section"),
        P("section", "fsdp", None),
        P("section", "fsdp", None),
        P("section", "fsdp", None),
        P("section", "fsdp", None),
        P("section", "fsdp", None),
        P("section", None),
    )
    return jax.shard_map(shards, mesh=mesh, in_specs=in_specs, out_specs=out_specs, check_vma=False)
```

```python
import math

import jax
import jax.numpy as jnp
from jax import lax
from jax.experimental import pallas as pl
from jax.experimental.pallas import tpu as pltpu
from jax.sharding import PartitionSpec as P

H = 16
HD = 80


NORM_EPS = 1e-06
NEG_FILL = -1e30
LOG_BASE = 1.442695041


MESH_ID = pl.DeviceIdType.MESH
BF16 = jnp.bfloat16
F32 = jnp.float32
NZ = 4
TILE = 256
PIECES = 6
GAINS = 6
FIRST_IN = 5
FIRST_OUT = 4


def place():
    s, f = lax.axis_index("section"), lax.axis_index("fsdp")
    return s, f // 4, (f // 2) % 2, f % 2


def device(s, z, x, c):
    return (s, z * 4 + x * 2 + c)


def inside(z):
    return (z >= 0) & (z < NZ)


def clipped(z):
    return jnp.clip(z, 0, NZ - 1)


def neighbour_barrier(s, z, x, c):
    barrier = pltpu.get_barrier_semaphore()

    def tell(target):
        pl.semaphore_signal(barrier, inc=1, device_id=target, device_id_type=MESH_ID)

    tell(device(s, z, x, 1 - c))
    tell(device(s, z, 1 - x, c))
    tell(device(1 - s, z, x, c))
    tell(device(s, (z + 2) % NZ, x, c))
    pl.when(z > 0)(lambda: tell(device(s, z - 1, x, c)))
    pl.when(z < NZ - 1)(lambda: tell(device(s, z + 1, x, c)))
    pl.semaphore_wait(barrier, 4 + (z > 0).astype(jnp.int32) + (z < NZ - 1).astype(jnp.int32))


def remote(src, dst, send_sem, recv_sem, target):
    return pltpu.make_async_remote_copy(
        src, dst, send_sem, recv_sem, device_id=target, device_id_type=MESH_ID
    )


GATHER_STEPS = (
    ("own", 5),
    ("own", 6),
    ("own", 1),
    ("own", 0),
    ("relay", 0, 1, (-1,)),
    ("relay", 1, 1, (1,)),
    ("relay", 6, 1, (-1,)),
    ("relay", 6, 1, (1,)),
    ("relay", 6, 2, (-1,)),
    ("relay", 6, 2, (1,)),
    ("own", 2),
    ("relay", 0, 1, (1,)),
    ("relay", 0, 2, (-1,)),
    ("relay", 6, 3, (1,)),
    ("relay", 6, 3, (-1,)),
    ("across", 6, 0),
    ("relay", 1, 1, (-1,)),
    ("relay", 2, 1, (1,)),
    ("relay", 1, 2, (1,)),
    ("relay", 1, 2, (-1,)),
    ("across", 6, 1),
    ("relay", 0, 2, (1,)),
    ("relay", 0, 3, (1,)),
    ("across", 6, 2),
    ("relay", 1, 3, (-1,)),
    ("relay", 1, 3, (1,)),
    ("across", 1, 0),
    ("across", 6, 3),
    ("relay", 0, 3, (-1,)),
    ("across", 0, 0),
    ("across", 0, 1),
    ("turn", 5),
    ("across", 1, 1),
    ("relay", 2, 1, (-1,)),
    ("relay", 2, 2, (-1,)),
    ("relay", 5, 1, (-1,)),
    ("relay", 2, 2, (1,)),
    ("own", 3),
    ("relay", 2, 3, (-1,)),
    ("relay", 2, 3, (1,)),
    ("across", 0, 2),
    ("across", 0, 3),
    ("relay", 3, 1, (1,)),
    ("finish", 6),
    ("finish", 0),
    ("relay", 3, 1, (-1,)),
    ("across", 2, 0),
    ("across", 2, 1),
    ("across", 2, 2),
    ("across", 1, 2),
    ("across", 1, 3),
    ("relay", 3, 2, (-1,)),
    ("relay", 3, 2, (1,)),
    ("across", 2, 3),
    ("relay", 5, 1, (1,)),
    ("own", 4),
    ("finish", 1),
    ("relay", 4, 1, (-1,)),
    ("relay", 4, 1, (1,)),
    ("relay", 3, 3, (-1,)),
    ("finish", 2),
    ("relay", 3, 3, (1,)),
    ("relay", 4, 2, (1,)),
    ("relay", 5, 2, (1,)),
    ("across", 3, 0),
    ("across", 3, 1),
    ("relay", 4, 2, (-1,)),
    ("across", 3, 2),
    ("relay", 5, 2, (-1,)),
    ("across", 3, 3),
    ("relay", 4, 3, (1,)),
    ("relay", 4, 3, (-1,)),
    ("across", 4, 0),
    ("finish", 3),
    ("across", 4, 1),
    ("across", 4, 2),
    ("across", 4, 3),
    ("relay", 5, 3, (1,)),
    ("relay", 5, 3, (-1,)),
    ("finish", 4),
    ("finish", 5),
)
BACKWARD_STEPS = (
    (
        ("hidden",),
        ("weight", 5),
        ("core_send", 5),
        ("normed_two",),
        ("weight", 4),
        ("core_send", 4),
        ("core_add", 5),
        ("x_send", 5),
        ("core_add", 4),
        ("z_step", 4, 3, (1,)),
        ("z_step", 4, 3, (-1,)),
        ("middle",),
        ("attended",),
        ("heads", 0),
        ("z_step", 4, 2, (1,)),
        ("weight", 3),
        ("core_send", 3),
        ("z_step", 4, 2, (-1,)),
        ("heads", 1),
        ("core_add", 3),
        ("x_send", 3),
        ("z_step", 5, 3, (1,)),
        ("z_step", 4, 1, (1,)),
        ("normed",),
        ("weight", 2),
        ("z_step", 5, 3, (-1,)),
        ("z_step", 4, 1, (-1,)),
        ("z_step", 5, 2, (-1,)),
        ("z_step", 3, 3, (-1,)),
        ("weight", 0),
        ("core_send", 0),
        ("weight", 1),
        ("core_add", 0),
        ("x_send", 0),
        ("input",),
        ("core_send", 1),
        ("core_add", 1),
        ("x_send", 1),
        ("z_step", 3, 3, (1,)),
        ("z_step", 0, 3, (-1,)),
        ("z_step", 0, 2, (-1,)),
        ("z_step", 3, 2, (-1,)),
        ("small", 0),
        ("small", 1),
        ("z_step", 5, 1, (-1,)),
        ("z_step", 5, 2, (1,)),
        ("z_step", 5, 1, (1,)),
        ("z_step", 0, 1, (-1,)),
        ("core_send", 2),
        ("core_add", 2),
        ("x_send", 2),
        ("z_step", 3, 2, (1,)),
        ("z_step", 3, 1, (1,)),
        ("z_step", 0, 3, (1,)),
        ("z_step", 0, 2, (1,)),
        ("z_step", 0, 1, (1,)),
        ("z_step", 1, 3, (-1,)),
        ("z_step", 3, 1, (-1,)),
        ("z_step", 1, 3, (1,)),
        ("z_step", 1, 2, (-1,)),
        ("z_step", 2, 3, (-1,)),
        ("small", 2),
        ("turn", 4),
        ("z_step", 1, 1, (-1,)),
        ("close", 5),
        ("z_step", 2, 2, (-1,)),
        ("z_step", 1, 2, (1,)),
        ("z_step", 1, 1, (1,)),
        ("close", 3),
        ("z_step", 2, 3, (1,)),
        ("z_step", 2, 2, (1,)),
        ("small", 3),
        ("small", 4),
        ("close", 0),
        ("z_step", 2, 1, (1,)),
        ("z_step", 2, 1, (-1,)),
        ("close", 4),
        ("close", 1),
        ("close", 2),
    ),
    (
        ("hidden",),
        ("normed_two",),
        ("middle",),
        ("attended",),
        ("heads", 0),
        ("heads", 1),
        ("normed",),
        ("input",),
        ("weight", 5),
        ("core_send", 5),
        ("weight", 4),
        ("core_send", 4),
        ("core_add", 5),
        ("x_send", 5),
        ("core_add", 4),
        ("z_step", 4, 3, (1,)),
        ("z_step", 4, 3, (-1,)),
        ("z_step", 4, 2, (1,)),
        ("weight", 3),
        ("core_send", 3),
        ("z_step", 4, 2, (-1,)),
        ("core_add", 3),
        ("x_send", 3),
        ("z_step", 5, 3, (1,)),
        ("z_step", 4, 1, (1,)),
        ("weight", 2),
        ("z_step", 5, 3, (-1,)),
        ("z_step", 4, 1, (-1,)),
        ("z_step", 5, 2, (-1,)),
        ("z_step", 3, 3, (-1,)),
        ("weight", 0),
        ("core_send", 0),
        ("weight", 1),
        ("core_add", 0),
        ("x_send", 0),
        ("core_send", 1),
        ("core_add", 1),
        ("x_send", 1),
        ("z_step", 3, 3, (1,)),
        ("z_step", 0, 3, (-1,)),
        ("z_step", 0, 2, (-1,)),
        ("z_step", 3, 2, (-1,)),
        ("small", 0),
        ("small", 1),
        ("z_step", 5, 1, (-1,)),
        ("z_step", 5, 2, (1,)),
        ("z_step", 5, 1, (1,)),
        ("z_step", 0, 1, (-1,)),
        ("core_send", 2),
        ("core_add", 2),
        ("x_send", 2),
        ("z_step", 3, 2, (1,)),
        ("z_step", 3, 1, (1,)),
        ("z_step", 0, 3, (1,)),
        ("z_step", 0, 2, (1,)),
        ("z_step", 0, 1, (1,)),
        ("z_step", 1, 3, (-1,)),
        ("z_step", 3, 1, (-1,)),
        ("z_step", 1, 3, (1,)),
        ("z_step", 1, 2, (-1,)),
        ("z_step", 2, 3, (-1,)),
        ("small", 2),
        ("turn", 4),
        ("z_step", 1, 1, (-1,)),
        ("close", 5),
        ("z_step", 2, 2, (-1,)),
        ("z_step", 1, 2, (1,)),
        ("z_step", 1, 1, (1,)),
        ("close", 3),
        ("z_step", 2, 3, (1,)),
        ("z_step", 2, 2, (1,)),
        ("small", 3),
        ("small", 4),
        ("close", 0),
        ("z_step", 2, 1, (1,)),
        ("z_step", 2, 1, (-1,)),
        ("close", 4),
        ("close", 1),
        ("close", 2),
    ),
)


class Gather:
    def __init__(self, where, view, sems):
        self.where, self.view = where, view
        self.send_sem, self.recv_sem, self.core_send, self.core_recv = sems

    def ship(self, p, zz, xx, way, cond, wait):
        s, z, x, c = self.where
        i = zz * 2 + xx
        block = self.view(p, zz, xx, c)
        if way < 3:
            target = (
                device(s, clipped(z + 1), x, c),
                device(s, clipped(z - 1), x, c),
                device(s, z, 1 - x, c),
            )[way]
            cp = remote(block, block, self.send_sem.at[p, i, way], self.recv_sem.at[p, i], target)
        else:
            cp = remote(block, block, self.core_send.at[p, i], self.core_recv.at[p, i], device(s, z, x, 1 - c))
        act = cp.wait_send if wait else cp.start
        if cond is None:
            act()
        else:
            pl.when(cond)(act)

    def arrived(self, p, zz, xx):
        s, z, x, c = self.where
        block = self.view(p, zz, xx, c)
        i = zz * 2 + xx
        remote(block, block, self.send_sem.at[p, i, 0], self.recv_sem.at[p, i], device(s, z, 1 - x, c)).wait_recv()

    def own(self, p, wait=False):
        s, z, x, c = self.where
        for way, cond in ((0, z < NZ - 1), (1, z > 0), (2, None), (3, None)):
            self.ship(p, z, x, way, cond, wait)

    def turn(self, p, wait=False):
        s, z, x, c = self.where
        if not wait:
            self.arrived(p, z, 1 - x)
        self.ship(p, z, 1 - x, 0, z < NZ - 1, wait)
        self.ship(p, z, 1 - x, 1, z > 0, wait)
        self.ship(p, z, 1 - x, 3, None, wait)

    def relay(self, p, d, signs=(-1, 1), wait=False):
        s, z, x, c = self.where
        for sign in signs:
            way = 0 if sign < 0 else 1
            zz = clipped(z + sign * d)
            here = inside(z + sign * d)
            for xx in (x, 1 - x) if p == FIRST_IN else (x,):
                if not wait:
                    pl.when(here)(lambda zz=zz, xx=xx: self.arrived(p, zz, xx))
                self.ship(p, zz, xx, way, here & inside(z - sign), wait)
                if p != FIRST_IN:
                    self.ship(p, zz, xx, 2, here, wait)
                self.ship(p, zz, xx, 3, here, wait)

    def across(self, p, d, wait=False):
        s, z, x, c = self.where
        for sign in (-1, 1) if d else (1,):
            zz = clipped(z + sign * d)
            here = inside(z + sign * d)
            if not wait:
                pl.when(here)(lambda zz=zz: self.arrived(p, zz, 1 - x))
            self.ship(p, zz, 1 - x, 3, here, wait)

    def finish(self, p):
        s, z, x, c = self.where
        for zz in range(NZ):
            for xx in range(2):
                block = self.view(p, zz, xx, 1 - c)
                i = zz * 2 + xx
                remote(block, block, self.core_send.at[p, i], self.core_recv.at[p, i], device(s, z, x, 1 - c)).wait_recv()

    def drain(self, p):
        self.own(p, True)
        if p == FIRST_IN:
            self.turn(p, True)
        for d in range(NZ):
            if d:
                self.relay(p, d, wait=True)
            if p != FIRST_IN:
                self.across(p, d, True)


def add_block(dst, src):
    dst[...] = (dst[...].astype(F32) + src[...].astype(F32)).astype(BF16)


class Scatter:
    def __init__(self, where, view, bufs, sems, store):
        self.where, self.view, self.store = where, view, store
        self.got_core, self.got_x, self.got_z, self.got_zz = bufs
        self.core_s, self.core_r, self.x_s, self.x_r, self.z_s, self.z_r = sems

    def core_copy(self, p, i):
        s, z, x, c = self.where
        return remote(
            self.view(p, i // 2, i % 2, 1 - c),
            self.got_core.at[p, i],
            self.core_s.at[p, i],
            self.core_r.at[p, i],
            device(s, z, x, 1 - c),
        )

    def core_send(self, p):
        for i in range(2 * NZ):
            self.core_copy(p, i).start()

    def core_add(self, p):
        c = self.where[3]

        @pl.loop(0, 2 * NZ)
        def _(i):
            self.core_copy(p, i).wait_recv()
            add_block(self.view(p, i // 2, i % 2, c), self.got_core.at[p, i])

    def x_slot(self, p, zz):
        return self.got_x.at[(PIECES - 1) * NZ if p == FIRST_OUT else (p - (p > FIRST_OUT)) * NZ + zz]

    def x_copy(self, p, zz):
        s, z, x, c = self.where
        return remote(
            self.view(p, zz, 1 - x, c),
            self.x_slot(p, zz),
            self.x_s.at[p, zz],
            self.x_r.at[p, zz],
            device(s, z, 1 - x, c),
        )

    def steps(self):
        z = self.where[1]
        for d in range(NZ - 1, 0, -1):
            for sign in (1, -1):
                yield d, clipped(z + sign * d), inside(z + sign * d), sign

    def x_send(self, p):
        for _, zz, here, _ in self.steps():
            pl.when(here)(lambda zz=zz: self.x_copy(p, zz).start())
        self.x_copy(p, self.where[1]).start()

    def x_add(self, p, zz):
        s, z, x, c = self.where
        self.x_copy(p, zz).wait_recv()
        add_block(self.view(p, zz, x, c), self.x_slot(p, zz))

    def slot(self, p, k, xx):
        return self.got_zz.at[xx, k] if p == FIRST_OUT else self.got_z.at[p - (p > FIRST_OUT), k]

    def z_copy(self, p, zz, xx, sign, k):
        s, z, x, c = self.where
        return remote(
            self.view(p, zz, xx, c),
            self.slot(p, k, xx),
            self.z_s.at[p, xx, zz],
            self.z_r.at[p, xx, k],
            device(s, clipped(z + sign), x, c),
        )

    def z_out(self, p, zz, xx, sign):
        k = jnp.where((sign < 0) & (self.where[1] + sign == zz), NZ, zz)
        return self.z_copy(p, zz, xx, sign, k)

    def cols(self, p):
        x = self.where[2]
        return (x, 1 - x) if p == FIRST_OUT else (x,)

    def z_take(self, p, zz, xx, k):
        self.z_copy(p, zz, xx, 1, k).wait_recv()
        add_block(self.view(p, zz, xx, self.where[3]), self.slot(p, k, xx))

    def z_step(self, p, distance, signs=(1, -1)):
        z = self.where[1]
        for d, zz, here, sign in self.steps():
            if d != distance or sign not in signs:
                continue

            @pl.when(here)
            def _(zz=zz, sign=sign):
                if p != FIRST_OUT:
                    self.x_add(p, zz)
                for xx in self.cols(p):
                    pl.when(inside(z - sign))(lambda xx=xx: self.z_take(p, zz, xx, zz))
                    self.z_out(p, zz, xx, sign).start()

    def z_last(self, p, xx):
        z = self.where[1]
        pl.when(z > 0)(lambda: self.z_take(p, z, xx, z))
        pl.when(z < NZ - 1)(lambda: self.z_take(p, z, xx, NZ))

    def turn(self, p):
        s, z, x, c = self.where
        self.z_last(p, 1 - x)
        self.x_copy(p, z).start()

    def close(self, p):
        s, z, x, c = self.where
        if p == FIRST_OUT:
            self.z_last(p, x)
            self.x_add(p, z)
        else:
            self.x_add(p, z)
            self.z_last(p, x)
        self.store(p, self.view(p, z, x, c))

    def drain(self, p):
        for i in range(2 * NZ):
            self.core_copy(p, i).wait_send()
        for _, zz, here, sign in self.steps():
            if p != FIRST_OUT:
                pl.when(here)(lambda zz=zz: self.x_copy(p, zz).wait_send())
            for xx in self.cols(p):
                pl.when(here)(lambda zz=zz, xx=xx, sign=sign: self.z_out(p, zz, xx, sign).wait_send())
        self.x_copy(p, self.where[1]).wait_send()


def head_windows():
    for k in range(8):
        start = HD * k // 128 * 128
        offset = HD * k - start
        span = 128 if offset + HD <= 128 else 256
        yield k, start, offset, span


def layers_kernel(
    n,
    tokens,
    cotangent,
    lengths,
    gain_block,
    scale,
    wq,
    wo,
    wu,
    wd,
    out_half,
    token_half,
    d_q,
    d_o,
    d_u,
    d_d,
    small_out,
    held,
    gain_all,
    gain_rows,
    hb,
    a1,
    qf,
    qb,
    kb,
    vb,
    prob,
    ob,
    mid,
    a2,
    up,
    hid,
    grad,
    dup,
    dmid,
    low,
    dob,
    give,
    sums,
    swap,
    got_core,
    got_x,
    got_z,
    got_zz,
    *sems,
):
    where = s, z, x, c = place()
    rows, width = hb.shape
    slots = cotangent.shape[1]
    half = width // 2
    group = 8 * HD
    g_sems, r_sems = sems[:4], sems[4:10]
    swap_s, swap_r, hand_s, hand_r, back_s, back_r, end_s, end_r, load_sem = sems[10:]
    across_y = device(1 - s, z, x, c)

    def weight_view(p, zz, xx, cc):
        return held.at[p, pl.ds(pl.multiple_of((zz * 4 + xx * 2 + cc) * n, 16), n)]

    def view(p, zz, xx, cc):
        if p == GAINS:
            return gain_all.at[zz * 4 + xx * 2 + cc]
        return weight_view(p, zz, xx, cc)

    def store(p, block):
        value = block[...].astype(F32)
        if p < 3:
            d_q[:, p * width : (p + 1) * width] = value
        else:
            (d_o, d_u, d_d)[p - 3][...] = value

    gather = Gather(where, view, g_sems)
    scatter = Scatter(where, weight_view, (got_core, got_x, got_z, got_zz), r_sems, store)


    def row_loop(fn):
        @pl.loop(0, rows // 32)
        def _(k):
            fn(pl.ds(pl.multiple_of(k * 32, 32), 32))

    def tiles(emit, value):
        for k in range(width // TILE):
            emit(slice(k * TILE, (k + 1) * TILE), value[:, k * TILE : (k + 1) * TILE])

    def project(p, a, emit):
        tiles(emit, jnp.dot(a[...], held[p], preferred_element_type=F32))

    def project_back(pieces, emit):
        total = None
        for p, a in pieces:
            term = contract_cols(a[...], held[p])
            total = term if total is None else total + term
        tiles(emit, total)

    def weight_grad(p, a, g):
        held[p] = contract_rows(a[...], g[...]).astype(BF16)

    def recip_of(value):
        return lax.rsqrt(jnp.mean(value * value, -1, keepdims=True) + NORM_EPS)

    def norm(src, row, dst):
        def part(r):
            value = src[r].astype(F32)
            dst[r] = (value * recip_of(value) * gain_rows[row : row + 1]).astype(BF16)

        row_loop(part)

    def put(ref):
        def emit(lanes, value):
            ref[:, lanes] = value.astype(ref.dtype)

        return emit

    def emit_query(lanes, value):
        qf[:, lanes] = value
        qb[:, lanes] = (value * scale[0:1, lanes]).astype(BF16)

    def emit_up(lanes, value):
        up[:, lanes] = value
        hid[:, lanes] = (value / (1.0 + jnp.exp(-value))).astype(BF16)

    def emit_mid(lanes, value):
        mid[:, lanes] = hb[:, lanes].astype(F32) + value

    def emit_out(lanes, value):
        give[:, lanes] = (mid[:, lanes] + value).astype(BF16)

    def lane_mask(offset, span):
        lane = lax.broadcasted_iota(jnp.int32, (1, span), 1)
        return ((lane >= offset) & (lane < offset + HD)).astype(F32).astype(BF16)

    def attention(body, first, last):
        @pl.loop(2 * first, 2 * last)
        def _(it):
            seq, g = it // 2, it % 2
            r = pl.ds(pl.multiple_of(seq * slots, slots), slots)

            def window(ref, start, span):
                return ref[r, pl.ds(pl.multiple_of(g * group + start, 128), span)]

            body(it, seq, r, g, window)

    def spread(total, start, span, value):
        for j in range(span // 128):
            k = start // 128 + j
            term = value[:, j * 128 : (j + 1) * 128]
            total[k] = term if total[k] is None else total[k] + term

    def attend(it, seq, r, g, window):
        allowed = causal_allowed(slots, lengths[seq])
        total = [None] * (group // 128)
        for k, start, offset, span in head_windows():
            only = lane_mask(offset, span)
            scores = contract_cols(window(qb, start, span) * only, window(kb, start, span))
            scores = jnp.where(allowed, scores, NEG_FILL)
            expd = jnp.exp(scores - jnp.max(scores, -1, keepdims=True))
            probs = expd / jnp.sum(expd, -1, keepdims=True)
            prob[it, k] = probs
            value = jnp.dot(probs.astype(BF16), window(vb, start, span) * only, preferred_element_type=F32)
            spread(total, start, span, value)
        for k, value in enumerate(total):
            ob[r, pl.ds(pl.multiple_of(g * group + k * 128, 128), 128)] = value.astype(BF16)

    def attend_back(it, seq, r, g, window):
        count = group // 128
        t_q, t_k, t_v = [None] * count, [None] * count, [None] * count
        for k, start, offset, span in head_windows():
            only = lane_mask(offset, span)
            d_o_part = window(dob, start, span) * only
            probs = prob[it, k]
            d_probs = contract_cols(d_o_part, window(vb, start, span))
            spread(t_v, start, span, contract_rows(probs.astype(BF16), d_o_part))
            d_scores = probs * (d_probs - jnp.sum(probs * d_probs, -1, keepdims=True))
            d_scores = d_scores.astype(BF16)
            spread(t_q, start, span, jnp.dot(d_scores, window(kb, start, span) * only, preferred_element_type=F32))
            spread(t_k, start, span, contract_rows(d_scores, window(qb, start, span) * only))
        for k in range(count):
            lanes = pl.ds(pl.multiple_of(g * group + k * 128, 128), 128)
            products = t_q[k] * qf[r, lanes]
            sums[2, :, lanes] += jnp.sum(products.reshape(slots // 8, 8, 128), 0)
            qb[r, lanes] = (t_q[k] * scale[0:1, lanes]).astype(BF16)
            kb[r, lanes] = t_k[k].astype(BF16)
            vb[r, lanes] = t_v[k].astype(BF16)

    def emit_dup(lanes, value):
        u = up[:, lanes]
        sig = 1.0 / (1.0 + jnp.exp(-u))
        dup[:, lanes] = (value * sig * (1.0 + u * (1.0 - sig))).astype(BF16)

    def norm_grad(row, src, base, emit):
        def part(r):
            value, d_normed = src[r].astype(F32), up[r]
            recip = recip_of(value)
            sums[row] += jnp.sum((d_normed * value * recip).reshape(4, 8, width), 0)
            emit(r, base[r].astype(F32) + norm_back(value, recip, d_normed * gain_rows[row : row + 1]))

        row_loop(part)

    def emit_dmid(r, value):
        dmid[r] = value
        low[r] = value.astype(BF16)

    def emit_give(r, value):
        give[r] = value.astype(BF16)

    def spread_gains():
        gain_rows[...] = jnp.zeros_like(gain_rows)
        for f in range(4 * NZ):
            start = min(n * f // 128 * 128, width - 256)
            block = jnp.concatenate([gain_all[f], jnp.zeros((8, 128), F32)], -1)
            block = pltpu.roll(block, n * f - start, 1) if n * f > start else block
            gain_rows[:, start : start + 256] += block

    def forward_stage(p):
        if p == 0:
            spread_gains()
            norm(hb, 0, a1)
            project(0, a1, emit_query)
        elif p == 1:
            project(1, a1, put(kb))
        elif p == 2:
            project(2, a1, put(vb))
            attention(attend, 0, rows // slots)
        elif p == 3:
            project(3, ob, emit_mid)
            norm(mid, 1, a2)
        elif p == 4:
            project(4, a2, emit_up)
        else:
            project(5, hid, emit_out)


    def hand(k):
        r = pl.ds(k * slots, slots)
        return remote(give.at[r], hb.at[r], hand_s.at[k], hand_r.at[k], across_y)

    def back(k):
        r = pl.ds(k * slots, slots)
        return remote(give.at[r], grad.at[r], back_s.at[k], back_r.at[k], across_y)

    def end(which):
        dst, col = ((out_half, 0), (token_half, half))[which]
        return remote(give.at[:, col : col + half], dst, end_s.at[which], end_r.at[which], across_y)


    mine = pl.ds(pl.multiple_of((z * 4 + x * 2 + c) * n, 16), n)
    for k in range(3):
        held[k, mine] = wq[:, k * width : (k + 1) * width].astype(BF16)
    for k, ref in enumerate((wo, wu, wd)):
        held[3 + k, mine] = ref[...].astype(BF16)
    gain_all[z * 4 + x * 2 + c] = gain_block[...]
    sums[...] = jnp.zeros_like(sums)
    def load(k, wait=False):
        r = pl.ds(k * slots, slots)

        def first():
            cp = pltpu.make_async_copy(tokens.at[k], hb.at[r], load_sem.at[k])
            cp.wait() if wait else cp.start()

        def second():
            cp = pltpu.make_async_copy(cotangent.at[k], grad.at[r], load_sem.at[k])
            cp.wait() if wait else cp.start()

        pl.when(s == 0)(first)
        pl.when(s == 1)(second)

    for k in range(rows // slots):
        load(k)
    neighbour_barrier(s, z, x, c)
    for k in range(rows // slots):
        load(k, True)

    def gather_steps(steps):
        for step in steps:
            getattr(gather, step[0])(*step[1:])

    @pl.loop(0, 2)
    def _(phase):
        @pl.when((phase == 1) & (s == 1))
        def _():
            for k in range(rows // slots):
                hand(k).wait_recv()

        run = []
        for step in GATHER_STEPS:
            run.append(step)
            if step[0] == "finish":
                now, run = run, []
                pl.when(phase == 0)(lambda: gather_steps(now))
                if step[1] != GAINS:
                    pl.when(phase == s)(lambda: forward_stage(step[1]))

        @pl.when((phase == 0) & (s == 0))
        def _():
            for k in range(rows // slots):
                hand(k).start()

    for p in range(PIECES + 1):
        gather.drain(p)

    @pl.when(s == 0)
    def _():
        for k in range(rows // slots):
            hand(k).wait_send()
            back(k).wait_recv()

    @pl.when(s == 1)
    def _():
        end(0).start()
        out_half[...] = give[:, half:]
        for k in range(rows // slots):
            row = lax.broadcasted_iota(jnp.int32, (slots, 1), 0)
            live = (row < lengths[k]).astype(F32)
            part = pl.ds(k * slots, slots)
            grad[part] = (grad[part].astype(F32) * live).astype(BF16)

    grads = ((a1, qb), (a1, kb), (a1, vb), (ob, low), (a2, dup), (hid, grad))

    def exchange(k):
        partner = (
            device(s, z, x, 1 - c),
            device(s, z, 1 - x, c),
            device(s, z + 1 - 2 * (z % 2), x, c),
            device(s, (z + 2) % NZ, x, c),
        )[k]
        return remote(swap.at[k, 0], swap.at[k, 1], swap_s.at[k], swap_r.at[k], partner)

    def small(k):
        if k == 0:
            totals = [jnp.sum(sums[i], 0, keepdims=True) for i in range(3)]
            swap[0, 0] = jnp.concatenate(totals + [jnp.zeros((5, width), F32)], 0)
            exchange(0).start()
            return
        exchange(k - 1).wait_recv()
        value = swap[k - 1, 0] + swap[k - 1, 1]
        if k < 4:
            swap[k, 0] = value
            exchange(k).start()
        else:
            small_out[...] = value

    def finish_input(section):
        if section == 1:
            end(0).wait_send()
        norm_grad(0, hb, dmid, emit_give)
        if section == 1:
            for k in range(rows // slots):
                back(k).start()
        else:
            end(1).start()
            token_half[...] = give[:, :half]

    compute = dict(
        hidden=lambda section: project_back([(5, grad)], emit_dup),
        normed_two=lambda section: project_back([(4, dup)], put(up)),
        middle=lambda section: norm_grad(1, mid, grad, emit_dmid),
        attended=lambda section: project_back([(3, low)], put(dob)),
        heads=lambda section, k: attention(attend_back, k, k + 1),
        normed=lambda section: project_back([(0, qb), (1, kb), (2, vb)], put(up)),
        input=finish_input,
        weight=lambda section, p: weight_grad(p, *grads[p]),
        small=lambda section, k: small(k),
    )

    def backward(section):
        for step in BACKWARD_STEPS[section]:
            if step[0] in compute:
                compute[step[0]](section, *step[1:])
            else:
                getattr(scatter, step[0])(*step[1:])

    pl.when(s == 0)(lambda: backward(0))
    pl.when(s == 1)(lambda: backward(1))
    for p in range(PIECES):
        scatter.drain(p)
    for k in range(4):
        exchange(k).wait_send()

    @pl.when(s == 0)
    def _():
        end(1).wait_send()
        end(0).wait_recv()

    @pl.when(s == 1)
    def _():
        for k in range(rows // slots):
            back(k).wait_send()
        end(1).wait_recv()


def near_shards(
    tokens, cotangent, lengths, qkv_weight, out_weight, up_weight, down_weight, norm_gains, query_gain
):
    n, width = out_weight.shape
    count, slots, _ = tokens.shape
    rows = count * slots
    factor = LOG_BASE / math.sqrt(HD)
    scale = jnp.tile(jax.nn.softplus(query_gain) * factor, (8, H))
    gains = norm_gains.astype(BF16).astype(F32).T
    gain_block = jnp.pad(gains, ((0, 6), (0, 128 - n)))
    dma = pltpu.SemaphoreType.DMA
    whole = pl.BlockSpec(memory_space=pltpu.VMEM)
    block = (n, width)
    low_rows = pltpu.VMEM((rows, width), BF16)
    wide_rows = pltpu.VMEM((rows, width), F32)
    scratch = dict(
        held=pltpu.VMEM((PIECES, 4 * NZ * n, width), BF16),
        gain_all=pltpu.VMEM((4 * NZ, 8, 128), F32),
        gain_rows=pltpu.VMEM((8, width), F32),
        hb=low_rows,
        a1=low_rows,
        qf=wide_rows,
        qb=low_rows,
        kb=low_rows,
        vb=low_rows,
        prob=pltpu.VMEM((2 * count, 8, slots, slots), F32),
        ob=low_rows,
        mid=wide_rows,
        a2=low_rows,
        up=wide_rows,
        hid=low_rows,
        grad=low_rows,
        dup=low_rows,
        dmid=wide_rows,
        low=low_rows,
        dob=low_rows,
        give=low_rows,
        sums=pltpu.VMEM((3, 8, width), F32),
        swap=pltpu.VMEM((4, 2, 8, width), F32),
        got_core=pltpu.VMEM((PIECES, 2 * NZ) + block, BF16),
        got_x=pltpu.VMEM(((PIECES - 1) * NZ + 1,) + block, BF16),
        got_z=pltpu.VMEM((PIECES - 1, NZ + 1) + block, BF16),
        got_zz=pltpu.VMEM((2, NZ + 1) + block, BF16),
    )
    semaphores = [
        dma((PIECES + 1, 2 * NZ, 3)),
        dma((PIECES + 1, 2 * NZ)),
        dma((PIECES + 1, 2 * NZ)),
        dma((PIECES + 1, 2 * NZ)),
        dma((PIECES, 2 * NZ)),
        dma((PIECES, 2 * NZ)),
        dma((PIECES, NZ)),
        dma((PIECES, NZ)),
        dma((PIECES, 2, NZ)),
        dma((PIECES, 2, NZ + 1)),
        dma((4,)),
        dma((4,)),
        dma((count,)),
        dma((count,)),
        dma((count,)),
        dma((count,)),
        dma((2,)),
        dma((2,)),
        dma((count,)),
    ]
    half = jax.ShapeDtypeStruct((rows, width // 2), BF16)
    out, d_tokens, d_q, d_o, d_u, d_d, small = pl.pallas_call(
        lambda *refs: layers_kernel(n, *refs),
        out_shape=(
            half,
            half,
            jax.ShapeDtypeStruct((n, 3 * width), F32),
            jax.ShapeDtypeStruct(block, F32),
            jax.ShapeDtypeStruct(block, F32),
            jax.ShapeDtypeStruct(block, F32),
            jax.ShapeDtypeStruct((8, width), F32),
        ),
        in_specs=[pl.BlockSpec(memory_space=pl.ANY)] * 2 + [pl.BlockSpec(memory_space=pltpu.SMEM)] + [whole] * 6,
        out_specs=(whole,) * 7,
        scratch_shapes=list(scratch.values()) + semaphores,
        compiler_params=pltpu.CompilerParams(
            collective_id=1, has_side_effects=True, vmem_limit_bytes=63 << 20
        ),
        name="two_layers",
    )(tokens, cotangent, lengths, gain_block, scale, qkv_weight, out_weight, up_weight, down_weight)
    own = lax.dynamic_slice_in_dim(small[:2], lax.axis_index("fsdp") * n, n, 1).T
    d_scale = jnp.sum(small[2].reshape(H, HD), 0)
    d_query_gain = (d_scale * jax.nn.sigmoid(query_gain[0]) * factor)[None]
    shape = (count, slots, width // 2)
    return (
        out.reshape(shape),
        d_tokens.reshape(shape),
        d_q[None],
        d_o[None],
        d_u[None],
        d_d[None],
        own[None],
        d_query_gain,
    )


def swapped(value, axis, bit):
    return lax.ppermute(value, axis, [(i, i ^ 1 << bit) for i in range(lax.axis_size(axis))])


def causal_allowed(row_count, length):
    row_ids = lax.broadcasted_iota(jnp.int32, (row_count, row_count), 0)
    col_ids = lax.broadcasted_iota(jnp.int32, (row_count, row_count), 1)
    return (col_ids <= row_ids) & (col_ids < length)


def contract_rows(left, right):
    return lax.dot_general(
        left, right, (((0,), (0,)), ((), ())), preferred_element_type=jnp.float32
    )


def contract_cols(left, right):
    return lax.dot_general(
        left, right, (((1,), (1,)), ((), ())), preferred_element_type=jnp.float32
    )


def norm_back(source, recip, grad_flat):
    return recip * grad_flat - source * recip**3 * jnp.mean(grad_flat * source, -1, keepdims=True)


def layer_forward(layer_input, length, weights, query_scale):
    qkv_w, out_w, up_w, down_w, gain_pair = weights
    row_count, width = layer_input.shape
    gain_one = gain_pair[:, 0].astype(jnp.float32)
    gain_two = gain_pair[:, 1].astype(jnp.float32)
    recip_one = lax.rsqrt(jnp.mean(layer_input * layer_input, -1, keepdims=True) + NORM_EPS)
    normed = (layer_input * recip_one * gain_one).astype(jnp.bfloat16)
    proj = jnp.dot(normed, qkv_w, preferred_element_type=jnp.float32)
    query = proj[:, :width].reshape(row_count, H, HD)
    query_b = (query * query_scale).astype(jnp.bfloat16)
    keys_b = proj[:, width : 2 * width].astype(jnp.bfloat16).reshape(row_count, H, HD)
    values_b = proj[:, 2 * width :].astype(jnp.bfloat16).reshape(row_count, H, HD)
    scores = jnp.einsum("qhd,khd->hqk", query_b, keys_b, preferred_element_type=jnp.float32)
    scores = jnp.where(causal_allowed(row_count, length)[None], scores, NEG_FILL)
    row_peak = jnp.max(scores, -1, keepdims=True)
    expd = jnp.exp(scores - row_peak)
    row_total = jnp.sum(expd, -1, keepdims=True)
    probs = expd / row_total
    logsum = (row_peak + jnp.log(row_total))[..., 0]
    attended = (
        jnp.einsum(
            "hqk,khd->qhd", probs.astype(jnp.bfloat16), values_b, preferred_element_type=jnp.float32
        )
        .reshape(row_count, width)
        .astype(jnp.bfloat16)
    )
    middle = layer_input + jnp.dot(attended, out_w, preferred_element_type=jnp.float32)
    recip_two = lax.rsqrt(jnp.mean(middle * middle, -1, keepdims=True) + NORM_EPS)
    normed_two = (middle * recip_two * gain_two).astype(jnp.bfloat16)
    upper = jnp.dot(normed_two, up_w, preferred_element_type=jnp.float32)
    hidden = jax.nn.silu(upper).astype(jnp.bfloat16)
    layer_output = middle + jnp.dot(hidden, down_w, preferred_element_type=jnp.float32)
    saved = (
        layer_input,
        normed,
        query,
        query_b,
        keys_b,
        values_b,
        logsum,
        attended,
        middle,
        normed_two,
        upper,
        hidden,
        recip_one,
        recip_two,
    )
    return (layer_output, saved)


def layer_backward(saved, length, weights, query_scale, grad_output):
    qkv_w, out_w, up_w, down_w, gain_pair = weights
    (
        layer_input,
        normed,
        query,
        query_b,
        keys_b,
        values_b,
        logsum,
        attended,
        middle,
        normed_two,
        upper,
        hidden,
        recip_one,
        recip_two,
    ) = saved
    row_count, width = layer_input.shape
    gain_one = gain_pair[:, 0].astype(jnp.float32)
    gain_two = gain_pair[:, 1].astype(jnp.float32)
    grad_low = grad_output.astype(jnp.bfloat16)
    d_down = contract_rows(hidden, grad_low)
    d_hidden = contract_cols(grad_low, down_w)
    sigmoid_up = jax.nn.sigmoid(upper)
    d_upper = (d_hidden * sigmoid_up * (1.0 + upper * (1.0 - sigmoid_up))).astype(jnp.bfloat16)
    d_up = contract_rows(normed_two, d_upper)
    d_normed_two = contract_cols(d_upper, up_w)
    d_gain_two = jnp.sum(d_normed_two * middle * recip_two, 0)
    d_middle = grad_output + norm_back(middle, recip_two, d_normed_two * gain_two)
    middle_low = d_middle.astype(jnp.bfloat16)
    d_out = contract_rows(attended, middle_low)
    d_attended = contract_cols(middle_low, out_w).astype(jnp.bfloat16).reshape(row_count, H, HD)
    scores = jnp.einsum("qhd,khd->hqk", query_b, keys_b, preferred_element_type=jnp.float32)
    scores = jnp.where(causal_allowed(row_count, length)[None], scores, NEG_FILL)
    probs = jnp.exp(scores - logsum[..., None])
    d_probs = jnp.einsum("qhd,khd->hqk", d_attended, values_b, preferred_element_type=jnp.float32)
    d_values = jnp.einsum(
        "hqk,qhd->khd", probs.astype(jnp.bfloat16), d_attended, preferred_element_type=jnp.float32
    ).astype(jnp.bfloat16)
    d_scores = (probs * (d_probs - jnp.sum(probs * d_probs, -1, keepdims=True))).astype(
        jnp.bfloat16
    )
    d_query_s = jnp.einsum("hqk,khd->qhd", d_scores, keys_b, preferred_element_type=jnp.float32)
    d_keys = jnp.einsum(
        "hqk,qhd->khd", d_scores, query_b, preferred_element_type=jnp.float32
    ).astype(jnp.bfloat16)
    d_scale = jnp.sum(d_query_s * query, (0, 1))
    d_query = (d_query_s * query_scale).astype(jnp.bfloat16)
    d_proj = jnp.concatenate(
        [
            d_query.reshape(row_count, width),
            d_keys.reshape(row_count, width),
            d_values.reshape(row_count, width),
        ],
        -1,
    )
    d_qkv = contract_rows(normed, d_proj)
    d_normed = contract_cols(d_proj, qkv_w)
    d_gain_one = jnp.sum(d_normed * layer_input * recip_one, 0)
    d_input = d_middle + norm_back(layer_input, recip_one, d_normed * gain_one)
    d_gains = jnp.stack([d_gain_one, d_gain_two], -1)
    return (d_input, (d_qkv, d_out, d_up, d_down, d_gains), d_scale)


def shards(
    tokens,
    cotangent,
    lengths,
    qkv_weight,
    out_weight,
    up_weight,
    down_weight,
    norm_gains,
    query_gain,
):
    if lax.axis_size("fsdp") == 4 * NZ:
        return near_shards(
            tokens,
            cotangent,
            lengths,
            qkv_weight[0],
            out_weight[0],
            up_weight[0],
            down_weight[0],
            norm_gains[0],
            query_gain,
        )
    section_index = lax.axis_index("section")
    micro_count, slot_rows, width = tokens.shape
    half_width = width // 2
    scale_factor = LOG_BASE / math.sqrt(HD)
    query_scale = jax.nn.softplus(query_gain[0]) * scale_factor

    def gather_weights():
        pieces = (
            lax.all_gather(qkv_weight.astype(jnp.bfloat16), "fsdp", axis=1, tiled=True),
            lax.all_gather(out_weight.astype(jnp.bfloat16), "fsdp", axis=1, tiled=True),
            lax.all_gather(up_weight.astype(jnp.bfloat16), "fsdp", axis=1, tiled=True),
            lax.all_gather(down_weight.astype(jnp.bfloat16), "fsdp", axis=1, tiled=True),
            lax.all_gather(norm_gains.astype(jnp.bfloat16), "fsdp", axis=1, tiled=True),
        )
        return tuple((piece[0] for piece in pieces))

    def handoff(value):
        return swapped(value, "section", 0)

    weights = gather_weights()
    received = jnp.zeros((slot_rows, width), jnp.bfloat16)
    kept = []
    result_parts = []
    for tick_index in range(micro_count + 1):
        first_input = tokens[min(tick_index, micro_count - 1)].astype(jnp.float32)
        layer_input = jnp.where(section_index == 0, first_input, received.astype(jnp.float32))
        micro_index = jnp.clip(tick_index - section_index, 0, micro_count - 1)
        length = lengths[micro_index]
        layer_output, saved = layer_forward(layer_input, length, weights, query_scale)
        sent = layer_output.astype(jnp.bfloat16)
        received = handoff(sent)
        kept.append(saved)
        if tick_index >= 1:
            finished = jnp.where(section_index == 1, sent, received)
            result_parts.append(
                lax.dynamic_slice_in_dim(finished, section_index * half_width, half_width, 1)
            )
    output = jnp.stack(result_parts)
    weights = gather_weights()
    row_ids = lax.iota(jnp.int32, slot_rows)
    grad_received = jnp.zeros((slot_rows, width), jnp.bfloat16)
    grad_parts = []
    grad_totals = None
    scale_total = jnp.zeros((HD,), jnp.float32)
    for tick_index in range(micro_count + 1):
        offset = tick_index - 1 + section_index
        micro_index = jnp.clip(offset, 0, micro_count - 1)
        length = lengths[micro_index]
        live_tick = ((offset >= 0) & (offset < micro_count)).astype(jnp.float32)
        live_rows = (row_ids < length).astype(jnp.float32)[:, None]
        top_grad = cotangent[min(tick_index, micro_count - 1)].astype(jnp.float32) * live_rows
        grad_output = jnp.where(section_index == 1, top_grad, grad_received.astype(jnp.float32))
        saved = jax.tree.map(
            lambda early, late: jnp.where(section_index == 0, early, late),
            kept[max(tick_index - 1, 0)],
            kept[min(tick_index + 1, micro_count)],
        )
        d_input, weight_grads, scale_grad = layer_backward(
            saved, length, weights, query_scale, grad_output
        )
        weight_grads = tuple((item * live_tick for item in weight_grads))
        scale_total = scale_total + scale_grad * live_tick
        sent = d_input.astype(jnp.bfloat16)
        grad_received = handoff(sent)
        if tick_index >= 1:
            finished = jnp.where(section_index == 0, sent, grad_received)
            grad_parts.append(
                lax.dynamic_slice_in_dim(finished, section_index * half_width, half_width, 1)
            )
        if grad_totals is None:
            grad_totals = weight_grads
        else:
            grad_totals = tuple((total + piece for total, piece in zip(grad_totals, weight_grads)))
    d_tokens = jnp.stack(grad_parts)
    scattered = (
        lax.psum_scatter(grad_totals[0], "fsdp", scatter_dimension=0, tiled=True),
        lax.psum_scatter(grad_totals[1], "fsdp", scatter_dimension=0, tiled=True),
        lax.psum_scatter(grad_totals[2], "fsdp", scatter_dimension=0, tiled=True),
        lax.psum_scatter(grad_totals[3], "fsdp", scatter_dimension=0, tiled=True),
        lax.psum_scatter(grad_totals[4], "fsdp", scatter_dimension=0, tiled=True),
    )
    owned = tuple((item[None] for item in scattered))
    scale_sum = lax.psum(scale_total, "fsdp")
    d_query_gain = (scale_sum * jax.nn.sigmoid(query_gain[0]) * scale_factor)[None]
    return (output, d_tokens, owned[0], owned[1], owned[2], owned[3], owned[4], d_query_gain)


def solution(mesh):
    in_specs = (
        P("fsdp", None, None),
        P("fsdp", None, None),
        P("fsdp"),
        P("section", "fsdp", None),
        P("section", "fsdp", None),
        P("section", "fsdp", None),
        P("section", "fsdp", None),
        P("section", "fsdp", None),
        P("section", None),
    )
    out_specs = (
        P("fsdp", None, "section"),
        P("fsdp", None, "section"),
        P("section", "fsdp", None),
        P("section", "fsdp", None),
        P("section", "fsdp", None),
        P("section", "fsdp", None),
        P("section", "fsdp", None),
        P("section", None),
    )
    return jax.shard_map(shards, mesh=mesh, in_specs=in_specs, out_specs=out_specs, check_vma=False)
```

```python
import math

import jax
import jax.numpy as jnp
from jax import lax
from jax.experimental import pallas as pl
from jax.experimental.pallas import tpu as pltpu
from jax.sharding import PartitionSpec as P

H = 16
HD = 80


NORM_EPS = 1e-06
NEG_FILL = -1e30
LOG_BASE = 1.442695041


MESH_ID = pl.DeviceIdType.MESH
BF16 = jnp.bfloat16
F32 = jnp.float32
NZ = 4
TILE = 256
PIECES = 6
GAINS = 6
LENT = 7
LENT_IN = 5
TURN_IN = (4, 5)
LENT_OUT = 5
LENT_SUM = 6
TURN_OUT = (4, 4)


def place():
    s, f = lax.axis_index("section"), lax.axis_index("fsdp")
    return s, f // 4, (f // 2) % 2, f % 2


def device(s, z, x, c):
    return (s, z * 4 + x * 2 + c)


def inside(z):
    return (z >= 0) & (z < NZ)


def clipped(z):
    return jnp.clip(z, 0, NZ - 1)


def neighbour_barrier(s, z, x, c):
    barrier = pltpu.get_barrier_semaphore()

    def tell(target):
        pl.semaphore_signal(barrier, inc=1, device_id=target, device_id_type=MESH_ID)

    tell(device(s, z, x, 1 - c))
    tell(device(s, z, 1 - x, c))
    tell(device(1 - s, z, x, c))
    tell(device(s, (z + 2) % NZ, x, c))
    pl.when(z > 0)(lambda: tell(device(s, z - 1, x, c)))
    pl.when(z < NZ - 1)(lambda: tell(device(s, z + 1, x, c)))
    pl.semaphore_wait(barrier, 4 + (z > 0).astype(jnp.int32) + (z < NZ - 1).astype(jnp.int32))


def remote(src, dst, send_sem, recv_sem, target):
    return pltpu.make_async_remote_copy(
        src, dst, send_sem, recv_sem, device_id=target, device_id_type=MESH_ID
    )


GATHER_STEPS = (
    (
        ("own", 0),
        ("own", 2),
        ("own", 6),
        ("own", 4),
        ("own", 5),
        ("relay", 2, 1, (-1,)),
        ("own", 1),
        ("relay", 0, 1, (-1,)),
        ("relay", 0, 1, (1,)),
        ("relay", 0, 2, (-1,)),
        ("relay", 6, 1, (1,)),
        ("relay", 6, 1, (-1,)),
        ("relay", 2, 1, (1,)),
        ("relay", 6, 2, (1,)),
        ("relay", 1, 1, (-1,)),
        ("relay", 0, 2, (1,)),
        ("relay", 0, 3, (-1,)),
        ("relay", 6, 2, (-1,)),
        ("relay", 6, 3, (-1,)),
        ("relay", 1, 1, (1,)),
        ("relay", 1, 2, (-1,)),
        ("turn", 4),
        ("relay", 1, 2, (1,)),
        ("relay", 1, 3, (-1,)),
        ("relay", 0, 3, (1,)),
        ("across", 0, 0),
        ("relay", 6, 3, (1,)),
        ("across", 6, 0),
        ("across", 6, 1),
        ("relay", 2, 2, (-1,)),
        ("relay", 2, 2, (1,)),
        ("relay", 2, 3, (-1,)),
        ("across", 6, 2),
        ("across", 0, 1),
        ("across", 6, 3),
        ("own", 3),
        ("relay", 2, 3, (1,)),
        ("relay", 4, 1, (1,)),
        ("relay", 3, 1, (-1,)),
        ("home", 5, 0),
        ("home", 5, 1),
        ("relay", 1, 3, (1,)),
        ("across", 1, 0),
        ("across", 2, 0),
        ("home", 5, 2),
        ("across", 1, 1),
        ("relay", 4, 1, (-1,)),
        ("relay", 4, 2, (1,)),
        ("across", 1, 2),
        ("across", 2, 1),
        ("finish", 6),
        ("home", 5, 3),
        ("across", 2, 2),
        ("across", 2, 3),
        ("across", 1, 3),
        ("relay", 4, 2, (-1,)),
        ("across", 0, 2),
        ("across", 0, 3),
        ("finish", 0),
        ("stage", 0),
        ("relay", 3, 1, (1,)),
        ("finish", 5),
        ("relay", 3, 2, (-1,)),
        ("finish", 1),
        ("stage", 1),
        ("finish", 2),
        ("relay", 4, 3, (-1,)),
        ("relay", 4, 3, (1,)),
        ("finish", 4),
        ("relay", 3, 2, (1,)),
        ("relay", 3, 3, (-1,)),
        ("relay", 3, 3, (1,)),
        ("across", 3, 0),
        ("stage", 2),
        ("across", 3, 1),
        ("across", 3, 2),
        ("across", 3, 3),
        ("finish", 3),
        ("stage", 3),
        ("stage", 4),
        ("stage", 5),
    ),
    (
        ("own", 5),
        ("own", 0),
        ("own", 7),
        ("relay", 0, 1, (-1,)),
        ("relay", 7, 1, (-1,)),
        ("own", 6),
        ("own", 2),
        ("relay", 7, 1, (1,)),
        ("relay", 6, 1, (-1,)),
        ("relay", 7, 2, (-1,)),
        ("relay", 6, 1, (1,)),
        ("relay", 7, 2, (1,)),
        ("relay", 6, 2, (-1,)),
        ("relay", 7, 3, (-1,)),
        ("relay", 0, 1, (1,)),
        ("relay", 0, 2, (1,)),
        ("turn", 5),
        ("relay", 5, 1, (-1,)),
        ("relay", 6, 2, (1,)),
        ("own", 4),
        ("relay", 7, 3, (1,)),
        ("across", 7, 0),
        ("own", 3),
        ("own", 1),
        ("across", 7, 1),
        ("across", 7, 2),
        ("across", 7, 3),
        ("relay", 2, 1, (-1,)),
        ("relay", 1, 1, (1,)),
        ("relay", 6, 3, (1,)),
        ("relay", 0, 2, (-1,)),
        ("relay", 0, 3, (1,)),
        ("relay", 1, 1, (-1,)),
        ("relay", 0, 3, (-1,)),
        ("relay", 2, 1, (1,)),
        ("relay", 2, 2, (1,)),
        ("relay", 4, 1, (1,)),
        ("relay", 6, 3, (-1,)),
        ("across", 6, 0),
        ("across", 0, 0),
        ("relay", 1, 2, (1,)),
        ("across", 6, 1),
        ("relay", 1, 2, (-1,)),
        ("relay", 1, 3, (1,)),
        ("relay", 2, 2, (-1,)),
        ("relay", 2, 3, (1,)),
        ("relay", 1, 3, (-1,)),
        ("across", 6, 2),
        ("relay", 3, 1, (1,)),
        ("across", 0, 1),
        ("across", 0, 2),
        ("across", 0, 3),
        ("relay", 3, 1, (-1,)),
        ("relay", 5, 1, (1,)),
        ("relay", 3, 2, (-1,)),
        ("across", 1, 0),
        ("relay", 2, 3, (-1,)),
        ("relay", 3, 2, (1,)),
        ("relay", 3, 3, (-1,)),
        ("across", 1, 1),
        ("across", 1, 2),
        ("across", 2, 0),
        ("across", 2, 1),
        ("across", 2, 2),
        ("across", 2, 3),
        ("across", 1, 3),
        ("relay", 5, 2, (-1,)),
        ("relay", 4, 1, (-1,)),
        ("relay", 5, 2, (1,)),
        ("finish", 2),
        ("relay", 4, 2, (-1,)),
        ("finish", 1),
        ("relay", 3, 3, (1,)),
        ("finish", 0),
        ("across", 3, 0),
        ("across", 3, 1),
        ("relay", 5, 3, (1,)),
        ("across", 6, 3),
        ("relay", 5, 3, (-1,)),
        ("relay", 4, 2, (1,)),
        ("finish", 5),
        ("finish", 6),
        ("across", 3, 2),
        ("across", 3, 3),
        ("finish", 3),
        ("relay", 4, 3, (1,)),
        ("relay", 4, 3, (-1,)),
        ("across", 4, 0),
        ("across", 4, 1),
        ("hand",),
        ("stage", 0),
        ("stage", 1),
        ("stage", 2),
        ("across", 4, 2),
        ("across", 4, 3),
        ("stage", 3),
        ("finish", 4),
        ("stage", 4),
        ("stage", 5),
    ),
)
BACKWARD_STEPS = (
    (
        ("hidden",),
        ("normed_two",),
        ("weight", 4),
        ("core_send", 4),
        ("middle",),
        ("attended",),
        ("weight", 3),
        ("core_send", 3),
        ("core_add", 4),
        ("z_step", 4, 0),
        ("core_add", 3),
        ("weight", 5),
        ("core_send", 5),
        ("x_send", 3),
        ("heads", 1),
        ("z_step", 4, 1),
        ("heads", 0),
        ("normed",),
        ("weight", 0),
        ("z_step", 3, 0),
        ("core_send", 0),
        ("core_add", 0),
        ("x_send", 0),
        ("z_step", 4, 2),
        ("weight", 2),
        ("weight", 1),
        ("core_send", 1),
        ("core_add", 5),
        ("lend", 0),
        ("lend", 1),
        ("core_add", 1),
        ("input",),
        ("z_step", 0, 0),
        ("small", 0),
        ("small", 1),
        ("x_send", 1),
        ("z_step", 0, 1),
        ("z_step", 0, 2),
        ("core_send", 2),
        ("z_step", 1, 0),
        ("z_step", 3, 1),
        ("small", 2),
        ("core_add", 2),
        ("x_send", 2),
        ("close", 0),
        ("z_step", 1, 1),
        ("z_step", 1, 2),
        ("z_step", 2, 0),
        ("close", 1),
        ("z_step", 3, 2),
        ("z_step", 2, 1),
        ("turn", 4),
        ("z_step", 2, 2),
        ("small", 3),
        ("small", 4),
        ("close", 3),
        ("close", 4),
        ("close", 2),
        ("home",),
    ),
    (
        ("hidden",),
        ("normed_two",),
        ("middle",),
        ("attended",),
        ("weight", 5),
        ("core_send", 5),
        ("heads", 0),
        ("core_add", 5),
        ("x_send", 5),
        ("heads", 1),
        ("normed",),
        ("input",),
        ("weight", 3),
        ("core_send", 3),
        ("z_step", 5, 0),
        ("weight", 4),
        ("core_send", 4),
        ("core_add", 3),
        ("x_send", 3),
        ("weight", 0),
        ("core_send", 0),
        ("core_add", 4),
        ("z_step", 4, 0),
        ("core_add", 0),
        ("x_send", 0),
        ("weight", 2),
        ("core_send", 2),
        ("z_step", 5, 1),
        ("core_add", 2),
        ("x_send", 2),
        ("weight", 1),
        ("z_step", 4, 1),
        ("core_send", 1),
        ("small", 0),
        ("core_add", 1),
        ("z_step", 3, 0),
        ("z_step", 3, 1),
        ("z_step", 4, 2),
        ("small", 1),
        ("z_step", 0, 0),
        ("z_step", 5, 2),
        ("z_step", 2, 0),
        ("z_step", 2, 1),
        ("z_step", 2, 2),
        ("x_send", 1),
        ("z_step", 0, 1),
        ("x_send", 6, 0, 1),
        ("small", 2),
        ("z_step", 0, 2),
        ("close", 2),
        ("z_step", 3, 2),
        ("close", 0),
        ("z_step", 1, 0),
        ("x_send", 6, 1, 2),
        ("x_send", 6, 2, 3),
        ("z_step", 6, 0),
        ("z_step", 6, 1),
        ("z_step", 6, 2),
        ("x_send", 6, 3, 4),
        ("small", 3),
        ("z_step", 1, 1),
        ("close", 6),
        ("z_step", 1, 2),
        ("turn", 4),
        ("small", 4),
        ("close", 3),
        ("close", 5),
        ("close", 1),
        ("close", 4),
    ),
)


class Gather:
    def __init__(self, where, section, view, sems):
        self.where, self.section, self.view = where, section, view
        self.send_sem, self.recv_sem, self.core_send, self.core_recv = sems

    def ship(self, p, zz, xx, way, cond, wait):
        s, z, x, c = self.where
        i = zz * 2 + xx
        block = self.view(p, zz, xx, c)
        if way < 3:
            target = (
                device(s, clipped(z + 1), x, c),
                device(s, clipped(z - 1), x, c),
                device(s, z, 1 - x, c),
            )[way]
            cp = remote(block, block, self.send_sem.at[p, i, way], self.recv_sem.at[p, i], target)
        elif way == 3:
            cp = remote(block, block, self.core_send.at[p, i], self.core_recv.at[p, i], device(s, z, x, 1 - c))
        else:
            q = LENT if self.section == 0 else LENT_IN
            there = self.view(q, zz, xx, c)
            cp = remote(block, there, self.send_sem.at[p, i, 3], self.recv_sem.at[q, i], device(1 - s, z, x, c))
        act = cp.wait_send if wait else cp.start
        if cond is None:
            act()
        else:
            pl.when(cond)(act)

    def arrived(self, p, zz, xx):
        s, z, x, c = self.where
        block = self.view(p, zz, xx, c)
        i = zz * 2 + xx
        remote(block, block, self.send_sem.at[p, i, 0], self.recv_sem.at[p, i], device(s, z, 1 - x, c)).wait_recv()

    def own(self, p, wait=False):
        s, z, x, c = self.where
        ways = ((0, z < NZ - 1), (1, z > 0), (2, None), (3, None))
        if p == LENT:
            ways = ways[:3]
            if not wait:
                self.arrived(p, z, x)
        elif self.section == 0 and p == LENT_IN:
            ways = ((4, None), (3, None))
        for way, cond in ways:
            self.ship(p, z, x, way, cond, wait)

    def turn(self, p, wait=False):
        s, z, x, c = self.where
        if not wait:
            self.arrived(p, z, 1 - x)
        self.ship(p, z, 1 - x, 0, z < NZ - 1, wait)
        self.ship(p, z, 1 - x, 1, z > 0, wait)
        self.ship(p, z, 1 - x, 3, None, wait)

    def relay(self, p, d, signs=(-1, 1), wait=False):
        s, z, x, c = self.where
        turned = p == TURN_IN[self.section]
        for sign in signs:
            way = 0 if sign < 0 else 1
            zz = clipped(z + sign * d)
            here = inside(z + sign * d)
            for xx in (x, 1 - x) if turned else (x,):
                if not wait:
                    pl.when(here)(lambda zz=zz, xx=xx: self.arrived(p, zz, xx))
                self.ship(p, zz, xx, way, here & inside(z - sign), wait)
                if not turned:
                    self.ship(p, zz, xx, 2, here, wait)
                self.ship(p, zz, xx, 4 if p == LENT else 3, here, wait)

    def across(self, p, d, wait=False):
        s, z, x, c = self.where
        for sign in (-1, 1) if d else (1,):
            zz = clipped(z + sign * d)
            here = inside(z + sign * d)
            if not wait:
                pl.when(here)(lambda zz=zz: self.arrived(p, zz, 1 - x))
            self.ship(p, zz, 1 - x, 4 if p == LENT else 3, here, wait)

    def home(self, p, d, wait=False):
        s, z, x, c = self.where
        for sign in (-1, 1) if d else (1,):
            zz = clipped(z + sign * d)
            here = inside(z + sign * d)
            for xx in (x, 1 - x) if d else (1 - x,):
                if not wait:
                    pl.when(here)(lambda zz=zz, xx=xx: self.arrived(p, zz, xx))
                self.ship(p, zz, xx, 3, here, wait)

    def finish(self, p):
        s, z, x, c = self.where
        for zz in range(NZ):
            for xx in range(2):
                block = self.view(p, zz, xx, 1 - c)
                i = zz * 2 + xx
                remote(block, block, self.core_send.at[p, i], self.core_recv.at[p, i], device(s, z, x, 1 - c)).wait_recv()

    def drain(self):
        for step in GATHER_STEPS[self.section]:
            if step[0] not in ("finish", "stage", "hand"):
                getattr(self, step[0])(*step[1:], wait=True)


def add_into(dst, terms):
    total = dst[...].astype(F32)
    for ref, cond in terms:
        value = ref[...].astype(F32)
        total = total + (value if cond is None else jnp.where(cond, value, 0.0))
    return total


def farthest_first(z, k):
    orders = ((3, 2, 1, 0), (3, 0, 2, 1), (0, 3, 1, 2), (0, 1, 2, 3))
    return jnp.where(
        z == 0, orders[0][k], jnp.where(z == 1, orders[1][k], jnp.where(z == 2, orders[2][k], orders[3][k]))
    )


class Scatter:
    def __init__(self, where, section, view, bufs, sems, store):
        self.where, self.section, self.view, self.store = where, section, view, store
        self.got_core, self.got_x, self.got_z, self.got_zz, self.got_home = bufs
        self.core_s, self.core_r, self.x_s, self.x_r, self.z_s, self.z_r, self.lend_s, self.lend_r, self.home_s, self.home_r = sems
        self.turned = TURN_OUT[section]
        left_out = (self.turned, LENT_OUT, LENT_SUM) if section == 0 else (self.turned,)
        self.straight = [p for p in range(PIECES + 1) if p not in left_out]

    def core_copy(self, p, i):
        s, z, x, c = self.where
        return remote(
            self.view(p, i // 2, i % 2, 1 - c),
            self.got_core.at[p, i],
            self.core_s.at[p, i],
            self.core_r.at[p, i],
            device(s, z, x, 1 - c),
        )

    def core_send(self, p):
        for i in range(2 * NZ):
            self.core_copy(p, i).start()

    def core_add(self, p):
        c = self.where[3]

        @pl.loop(0, 2 * NZ)
        def _(i):
            self.core_copy(p, i).wait_recv()
            dst = self.view(p, i // 2, i % 2, c)
            dst[...] = add_into(dst, [(self.got_core.at[p, i], None)]).astype(BF16)

    def x_slot(self, p, zz):
        return self.got_x.at[PIECES * NZ if p == self.turned else self.straight.index(p) * NZ + zz]

    def x_copy(self, p, zz):
        s, z, x, c = self.where
        return remote(
            self.view(p, zz, 1 - x, c),
            self.x_slot(p, zz),
            self.x_s.at[p, zz],
            self.x_r.at[p, zz],
            device(s, z, 1 - x, c),
        )

    def lent_copy(self, zz, xx):
        s, z, x, c = self.where
        i = zz * 2 + xx
        dst = self.view(LENT_SUM, zz, xx, c)
        src = self.view(LENT_OUT, zz, xx, c) if self.section == 0 else dst
        return remote(src, dst, self.lend_s.at[i], self.lend_r.at[i], device(1 - s, z, x, c))

    def lend(self, side, wait=False):
        s, z, x, c = self.where
        xx = 1 - x if side == 0 else x

        for i in range(NZ):
            cp = self.lent_copy(farthest_first(z, i), xx)
            cp.wait_send() if wait else cp.start()

    def home_copy(self):
        s, z, x, c = self.where
        return remote(self.view(LENT_SUM, z, x, c), self.got_home, self.home_s.at[0], self.home_r.at[0], device(1 - s, z, x, c))

    def home(self):
        self.home_copy().wait_recv()
        self.store(LENT_OUT, self.got_home[...].astype(F32))

    def x_send(self, p, first=0, last=NZ):
        s, z, x, c = self.where
        for i in range(first, last):
            zz = farthest_first(z, i)
            if p == LENT_SUM:
                self.lent_copy(zz, 1 - x).wait_recv()
            self.x_copy(p, zz).start()

    def x_wait(self, p, zz):
        if p == LENT_SUM:
            self.lent_copy(zz, self.where[2]).wait_recv()
        self.x_copy(p, zz).wait_recv()
        return self.x_slot(p, zz), None

    def slot(self, p, k, xx):
        return self.got_zz.at[xx, k] if p == self.turned else self.got_z.at[self.straight.index(p), k]

    def z_copy(self, p, zz, xx, sign, k):
        s, z, x, c = self.where
        return remote(
            self.view(p, zz, xx, c),
            self.slot(p, k, xx),
            self.z_s.at[p, xx, zz],
            self.z_r.at[p, xx, k],
            device(s, clipped(z + sign), x, c),
        )

    def z_out(self, p, zz, xx, sign):
        k = jnp.where((sign < 0) & (self.where[1] + sign == zz), NZ, zz)
        return self.z_copy(p, zz, xx, sign, k)

    def cols(self, p):
        x = self.where[2]
        return (x, 1 - x) if p == self.turned else (x,)

    def z_wait(self, p, zz, xx, k, cond):
        pl.when(cond)(lambda: self.z_copy(p, zz, xx, 1, k).wait_recv())
        return self.slot(p, k, xx), cond

    def z_step(self, p, k):
        s, z, x, c = self.where
        zz = farthest_first(z, k)
        sign = jnp.where(zz > z, 1, -1)
        before = inside(z - sign)
        terms = [] if p == self.turned else [self.x_wait(p, zz)]
        for xx in self.cols(p):
            dst = self.view(p, zz, xx, c)
            dst[...] = add_into(dst, terms + [self.z_wait(p, zz, xx, zz, before)]).astype(BF16)
            self.z_out(p, zz, xx, sign).start()

    def z_last(self, p, xx):
        z = self.where[1]
        return [self.z_wait(p, z, xx, z, z > 0), self.z_wait(p, z, xx, NZ, z < NZ - 1)]

    def turn(self, p):
        s, z, x, c = self.where
        dst = self.view(p, z, 1 - x, c)
        dst[...] = add_into(dst, self.z_last(p, 1 - x)).astype(BF16)
        self.x_copy(p, z).start()

    def close(self, p):
        s, z, x, c = self.where
        dst = self.view(p, z, x, c)
        total = add_into(dst, [self.x_wait(p, z)] + self.z_last(p, x))
        if p == LENT_SUM:
            dst[...] = total.astype(BF16)
            self.home_copy().start()
        else:
            self.store(p, total)

    def drain(self):
        for p in range(PIECES):
            for i in range(2 * NZ):
                self.core_copy(p, i).wait_send()
        for p in self.straight + [self.turned]:
            self.drain_links(p)
        if self.section == 0:
            self.lend(0, True)
            self.lend(1, True)
        else:
            self.home_copy().wait_send()

    def drain_links(self, p):
        z = self.where[1]
        for i in range(NZ - 1):
            zz = farthest_first(z, i)
            if p != self.turned:
                self.x_copy(p, zz).wait_send()
            for xx in self.cols(p):
                self.z_out(p, zz, xx, jnp.where(zz > z, 1, -1)).wait_send()
        self.x_copy(p, z).wait_send()


def head_windows():
    for k in range(8):
        start = HD * k // 128 * 128
        offset = HD * k - start
        span = 128 if offset + HD <= 128 else 256
        yield k, start, offset, span


def layers_kernel(
    n,
    tokens,
    cotangent,
    lengths,
    norm_gains,
    query_gain,
    wq,
    wo,
    wu,
    wd,
    out_half,
    token_half,
    d_q,
    d_o,
    d_u,
    d_d,
    small_out,
    held,
    lent,
    gain_all,
    gain_rows,
    query_block,
    hb,
    a1,
    qf,
    qb,
    kb,
    vb,
    prob,
    ob,
    mid,
    a2,
    up,
    hid,
    grad,
    dup,
    dmid,
    low,
    dob,
    give,
    sums,
    swap,
    got_core,
    got_x,
    got_z,
    got_zz,
    got_home,
    *sems,
):
    where = s, z, x, c = place()
    rows, width = hb.shape
    slots = cotangent.shape[1]
    half = width // 2
    group = 8 * HD
    factor = LOG_BASE / math.sqrt(HD)
    g_sems, r_sems = sems[:4], sems[4:14]
    swap_s, swap_r, hand_s, hand_r, back_s, back_r, end_s, end_r, load_sem, out_sem = sems[14:]
    across_y = device(1 - s, z, x, c)

    def view(p, zz, xx, cc):
        if p == GAINS:
            return gain_all.at[zz * 4 + xx * 2 + cc]
        if p == LENT:
            return lent.at[zz * 2 + xx]
        return held.at[p, pl.ds(pl.multiple_of((zz * 4 + xx * 2 + cc) * n, 16), n)]

    def sum_view(p, zz, xx, cc):
        return view(LENT if p == LENT_SUM else p, zz, xx, cc)

    def staged(p):
        return (qf if p < 3 else mid).at[pl.ds(p % 3 * n, n)]

    def in_hbm(p, first, others):
        return first.at[:, pl.ds(p * width, width)] if p < 3 else others[p - 3]

    def store_copy(p):
        return pltpu.make_async_copy(staged(p), in_hbm(p, d_q, (d_o, d_u, d_d)), out_sem.at[p])

    def store(p, value):
        staged(p)[...] = value
        store_copy(p).start()

    gathers = [Gather(where, k, view, g_sems) for k in range(2)]
    scatters = [
        Scatter(where, k, sum_view, (got_core, got_x, got_z, got_zz, got_home), r_sems, store) for k in range(2)
    ]


    def row_loop(fn):
        @pl.loop(0, rows // 32)
        def _(k):
            fn(pl.ds(pl.multiple_of(k * 32, 32), 32))

    def tiles(emit, value):
        for k in range(width // TILE):
            emit(slice(k * TILE, (k + 1) * TILE), value[:, k * TILE : (k + 1) * TILE])

    def project(p, a, emit):
        tiles(emit, jnp.dot(a[...], held[p], preferred_element_type=F32))

    def project_back(pieces, emit):
        total = None
        for p, a in pieces:
            term = contract_cols(a[...], held[p])
            total = term if total is None else total + term
        tiles(emit, total)

    def weight_grad(p, a, g):
        held[p] = contract_rows(a[...], g[...]).astype(BF16)

    def recip_of(value):
        return lax.rsqrt(jnp.mean(value * value, -1, keepdims=True) + NORM_EPS)

    def norm(src, row, dst):
        def part(r):
            value = src[r].astype(F32)
            dst[r] = (value * recip_of(value) * gain_rows[row : row + 1]).astype(BF16)

        row_loop(part)

    def put(ref):
        def emit(lanes, value):
            ref[:, lanes] = value.astype(ref.dtype)

        return emit

    def emit_query(lanes, value):
        qf[:, lanes] = value
        qb[:, lanes] = (value * gain_rows[2:3, lanes]).astype(BF16)

    def emit_up(lanes, value):
        up[:, lanes] = value
        hid[:, lanes] = (value / (1.0 + jnp.exp(-value))).astype(BF16)

    def emit_mid(lanes, value):
        mid[:, lanes] = hb[:, lanes].astype(F32) + value

    def emit_out(lanes, value):
        give[:, lanes] = (mid[:, lanes] + value).astype(BF16)

    def lane_mask(offset, span):
        lane = lax.broadcasted_iota(jnp.int32, (1, span), 1)
        return ((lane >= offset) & (lane < offset + HD)).astype(F32).astype(BF16)

    def attention(body, first, last):
        @pl.loop(2 * first, 2 * last)
        def _(it):
            seq, g = it // 2, it % 2
            r = pl.ds(pl.multiple_of(seq * slots, slots), slots)

            def window(ref, start, span):
                return ref[r, pl.ds(pl.multiple_of(g * group + start, 128), span)]

            body(it, seq, r, g, window)

    def spread(total, start, span, value):
        for j in range(span // 128):
            k = start // 128 + j
            term = value[:, j * 128 : (j + 1) * 128]
            total[k] = term if total[k] is None else total[k] + term

    def attend(it, seq, r, g, window):
        allowed = causal_allowed(slots, lengths[seq])
        total = [None] * (group // 128)
        for k, start, offset, span in head_windows():
            only = lane_mask(offset, span)
            scores = contract_cols(window(qb, start, span) * only, window(kb, start, span))
            scores = jnp.where(allowed, scores, NEG_FILL)
            expd = jnp.exp(scores - jnp.max(scores, -1, keepdims=True))
            probs = expd / jnp.sum(expd, -1, keepdims=True)
            prob[it, k] = probs
            value = jnp.dot(probs.astype(BF16), window(vb, start, span) * only, preferred_element_type=F32)
            spread(total, start, span, value)
        for k, value in enumerate(total):
            ob[r, pl.ds(pl.multiple_of(g * group + k * 128, 128), 128)] = value.astype(BF16)

    def attend_back(it, seq, r, g, window):
        count = group // 128
        t_q, t_k, t_v = [None] * count, [None] * count, [None] * count
        for k, start, offset, span in head_windows():
            only = lane_mask(offset, span)
            d_o_part = window(dob, start, span) * only
            probs = prob[it, k]
            d_probs = contract_cols(d_o_part, window(vb, start, span))
            spread(t_v, start, span, contract_rows(probs.astype(BF16), d_o_part))
            d_scores = probs * (d_probs - jnp.sum(probs * d_probs, -1, keepdims=True))
            d_scores = d_scores.astype(BF16)
            spread(t_q, start, span, jnp.dot(d_scores, window(kb, start, span) * only, preferred_element_type=F32))
            spread(t_k, start, span, contract_rows(d_scores, window(qb, start, span) * only))
        for k in range(count):
            lanes = pl.ds(pl.multiple_of(g * group + k * 128, 128), 128)
            products = t_q[k] * qf[r, lanes]
            sums[2, :, lanes] += jnp.sum(products.reshape(slots // 8, 8, 128), 0)
            qb[r, lanes] = (t_q[k] * gain_rows[2:3, lanes]).astype(BF16)
            kb[r, lanes] = t_k[k].astype(BF16)
            vb[r, lanes] = t_v[k].astype(BF16)

    def emit_dup(lanes, value):
        u = up[:, lanes]
        sig = 1.0 / (1.0 + jnp.exp(-u))
        dup[:, lanes] = (value * sig * (1.0 + u * (1.0 - sig))).astype(BF16)

    def norm_grad(row, src, base, emit):
        def part(r):
            value, d_normed = src[r].astype(F32), up[r]
            recip = recip_of(value)
            sums[row] += jnp.sum((d_normed * value * recip).reshape(4, 8, width), 0)
            emit(r, base[r].astype(F32) + norm_back(value, recip, d_normed * gain_rows[row : row + 1]))

        row_loop(part)

    def emit_dmid(r, value):
        dmid[r] = value
        low[r] = value.astype(BF16)

    def emit_give(r, value):
        give[r] = value.astype(BF16)

    def window_of(k, size):
        start = min(size * k // 128 * 128, width - 256)
        return start, size * k - start

    def rolled(block, shift):
        return pltpu.roll(block, shift, 1) if shift else block

    def spread_gains():
        gain_rows[...] = jnp.zeros_like(gain_rows)
        none = jnp.zeros((8, 128), F32)
        for f in range(4 * NZ):
            start, shift = window_of(f, n)
            gain_rows[:, start : start + 256] += rolled(jnp.concatenate([gain_all[f], none], -1), shift)
        value = query_block[...]
        scale = (jnp.maximum(value, 0.0) + jnp.log1p(jnp.exp(-jnp.abs(value)))) * factor
        lane = lax.broadcasted_iota(jnp.int32, (8, 128), 1)
        row = lax.broadcasted_iota(jnp.int32, (8, 128), 0)
        scale = jnp.where((lane < HD) & (row == 2), scale, 0.0)
        for k in range(H):
            start, shift = window_of(k, HD)
            gain_rows[:, start : start + 256] += rolled(jnp.concatenate([scale, none], -1), shift)

    def finish_small(value):
        me = z * 4 + x * 2 + c
        own = jnp.zeros((8, 128), F32)
        for f in range(4 * NZ):
            start, shift = window_of(f, n)
            part = rolled(value[:, start : start + 256], (256 - shift) % 256)[:, :128]
            own = own + jnp.where(me == f, part, 0.0)
        heads = jnp.zeros((8, 128), F32)
        for k in range(H):
            start, shift = window_of(k, HD)
            heads = heads + rolled(value[:, start : start + 256], (256 - shift) % 256)[:, :128]
        gate = factor / (1.0 + jnp.exp(-query_block[...]))
        row = lax.broadcasted_iota(jnp.int32, (8, 128), 0)
        small_out[...] = jnp.where(row == 2, heads * gate, own)

    def forward_stage(p):
        if p == 0:
            spread_gains()
            norm(hb, 0, a1)
            project(0, a1, emit_query)
        elif p == 1:
            project(1, a1, put(kb))
        elif p == 2:
            project(2, a1, put(vb))
            attention(attend, 0, rows // slots)
        elif p == 3:
            project(3, ob, emit_mid)
            norm(mid, 1, a2)
        elif p == 4:
            project(4, a2, emit_up)
        else:
            project(5, hid, emit_out)


    def hand(k):
        r = pl.ds(k * slots, slots)
        return remote(give.at[r], hb.at[r], hand_s.at[k], hand_r.at[k], across_y)

    def back(k):
        r = pl.ds(k * slots, slots)
        return remote(give.at[r], grad.at[r], back_s.at[k], back_r.at[k], across_y)

    def end(which):
        dst, col = ((out_half, 0), (token_half, half))[which]
        return remote(give.at[:, col : col + half], dst, end_s.at[which], end_r.at[which], across_y)


    def load(act):
        for k in range(rows // slots):
            r = pl.ds(k * slots, slots)
            here = pltpu.make_async_copy(tokens.at[k], hb.at[r], load_sem.at[k])
            there = pltpu.make_async_copy(cotangent.at[k], grad.at[r], load_sem.at[k])
            pl.when(s == 0)(getattr(here, act))
            pl.when(s == 1)(getattr(there, act))
        for p in range(PIECES):
            cp = pltpu.make_async_copy(in_hbm(p, wq, (wo, wu, wd)), staged(p), load_sem.at[rows // slots + p])
            getattr(cp, act)()

    load("start")
    me = z * 4 + x * 2 + c
    gain_all[me] = jnp.zeros((8, 128), F32)
    gain_all[me, 0:2, 0:n] = norm_gains[...].astype(BF16).astype(F32)
    query_block[...] = jnp.zeros_like(query_block)
    query_block[:, 0:HD] = jnp.broadcast_to(query_gain[...], (8, HD))
    sums[...] = jnp.zeros_like(sums)
    neighbour_barrier(s, z, x, c)
    load("wait")
    mine = pl.ds(pl.multiple_of((z * 4 + x * 2 + c) * n, 16), n)
    for p in range(PIECES):
        held[p, mine] = staged(p)[...].astype(BF16)

    def forward(section):
        for step in GATHER_STEPS[section]:
            if step[0] == "stage":
                forward_stage(step[1])
            elif step[0] == "hand":
                for k in range(rows // slots):
                    hand(k).wait_recv()
            else:
                getattr(gathers[section], step[0])(*step[1:])

    def hand_start():
        for k in range(rows // slots):
            hand(k).start()

    @pl.when(s == 0)
    def _():
        forward(0)
        hand_start()
        gathers[0].drain()
        for k in range(rows // slots):
            hand(k).wait_send()
            back(k).wait_recv()

    @pl.when(s == 1)
    def _():
        forward(1)
        gathers[1].drain()
        end(0).start()
        out_half[...] = give[:, half:]
        for k in range(rows // slots):
            row = lax.broadcasted_iota(jnp.int32, (slots, 1), 0)
            live = (row < lengths[k]).astype(F32)
            part = pl.ds(k * slots, slots)
            grad[part] = (grad[part].astype(F32) * live).astype(BF16)

    grads = ((a1, qb), (a1, kb), (a1, vb), (ob, low), (a2, dup), (hid, grad))

    def exchange(k):
        partner = (
            device(s, z, x, 1 - c),
            device(s, z, 1 - x, c),
            device(s, z + 1 - 2 * (z % 2), x, c),
            device(s, (z + 2) % NZ, x, c),
        )[k]
        return remote(swap.at[k, 0], swap.at[k, 1], swap_s.at[k], swap_r.at[k], partner)

    def small(k):
        if k == 0:
            totals = [jnp.sum(sums[i], 0, keepdims=True) for i in range(3)]
            swap[0, 0] = jnp.concatenate(totals + [jnp.zeros((5, width), F32)], 0)
            exchange(0).start()
            return
        exchange(k - 1).wait_recv()
        value = swap[k - 1, 0] + swap[k - 1, 1]
        if k < 4:
            swap[k, 0] = value
            exchange(k).start()
        else:
            finish_small(value)

    def finish_input(section):
        if section == 1:
            end(0).wait_send()
        norm_grad(0, hb, dmid, emit_give)
        if section == 1:
            for k in range(rows // slots):
                back(k).start()
        else:
            end(1).start()
            token_half[...] = give[:, :half]

    compute = dict(
        hidden=lambda section: project_back([(5, grad)], emit_dup),
        normed_two=lambda section: project_back([(4, dup)], put(up)),
        middle=lambda section: norm_grad(1, mid, grad, emit_dmid),
        attended=lambda section: project_back([(3, low)], put(dob)),
        heads=lambda section, k: attention(attend_back, k, k + 1),
        normed=lambda section: project_back([(0, qb), (1, kb), (2, vb)], put(up)),
        input=finish_input,
        weight=lambda section, p: weight_grad(p, *grads[p]),
        small=lambda section, k: small(k),
    )

    def backward(section):
        for step in BACKWARD_STEPS[section]:
            if step[0] in compute:
                compute[step[0]](section, *step[1:])
            else:
                getattr(scatters[section], step[0])(*step[1:])

    pl.when(s == 0)(lambda: backward(0))
    pl.when(s == 1)(lambda: backward(1))
    pl.when(s == 0)(scatters[0].drain)
    pl.when(s == 1)(scatters[1].drain)
    for p in range(PIECES):
        store_copy(p).wait()
    for k in range(4):
        exchange(k).wait_send()

    @pl.when(s == 0)
    def _():
        end(1).wait_send()
        end(0).wait_recv()

    @pl.when(s == 1)
    def _():
        for k in range(rows // slots):
            back(k).wait_send()
        end(1).wait_recv()


def finish_kernel(small, *refs):
    froms, tos, (d_gains, d_query), held, (in_sem, out_sem) = refs[:6], refs[6:12], refs[12:14], refs[14:20], refs[20:]
    ins = [pltpu.make_async_copy(a, h, in_sem.at[k]) for k, (a, h) in enumerate(zip(froms, held))]
    outs = [pltpu.make_async_copy(h, b, out_sem.at[k]) for k, (h, b) in enumerate(zip(held, tos))]
    for cp in ins:
        cp.start()
    d_gains[...] = small[0:2, : d_gains.shape[1]]
    d_query[...] = small[2:3, :HD]
    for came, goes in zip(ins, outs):
        came.wait()
        goes.start()
    for cp in outs:
        cp.wait()


def near_shards(
    tokens, cotangent, lengths, qkv_weight, out_weight, up_weight, down_weight, norm_gains, query_gain
):
    n, width = out_weight.shape
    count, slots, _ = tokens.shape
    rows = count * slots
    dma = pltpu.SemaphoreType.DMA
    whole = pl.BlockSpec(memory_space=pltpu.VMEM)
    far = pl.BlockSpec(memory_space=pl.ANY)
    block = (n, width)
    low_rows = pltpu.VMEM((rows, width), BF16)
    wide_rows = pltpu.VMEM((rows, width), F32)
    scratch = dict(
        held=pltpu.VMEM((PIECES, 4 * NZ * n, width), BF16),
        lent=pltpu.VMEM((2 * NZ,) + block, BF16),
        gain_all=pltpu.VMEM((4 * NZ, 8, 128), F32),
        gain_rows=pltpu.VMEM((8, width), F32),
        query_block=pltpu.VMEM((8, 128), F32),
        hb=low_rows,
        a1=low_rows,
        qf=wide_rows,
        qb=low_rows,
        kb=low_rows,
        vb=low_rows,
        prob=pltpu.VMEM((2 * count, 8, slots, slots), F32),
        ob=low_rows,
        mid=wide_rows,
        a2=low_rows,
        up=wide_rows,
        hid=low_rows,
        grad=low_rows,
        dup=low_rows,
        dmid=wide_rows,
        low=low_rows,
        dob=low_rows,
        give=low_rows,
        sums=pltpu.VMEM((3, 8, width), F32),
        swap=pltpu.VMEM((4, 2, 8, width), F32),
        got_core=pltpu.VMEM((PIECES, 2 * NZ) + block, BF16),
        got_x=pltpu.VMEM((PIECES * NZ + 1,) + block, BF16),
        got_z=pltpu.VMEM((PIECES, NZ + 1) + block, BF16),
        got_zz=pltpu.VMEM((2, NZ + 1) + block, BF16),
        got_home=pltpu.VMEM(block, BF16),
    )
    pieces = PIECES + 2
    semaphores = [
        dma((pieces, 2 * NZ, 4)),
        dma((pieces, 2 * NZ)),
        dma((pieces, 2 * NZ)),
        dma((pieces, 2 * NZ)),
        dma((PIECES, 2 * NZ)),
        dma((PIECES, 2 * NZ)),
        dma((PIECES + 1, NZ)),
        dma((PIECES + 1, NZ)),
        dma((PIECES + 1, 2, NZ)),
        dma((PIECES + 1, 2, NZ + 1)),
        dma((2 * NZ,)),
        dma((2 * NZ,)),
        dma((1,)),
        dma((1,)),
        dma((4,)),
        dma((4,)),
        dma((count,)),
        dma((count,)),
        dma((count,)),
        dma((count,)),
        dma((2,)),
        dma((2,)),
        dma((count + PIECES,)),
        dma((PIECES,)),
    ]
    half = jax.ShapeDtypeStruct((rows, width // 2), BF16)
    square = jax.ShapeDtypeStruct(block, F32)
    shapes = (half, half, jax.ShapeDtypeStruct((n, 3 * width), F32), square, square, square)
    *results, small = pl.pallas_call(
        lambda *refs: layers_kernel(n, *refs),
        out_shape=shapes + (jax.ShapeDtypeStruct((8, 128), F32),),
        in_specs=[far, far, pl.BlockSpec(memory_space=pltpu.SMEM), whole, whole] + [far] * 4,
        out_specs=(whole, whole) + (far,) * 4 + (whole,),
        scratch_shapes=list(scratch.values()) + semaphores,
        compiler_params=pltpu.CompilerParams(
            collective_id=1, has_side_effects=True, vmem_limit_bytes=63 << 20
        ),
        name="two_layers",
    )(tokens, cotangent, lengths, norm_gains.T, query_gain, qkv_weight, out_weight, up_weight, down_weight)
    out, d_tokens, d_q, d_o, d_u, d_d, d_gains, d_query = pl.pallas_call(
        finish_kernel,
        out_shape=shapes + (jax.ShapeDtypeStruct((2, n), F32), jax.ShapeDtypeStruct((1, HD), F32)),
        in_specs=[whole] + [far] * 6,
        out_specs=(far,) * 6 + (whole,) * 2,
        scratch_shapes=[pltpu.VMEM(item.shape, item.dtype) for item in shapes] + [dma((6,)), dma((6,))],
        compiler_params=pltpu.CompilerParams(vmem_limit_bytes=63 << 20),
        name="results",
    )(small, *results)
    shape = (count, slots, width // 2)
    return (
        out.reshape(shape),
        d_tokens.reshape(shape),
        d_q[None],
        d_o[None],
        d_u[None],
        d_d[None],
        d_gains.T[None],
        d_query,
    )


def swapped(value, axis, bit):
    return lax.ppermute(value, axis, [(i, i ^ 1 << bit) for i in range(lax.axis_size(axis))])


def causal_allowed(row_count, length):
    row_ids = lax.broadcasted_iota(jnp.int32, (row_count, row_count), 0)
    col_ids = lax.broadcasted_iota(jnp.int32, (row_count, row_count), 1)
    return (col_ids <= row_ids) & (col_ids < length)


def contract_rows(left, right):
    return lax.dot_general(
        left, right, (((0,), (0,)), ((), ())), preferred_element_type=jnp.float32
    )


def contract_cols(left, right):
    return lax.dot_general(
        left, right, (((1,), (1,)), ((), ())), preferred_element_type=jnp.float32
    )


def norm_back(source, recip, grad_flat):
    return recip * grad_flat - source * recip**3 * jnp.mean(grad_flat * source, -1, keepdims=True)


def layer_forward(layer_input, length, weights, query_scale):
    qkv_w, out_w, up_w, down_w, gain_pair = weights
    row_count, width = layer_input.shape
    gain_one = gain_pair[:, 0].astype(jnp.float32)
    gain_two = gain_pair[:, 1].astype(jnp.float32)
    recip_one = lax.rsqrt(jnp.mean(layer_input * layer_input, -1, keepdims=True) + NORM_EPS)
    normed = (layer_input * recip_one * gain_one).astype(jnp.bfloat16)
    proj = jnp.dot(normed, qkv_w, preferred_element_type=jnp.float32)
    query = proj[:, :width].reshape(row_count, H, HD)
    query_b = (query * query_scale).astype(jnp.bfloat16)
    keys_b = proj[:, width : 2 * width].astype(jnp.bfloat16).reshape(row_count, H, HD)
    values_b = proj[:, 2 * width :].astype(jnp.bfloat16).reshape(row_count, H, HD)
    scores = jnp.einsum("qhd,khd->hqk", query_b, keys_b, preferred_element_type=jnp.float32)
    scores = jnp.where(causal_allowed(row_count, length)[None], scores, NEG_FILL)
    row_peak = jnp.max(scores, -1, keepdims=True)
    expd = jnp.exp(scores - row_peak)
    row_total = jnp.sum(expd, -1, keepdims=True)
    probs = expd / row_total
    logsum = (row_peak + jnp.log(row_total))[..., 0]
    attended = (
        jnp.einsum(
            "hqk,khd->qhd", probs.astype(jnp.bfloat16), values_b, preferred_element_type=jnp.float32
        )
        .reshape(row_count, width)
        .astype(jnp.bfloat16)
    )
    middle = layer_input + jnp.dot(attended, out_w, preferred_element_type=jnp.float32)
    recip_two = lax.rsqrt(jnp.mean(middle * middle, -1, keepdims=True) + NORM_EPS)
    normed_two = (middle * recip_two * gain_two).astype(jnp.bfloat16)
    upper = jnp.dot(normed_two, up_w, preferred_element_type=jnp.float32)
    hidden = jax.nn.silu(upper).astype(jnp.bfloat16)
    layer_output = middle + jnp.dot(hidden, down_w, preferred_element_type=jnp.float32)
    saved = (
        layer_input,
        normed,
        query,
        query_b,
        keys_b,
        values_b,
        logsum,
        attended,
        middle,
        normed_two,
        upper,
        hidden,
        recip_one,
        recip_two,
    )
    return (layer_output, saved)


def layer_backward(saved, length, weights, query_scale, grad_output):
    qkv_w, out_w, up_w, down_w, gain_pair = weights
    (
        layer_input,
        normed,
        query,
        query_b,
        keys_b,
        values_b,
        logsum,
        attended,
        middle,
        normed_two,
        upper,
        hidden,
        recip_one,
        recip_two,
    ) = saved
    row_count, width = layer_input.shape
    gain_one = gain_pair[:, 0].astype(jnp.float32)
    gain_two = gain_pair[:, 1].astype(jnp.float32)
    grad_low = grad_output.astype(jnp.bfloat16)
    d_down = contract_rows(hidden, grad_low)
    d_hidden = contract_cols(grad_low, down_w)
    sigmoid_up = jax.nn.sigmoid(upper)
    d_upper = (d_hidden * sigmoid_up * (1.0 + upper * (1.0 - sigmoid_up))).astype(jnp.bfloat16)
    d_up = contract_rows(normed_two, d_upper)
    d_normed_two = contract_cols(d_upper, up_w)
    d_gain_two = jnp.sum(d_normed_two * middle * recip_two, 0)
    d_middle = grad_output + norm_back(middle, recip_two, d_normed_two * gain_two)
    middle_low = d_middle.astype(jnp.bfloat16)
    d_out = contract_rows(attended, middle_low)
    d_attended = contract_cols(middle_low, out_w).astype(jnp.bfloat16).reshape(row_count, H, HD)
    scores = jnp.einsum("qhd,khd->hqk", query_b, keys_b, preferred_element_type=jnp.float32)
    scores = jnp.where(causal_allowed(row_count, length)[None], scores, NEG_FILL)
    probs = jnp.exp(scores - logsum[..., None])
    d_probs = jnp.einsum("qhd,khd->hqk", d_attended, values_b, preferred_element_type=jnp.float32)
    d_values = jnp.einsum(
        "hqk,qhd->khd", probs.astype(jnp.bfloat16), d_attended, preferred_element_type=jnp.float32
    ).astype(jnp.bfloat16)
    d_scores = (probs * (d_probs - jnp.sum(probs * d_probs, -1, keepdims=True))).astype(
        jnp.bfloat16
    )
    d_query_s = jnp.einsum("hqk,khd->qhd", d_scores, keys_b, preferred_element_type=jnp.float32)
    d_keys = jnp.einsum(
        "hqk,qhd->khd", d_scores, query_b, preferred_element_type=jnp.float32
    ).astype(jnp.bfloat16)
    d_scale = jnp.sum(d_query_s * query, (0, 1))
    d_query = (d_query_s * query_scale).astype(jnp.bfloat16)
    d_proj = jnp.concatenate(
        [
            d_query.reshape(row_count, width),
            d_keys.reshape(row_count, width),
            d_values.reshape(row_count, width),
        ],
        -1,
    )
    d_qkv = contract_rows(normed, d_proj)
    d_normed = contract_cols(d_proj, qkv_w)
    d_gain_one = jnp.sum(d_normed * layer_input * recip_one, 0)
    d_input = d_middle + norm_back(layer_input, recip_one, d_normed * gain_one)
    d_gains = jnp.stack([d_gain_one, d_gain_two], -1)
    return (d_input, (d_qkv, d_out, d_up, d_down, d_gains), d_scale)


def shards(
    tokens,
    cotangent,
    lengths,
    qkv_weight,
    out_weight,
    up_weight,
    down_weight,
    norm_gains,
    query_gain,
):
    if lax.axis_size("fsdp") == 4 * NZ:
        return near_shards(
            tokens,
            cotangent,
            lengths,
            qkv_weight[0],
            out_weight[0],
            up_weight[0],
            down_weight[0],
            norm_gains[0],
            query_gain,
        )
    section_index = lax.axis_index("section")
    micro_count, slot_rows, width = tokens.shape
    half_width = width // 2
    scale_factor = LOG_BASE / math.sqrt(HD)
    query_scale = jax.nn.softplus(query_gain[0]) * scale_factor

    def gather_weights():
        pieces = (
            lax.all_gather(qkv_weight.astype(jnp.bfloat16), "fsdp", axis=1, tiled=True),
            lax.all_gather(out_weight.astype(jnp.bfloat16), "fsdp", axis=1, tiled=True),
            lax.all_gather(up_weight.astype(jnp.bfloat16), "fsdp", axis=1, tiled=True),
            lax.all_gather(down_weight.astype(jnp.bfloat16), "fsdp", axis=1, tiled=True),
            lax.all_gather(norm_gains.astype(jnp.bfloat16), "fsdp", axis=1, tiled=True),
        )
        return tuple((piece[0] for piece in pieces))

    def handoff(value):
        return swapped(value, "section", 0)

    weights = gather_weights()
    received = jnp.zeros((slot_rows, width), jnp.bfloat16)
    kept = []
    result_parts = []
    for tick_index in range(micro_count + 1):
        first_input = tokens[min(tick_index, micro_count - 1)].astype(jnp.float32)
        layer_input = jnp.where(section_index == 0, first_input, received.astype(jnp.float32))
        micro_index = jnp.clip(tick_index - section_index, 0, micro_count - 1)
        length = lengths[micro_index]
        layer_output, saved = layer_forward(layer_input, length, weights, query_scale)
        sent = layer_output.astype(jnp.bfloat16)
        received = handoff(sent)
        kept.append(saved)
        if tick_index >= 1:
            finished = jnp.where(section_index == 1, sent, received)
            result_parts.append(
                lax.dynamic_slice_in_dim(finished, section_index * half_width, half_width, 1)
            )
    output = jnp.stack(result_parts)
    weights = gather_weights()
    row_ids = lax.iota(jnp.int32, slot_rows)
    grad_received = jnp.zeros((slot_rows, width), jnp.bfloat16)
    grad_parts = []
    grad_totals = None
    scale_total = jnp.zeros((HD,), jnp.float32)
    for tick_index in range(micro_count + 1):
        offset = tick_index - 1 + section_index
        micro_index = jnp.clip(offset, 0, micro_count - 1)
        length = lengths[micro_index]
        live_tick = ((offset >= 0) & (offset < micro_count)).astype(jnp.float32)
        live_rows = (row_ids < length).astype(jnp.float32)[:, None]
        top_grad = cotangent[min(tick_index, micro_count - 1)].astype(jnp.float32) * live_rows
        grad_output = jnp.where(section_index == 1, top_grad, grad_received.astype(jnp.float32))
        saved = jax.tree.map(
            lambda early, late: jnp.where(section_index == 0, early, late),
            kept[max(tick_index - 1, 0)],
            kept[min(tick_index + 1, micro_count)],
        )
        d_input, weight_grads, scale_grad = layer_backward(
            saved, length, weights, query_scale, grad_output
        )
        weight_grads = tuple((item * live_tick for item in weight_grads))
        scale_total = scale_total + scale_grad * live_tick
        sent = d_input.astype(jnp.bfloat16)
        grad_received = handoff(sent)
        if tick_index >= 1:
            finished = jnp.where(section_index == 0, sent, grad_received)
            grad_parts.append(
                lax.dynamic_slice_in_dim(finished, section_index * half_width, half_width, 1)
            )
        if grad_totals is None:
            grad_totals = weight_grads
        else:
            grad_totals = tuple((total + piece for total, piece in zip(grad_totals, weight_grads)))
    d_tokens = jnp.stack(grad_parts)
    scattered = (
        lax.psum_scatter(grad_totals[0], "fsdp", scatter_dimension=0, tiled=True),
        lax.psum_scatter(grad_totals[1], "fsdp", scatter_dimension=0, tiled=True),
        lax.psum_scatter(grad_totals[2], "fsdp", scatter_dimension=0, tiled=True),
        lax.psum_scatter(grad_totals[3], "fsdp", scatter_dimension=0, tiled=True),
        lax.psum_scatter(grad_totals[4], "fsdp", scatter_dimension=0, tiled=True),
    )
    owned = tuple((item[None] for item in scattered))
    scale_sum = lax.psum(scale_total, "fsdp")
    d_query_gain = (scale_sum * jax.nn.sigmoid(query_gain[0]) * scale_factor)[None]
    return (output, d_tokens, owned[0], owned[1], owned[2], owned[3], owned[4], d_query_gain)


def solution(mesh):
    in_specs = (
        P("fsdp", None, None),
        P("fsdp", None, None),
        P("fsdp"),
        P("section", "fsdp", None),
        P("section", "fsdp", None),
        P("section", "fsdp", None),
        P("section", "fsdp", None),
        P("section", "fsdp", None),
        P("section", None),
    )
    out_specs = (
        P("fsdp", None, "section"),
        P("fsdp", None, "section"),
        P("section", "fsdp", None),
        P("section", "fsdp", None),
        P("section", "fsdp", None),
        P("section", "fsdp", None),
        P("section", "fsdp", None),
        P("section", None),
    )
    return jax.shard_map(shards, mesh=mesh, in_specs=in_specs, out_specs=out_specs, check_vma=False)
```

```python
import math

import jax
import jax.numpy as jnp
from jax import lax
from jax.experimental import pallas as pl
from jax.experimental.pallas import tpu as pltpu
from jax.sharding import PartitionSpec as P

H = 16
HD = 80


NORM_EPS = 1e-06
NEG_FILL = -1e30
LOG_BASE = 1.442695041


MESH_ID = pl.DeviceIdType.MESH
BF16 = jnp.bfloat16
F32 = jnp.float32
NZ = 4
TILE = 256
PIECES = 6
GAINS = 6
LENT = 7
LENT_IN = 5
TURN_IN = (4, 5)
LENT_OUT = 5
LENT_SUM = 6
TURN_OUT = (4, 4)


def place():
    s, f = lax.axis_index("section"), lax.axis_index("fsdp")
    return s, f // 4, (f // 2) % 2, f % 2


def device(s, z, x, c):
    return (s, z * 4 + x * 2 + c)


def inside(z):
    return (z >= 0) & (z < NZ)


def clipped(z):
    return jnp.clip(z, 0, NZ - 1)


def neighbour_barrier(s, z, x, c):
    barrier = pltpu.get_barrier_semaphore()

    def tell(target):
        pl.semaphore_signal(barrier, inc=1, device_id=target, device_id_type=MESH_ID)

    tell(device(s, z, x, 1 - c))
    tell(device(s, z, 1 - x, c))
    tell(device(1 - s, z, x, c))
    tell(device(s, (z + 2) % NZ, x, c))
    pl.when(z > 0)(lambda: tell(device(s, z - 1, x, c)))
    pl.when(z < NZ - 1)(lambda: tell(device(s, z + 1, x, c)))
    pl.semaphore_wait(barrier, 4 + (z > 0).astype(jnp.int32) + (z < NZ - 1).astype(jnp.int32))


def remote(src, dst, send_sem, recv_sem, target):
    return pltpu.make_async_remote_copy(
        src, dst, send_sem, recv_sem, device_id=target, device_id_type=MESH_ID
    )


GATHER_STEPS = (
    (
        ("own", 0),
        ("own", 2),
        ("own", 6),
        ("own", 4),
        ("own", 5),
        ("relay", 2, 1, (-1,)),
        ("own", 1),
        ("relay", 0, 1, (-1,)),
        ("relay", 0, 1, (1,)),
        ("relay", 0, 2, (-1,)),
        ("relay", 6, 1, (1,)),
        ("relay", 6, 1, (-1,)),
        ("relay", 2, 1, (1,)),
        ("relay", 6, 2, (1,)),
        ("relay", 1, 1, (-1,)),
        ("relay", 0, 2, (1,)),
        ("relay", 0, 3, (-1,)),
        ("relay", 6, 2, (-1,)),
        ("relay", 6, 3, (-1,)),
        ("relay", 1, 1, (1,)),
        ("relay", 1, 2, (-1,)),
        ("turn", 4),
        ("relay", 1, 2, (1,)),
        ("relay", 1, 3, (-1,)),
        ("relay", 0, 3, (1,)),
        ("across", 0, 0),
        ("relay", 6, 3, (1,)),
        ("across", 6, 0),
        ("across", 6, 1),
        ("relay", 2, 2, (-1,)),
        ("relay", 2, 2, (1,)),
        ("relay", 2, 3, (-1,)),
        ("across", 6, 2),
        ("across", 0, 1),
        ("across", 6, 3),
        ("own", 3),
        ("relay", 2, 3, (1,)),
        ("relay", 4, 1, (1,)),
        ("relay", 3, 1, (-1,)),
        ("home", 5, 0),
        ("home", 5, 1),
        ("relay", 1, 3, (1,)),
        ("across", 1, 0),
        ("across", 2, 0),
        ("home", 5, 2),
        ("across", 1, 1),
        ("relay", 4, 1, (-1,)),
        ("relay", 4, 2, (1,)),
        ("across", 1, 2),
        ("across", 2, 1),
        ("finish", 6),
        ("home", 5, 3),
        ("across", 2, 2),
        ("across", 2, 3),
        ("across", 1, 3),
        ("relay", 4, 2, (-1,)),
        ("across", 0, 2),
        ("across", 0, 3),
        ("finish", 0),
        ("stage", 0),
        ("relay", 3, 1, (1,)),
        ("finish", 5),
        ("relay", 3, 2, (-1,)),
        ("finish", 1),
        ("stage", 1),
        ("finish", 2),
        ("relay", 4, 3, (-1,)),
        ("relay", 4, 3, (1,)),
        ("finish", 4),
        ("relay", 3, 2, (1,)),
        ("relay", 3, 3, (-1,)),
        ("relay", 3, 3, (1,)),
        ("across", 3, 0),
        ("stage", 2),
        ("across", 3, 1),
        ("across", 3, 2),
        ("across", 3, 3),
        ("finish", 3),
        ("stage", 3),
        ("stage", 4),
        ("stage", 5),
    ),
    (
        ("own", 5),
        ("own", 0),
        ("own", 7),
        ("relay", 0, 1, (-1,)),
        ("relay", 7, 1, (-1,)),
        ("own", 6),
        ("own", 2),
        ("relay", 7, 1, (1,)),
        ("relay", 6, 1, (-1,)),
        ("relay", 7, 2, (-1,)),
        ("relay", 6, 1, (1,)),
        ("relay", 7, 2, (1,)),
        ("relay", 6, 2, (-1,)),
        ("relay", 7, 3, (-1,)),
        ("relay", 0, 1, (1,)),
        ("relay", 0, 2, (1,)),
        ("turn", 5),
        ("relay", 5, 1, (-1,)),
        ("relay", 6, 2, (1,)),
        ("own", 4),
        ("relay", 7, 3, (1,)),
        ("across", 7, 0),
        ("own", 3),
        ("own", 1),
        ("across", 7, 1),
        ("across", 7, 2),
        ("across", 7, 3),
        ("relay", 2, 1, (-1,)),
        ("relay", 1, 1, (1,)),
        ("relay", 6, 3, (1,)),
        ("relay", 0, 2, (-1,)),
        ("relay", 0, 3, (1,)),
        ("relay", 1, 1, (-1,)),
        ("relay", 0, 3, (-1,)),
        ("relay", 2, 1, (1,)),
        ("relay", 2, 2, (1,)),
        ("relay", 4, 1, (1,)),
        ("relay", 6, 3, (-1,)),
        ("across", 6, 0),
        ("across", 0, 0),
        ("relay", 1, 2, (1,)),
        ("across", 6, 1),
        ("relay", 1, 2, (-1,)),
        ("relay", 1, 3, (1,)),
        ("relay", 2, 2, (-1,)),
        ("relay", 2, 3, (1,)),
        ("relay", 1, 3, (-1,)),
        ("across", 6, 2),
        ("relay", 3, 1, (1,)),
        ("across", 0, 1),
        ("across", 0, 2),
        ("across", 0, 3),
        ("relay", 3, 1, (-1,)),
        ("relay", 5, 1, (1,)),
        ("relay", 3, 2, (-1,)),
        ("across", 1, 0),
        ("relay", 2, 3, (-1,)),
        ("relay", 3, 2, (1,)),
        ("relay", 3, 3, (-1,)),
        ("across", 1, 1),
        ("across", 1, 2),
        ("across", 2, 0),
        ("across", 2, 1),
        ("across", 2, 2),
        ("across", 2, 3),
        ("across", 1, 3),
        ("relay", 5, 2, (-1,)),
        ("relay", 4, 1, (-1,)),
        ("relay", 5, 2, (1,)),
        ("finish", 2),
        ("relay", 4, 2, (-1,)),
        ("finish", 1),
        ("relay", 3, 3, (1,)),
        ("finish", 0),
        ("across", 3, 0),
        ("across", 3, 1),
        ("relay", 5, 3, (1,)),
        ("across", 6, 3),
        ("relay", 5, 3, (-1,)),
        ("relay", 4, 2, (1,)),
        ("finish", 5),
        ("finish", 6),
        ("across", 3, 2),
        ("across", 3, 3),
        ("finish", 3),
        ("relay", 4, 3, (1,)),
        ("relay", 4, 3, (-1,)),
        ("across", 4, 0),
        ("across", 4, 1),
        ("hand",),
        ("stage", 0),
        ("stage", 1),
        ("stage", 2),
        ("across", 4, 2),
        ("across", 4, 3),
        ("stage", 3),
        ("finish", 4),
        ("stage", 4),
        ("stage", 5),
    ),
)
BACKWARD_STEPS = (
    (
        ("hidden",),
        ("normed_two",),
        ("weight", 4),
        ("core_send", 4),
        ("middle",),
        ("attended",),
        ("weight", 3),
        ("core_send", 3),
        ("core_add", 4),
        ("z_step", 4, 0),
        ("core_add", 3),
        ("weight", 5),
        ("core_send", 5),
        ("x_send", 3),
        ("z_step", 4, 1),
        ("heads",),
        ("normed",),
        ("weight", 0),
        ("z_step", 3, 0),
        ("core_send", 0),
        ("core_add", 0),
        ("x_send", 0),
        ("z_step", 4, 2),
        ("weight", 2),
        ("weight", 1),
        ("core_send", 1),
        ("core_add", 5),
        ("lend", 0),
        ("lend", 1),
        ("core_add", 1),
        ("input",),
        ("z_step", 0, 0),
        ("small", 0),
        ("small", 1),
        ("x_send", 1),
        ("z_step", 0, 1),
        ("z_step", 0, 2),
        ("core_send", 2),
        ("z_step", 1, 0),
        ("z_step", 3, 1),
        ("small", 2),
        ("core_add", 2),
        ("x_send", 2),
        ("close", 0),
        ("z_step", 1, 1),
        ("z_step", 1, 2),
        ("z_step", 2, 0),
        ("close", 1),
        ("z_step", 3, 2),
        ("z_step", 2, 1),
        ("turn", 4),
        ("z_step", 2, 2),
        ("small", 3),
        ("small", 4),
        ("close", 3),
        ("close", 4),
        ("close", 2),
        ("home",),
    ),
    (
        ("hidden",),
        ("normed_two",),
        ("middle",),
        ("attended",),
        ("weight", 5),
        ("core_send", 5),
        ("core_add", 5),
        ("x_send", 5),
        ("heads",),
        ("normed",),
        ("input",),
        ("weight", 3),
        ("core_send", 3),
        ("z_step", 5, 0),
        ("weight", 4),
        ("core_send", 4),
        ("core_add", 3),
        ("x_send", 3),
        ("weight", 0),
        ("core_send", 0),
        ("core_add", 4),
        ("z_step", 4, 0),
        ("core_add", 0),
        ("x_send", 0),
        ("weight", 2),
        ("core_send", 2),
        ("z_step", 5, 1),
        ("core_add", 2),
        ("x_send", 2),
        ("weight", 1),
        ("z_step", 4, 1),
        ("core_send", 1),
        ("small", 0),
        ("core_add", 1),
        ("z_step", 3, 0),
        ("z_step", 3, 1),
        ("z_step", 4, 2),
        ("small", 1),
        ("z_step", 0, 0),
        ("z_step", 5, 2),
        ("z_step", 2, 0),
        ("z_step", 2, 1),
        ("z_step", 2, 2),
        ("x_send", 1),
        ("z_step", 0, 1),
        ("x_send", 6, 0, 1),
        ("small", 2),
        ("z_step", 0, 2),
        ("close", 2),
        ("z_step", 3, 2),
        ("close", 0),
        ("z_step", 1, 0),
        ("x_send", 6, 1, 2),
        ("x_send", 6, 2, 3),
        ("z_step", 6, 0),
        ("z_step", 6, 1),
        ("z_step", 6, 2),
        ("x_send", 6, 3, 4),
        ("small", 3),
        ("z_step", 1, 1),
        ("close", 6),
        ("z_step", 1, 2),
        ("turn", 4),
        ("small", 4),
        ("close", 3),
        ("close", 5),
        ("close", 1),
        ("close", 4),
    ),
)


class Gather:
    def __init__(self, where, section, view, sems):
        self.where, self.section, self.view = where, section, view
        self.send_sem, self.recv_sem, self.core_send, self.core_recv = sems

    def ship(self, p, zz, xx, way, cond, wait):
        s, z, x, c = self.where
        i = zz * 2 + xx
        block = self.view(p, zz, xx, c)
        if way < 3:
            target = (
                device(s, clipped(z + 1), x, c),
                device(s, clipped(z - 1), x, c),
                device(s, z, 1 - x, c),
            )[way]
            cp = remote(block, block, self.send_sem.at[p, i, way], self.recv_sem.at[p, i], target)
        elif way == 3:
            cp = remote(block, block, self.core_send.at[p, i], self.core_recv.at[p, i], device(s, z, x, 1 - c))
        else:
            q = LENT if self.section == 0 else LENT_IN
            there = self.view(q, zz, xx, c)
            cp = remote(block, there, self.send_sem.at[p, i, 3], self.recv_sem.at[q, i], device(1 - s, z, x, c))
        act = cp.wait_send if wait else cp.start
        if cond is None:
            act()
        else:
            pl.when(cond)(act)

    def arrived(self, p, zz, xx):
        s, z, x, c = self.where
        block = self.view(p, zz, xx, c)
        i = zz * 2 + xx
        remote(block, block, self.send_sem.at[p, i, 0], self.recv_sem.at[p, i], device(s, z, 1 - x, c)).wait_recv()

    def own(self, p, wait=False):
        s, z, x, c = self.where
        ways = ((0, z < NZ - 1), (1, z > 0), (2, None), (3, None))
        if p == LENT:
            ways = ways[:3]
            if not wait:
                self.arrived(p, z, x)
        elif self.section == 0 and p == LENT_IN:
            ways = ((4, None), (3, None))
        for way, cond in ways:
            self.ship(p, z, x, way, cond, wait)

    def turn(self, p, wait=False):
        s, z, x, c = self.where
        if not wait:
            self.arrived(p, z, 1 - x)
        self.ship(p, z, 1 - x, 0, z < NZ - 1, wait)
        self.ship(p, z, 1 - x, 1, z > 0, wait)
        self.ship(p, z, 1 - x, 3, None, wait)

    def relay(self, p, d, signs=(-1, 1), wait=False):
        s, z, x, c = self.where
        turned = p == TURN_IN[self.section]
        for sign in signs:
            way = 0 if sign < 0 else 1
            zz = clipped(z + sign * d)
            here = inside(z + sign * d)
            for xx in (x, 1 - x) if turned else (x,):
                if not wait:
                    pl.when(here)(lambda zz=zz, xx=xx: self.arrived(p, zz, xx))
                self.ship(p, zz, xx, way, here & inside(z - sign), wait)
                if not turned:
                    self.ship(p, zz, xx, 2, here, wait)
                self.ship(p, zz, xx, 4 if p == LENT else 3, here, wait)

    def across(self, p, d, wait=False):
        s, z, x, c = self.where
        for sign in (-1, 1) if d else (1,):
            zz = clipped(z + sign * d)
            here = inside(z + sign * d)
            if not wait:
                pl.when(here)(lambda zz=zz: self.arrived(p, zz, 1 - x))
            self.ship(p, zz, 1 - x, 4 if p == LENT else 3, here, wait)

    def home(self, p, d, wait=False):
        s, z, x, c = self.where
        for sign in (-1, 1) if d else (1,):
            zz = clipped(z + sign * d)
            here = inside(z + sign * d)
            for xx in (x, 1 - x) if d else (1 - x,):
                if not wait:
                    pl.when(here)(lambda zz=zz, xx=xx: self.arrived(p, zz, xx))
                self.ship(p, zz, xx, 3, here, wait)

    def finish(self, p):
        s, z, x, c = self.where
        for zz in range(NZ):
            for xx in range(2):
                block = self.view(p, zz, xx, 1 - c)
                i = zz * 2 + xx
                remote(block, block, self.core_send.at[p, i], self.core_recv.at[p, i], device(s, z, x, 1 - c)).wait_recv()

    def drain(self):
        for step in GATHER_STEPS[self.section]:
            if step[0] not in ("finish", "stage", "hand"):
                getattr(self, step[0])(*step[1:], wait=True)


def add_into(out, dst, terms):
    @pl.loop(0, dst.shape[0] // 16)
    def _(k):
        r = pl.ds(pl.multiple_of(k * 16, 16), 16)
        total = dst[r].astype(F32)
        for ref, cond in terms:
            value = ref[r].astype(F32)
            total = total + (value if cond is None else jnp.where(cond, value, 0.0))
        out[r] = total.astype(out.dtype)


def farthest_first(z, k):
    orders = ((3, 2, 1, 0), (3, 0, 2, 1), (0, 3, 1, 2), (0, 1, 2, 3))
    return jnp.where(
        z == 0, orders[0][k], jnp.where(z == 1, orders[1][k], jnp.where(z == 2, orders[2][k], orders[3][k]))
    )


class Scatter:
    def __init__(self, where, section, view, bufs, sems, store):
        self.where, self.section, self.view, self.store = where, section, view, store
        self.got_core, self.got_x, self.got_z, self.got_zz, self.got_home = bufs
        self.core_s, self.core_r, self.x_s, self.x_r, self.z_s, self.z_r, self.lend_s, self.lend_r, self.home_s, self.home_r = sems
        self.turned = TURN_OUT[section]
        left_out = (self.turned, LENT_OUT, LENT_SUM) if section == 0 else (self.turned,)
        self.straight = [p for p in range(PIECES + 1) if p not in left_out]

    def core_copy(self, p, i):
        s, z, x, c = self.where
        return remote(
            self.view(p, i // 2, i % 2, 1 - c),
            self.got_core.at[p, i],
            self.core_s.at[p, i],
            self.core_r.at[p, i],
            device(s, z, x, 1 - c),
        )

    def core_send(self, p):
        for i in range(2 * NZ):
            self.core_copy(p, i).start()

    def core_add(self, p):
        c = self.where[3]

        @pl.loop(0, 2 * NZ)
        def _(i):
            self.core_copy(p, i).wait_recv()
            dst = self.view(p, i // 2, i % 2, c)
            add_into(dst, dst, [(self.got_core.at[p, i], None)])

    def x_slot(self, p, zz):
        return self.got_x.at[PIECES * NZ if p == self.turned else self.straight.index(p) * NZ + zz]

    def x_copy(self, p, zz):
        s, z, x, c = self.where
        return remote(
            self.view(p, zz, 1 - x, c),
            self.x_slot(p, zz),
            self.x_s.at[p, zz],
            self.x_r.at[p, zz],
            device(s, z, 1 - x, c),
        )

    def lent_copy(self, zz, xx):
        s, z, x, c = self.where
        i = zz * 2 + xx
        dst = self.view(LENT_SUM, zz, xx, c)
        src = self.view(LENT_OUT, zz, xx, c) if self.section == 0 else dst
        return remote(src, dst, self.lend_s.at[i], self.lend_r.at[i], device(1 - s, z, x, c))

    def lend(self, side, wait=False):
        s, z, x, c = self.where
        xx = 1 - x if side == 0 else x

        for i in range(NZ):
            cp = self.lent_copy(farthest_first(z, i), xx)
            cp.wait_send() if wait else cp.start()

    def home_copy(self):
        s, z, x, c = self.where
        return remote(self.view(LENT_SUM, z, x, c), self.got_home, self.home_s.at[0], self.home_r.at[0], device(1 - s, z, x, c))

    def home(self):
        self.home_copy().wait_recv()
        self.store(LENT_OUT, self.got_home, [])

    def x_send(self, p, first=0, last=NZ):
        s, z, x, c = self.where
        for i in range(first, last):
            zz = farthest_first(z, i)
            if p == LENT_SUM:
                self.lent_copy(zz, 1 - x).wait_recv()
            self.x_copy(p, zz).start()

    def x_wait(self, p, zz):
        if p == LENT_SUM:
            self.lent_copy(zz, self.where[2]).wait_recv()
        self.x_copy(p, zz).wait_recv()
        return self.x_slot(p, zz), None

    def slot(self, p, k, xx):
        return self.got_zz.at[xx, k] if p == self.turned else self.got_z.at[self.straight.index(p), k]

    def z_copy(self, p, zz, xx, sign, k):
        s, z, x, c = self.where
        return remote(
            self.view(p, zz, xx, c),
            self.slot(p, k, xx),
            self.z_s.at[p, xx, zz],
            self.z_r.at[p, xx, k],
            device(s, clipped(z + sign), x, c),
        )

    def z_out(self, p, zz, xx, sign):
        k = jnp.where((sign < 0) & (self.where[1] + sign == zz), NZ, zz)
        return self.z_copy(p, zz, xx, sign, k)

    def cols(self, p):
        x = self.where[2]
        return (x, 1 - x) if p == self.turned else (x,)

    def z_wait(self, p, zz, xx, k, cond):
        pl.when(cond)(lambda: self.z_copy(p, zz, xx, 1, k).wait_recv())
        return self.slot(p, k, xx), cond

    def z_step(self, p, k):
        s, z, x, c = self.where
        zz = farthest_first(z, k)
        sign = jnp.where(zz > z, 1, -1)
        before = inside(z - sign)
        terms = [] if p == self.turned else [self.x_wait(p, zz)]
        for xx in self.cols(p):
            dst = self.view(p, zz, xx, c)
            add_into(dst, dst, terms + [self.z_wait(p, zz, xx, zz, before)])
            self.z_out(p, zz, xx, sign).start()

    def z_last(self, p, xx):
        z = self.where[1]
        return [self.z_wait(p, z, xx, z, z > 0), self.z_wait(p, z, xx, NZ, z < NZ - 1)]

    def turn(self, p):
        s, z, x, c = self.where
        dst = self.view(p, z, 1 - x, c)
        add_into(dst, dst, self.z_last(p, 1 - x))
        self.x_copy(p, z).start()

    def close(self, p):
        s, z, x, c = self.where
        dst = self.view(p, z, x, c)
        terms = [self.x_wait(p, z)] + self.z_last(p, x)
        if p == LENT_SUM:
            add_into(dst, dst, terms)
            self.home_copy().start()
        else:
            self.store(p, dst, terms)

    def drain(self):
        for p in range(PIECES):
            for i in range(2 * NZ):
                self.core_copy(p, i).wait_send()
        for p in self.straight + [self.turned]:
            self.drain_links(p)
        if self.section == 0:
            self.lend(0, True)
            self.lend(1, True)
        else:
            self.home_copy().wait_send()

    def drain_links(self, p):
        z = self.where[1]
        for i in range(NZ - 1):
            zz = farthest_first(z, i)
            if p != self.turned:
                self.x_copy(p, zz).wait_send()
            for xx in self.cols(p):
                self.z_out(p, zz, xx, jnp.where(zz > z, 1, -1)).wait_send()
        self.x_copy(p, z).wait_send()


def head_windows():
    for k in range(8):
        start = HD * k // 128 * 128
        offset = HD * k - start
        span = 128 if offset + HD <= 128 else 256
        yield k, start, offset, span


def layers_kernel(
    n,
    tokens,
    cotangent,
    lengths,
    norm_gains,
    query_gain,
    wq,
    wo,
    wu,
    wd,
    out_half,
    token_half,
    d_q,
    d_o,
    d_u,
    d_d,
    small_out,
    held,
    lent,
    gain_all,
    gain_rows,
    query_block,
    hb,
    a1,
    qf,
    qb,
    kb,
    vb,
    prob,
    ob,
    mid,
    a2,
    up,
    hid,
    grad,
    dup,
    dmid,
    low,
    dob,
    give,
    sums,
    swap,
    got_core,
    got_x,
    got_z,
    got_zz,
    got_home,
    *sems,
):
    where = s, z, x, c = place()
    rows, width = hb.shape
    slots = cotangent.shape[1]
    half = width // 2
    group = 8 * HD
    factor = LOG_BASE / math.sqrt(HD)
    g_sems, r_sems = sems[:4], sems[4:14]
    swap_s, swap_r, hand_s, hand_r, back_s, back_r, end_s, end_r, load_sem, out_sem = sems[14:]
    across_y = device(1 - s, z, x, c)

    def view(p, zz, xx, cc):
        if p == GAINS:
            return gain_all.at[zz * 4 + xx * 2 + cc]
        if p == LENT:
            return lent.at[zz * 2 + xx]
        return held.at[p, pl.ds(pl.multiple_of((zz * 4 + xx * 2 + cc) * n, 16), n)]

    def sum_view(p, zz, xx, cc):
        return view(LENT if p == LENT_SUM else p, zz, xx, cc)

    def staged(p):
        return (qf if p < 3 else mid).at[pl.ds(p % 3 * n, n)]

    def in_hbm(p, first, others):
        return first.at[:, pl.ds(p * width, width)] if p < 3 else others[p - 3]

    def store_copy(p):
        return pltpu.make_async_copy(staged(p), in_hbm(p, d_q, (d_o, d_u, d_d)), out_sem.at[p])

    def store(p, block, terms):
        add_into(staged(p), block, terms)
        store_copy(p).start()

    gathers = [Gather(where, k, view, g_sems) for k in range(2)]
    scatters = [
        Scatter(where, k, sum_view, (got_core, got_x, got_z, got_zz, got_home), r_sems, store) for k in range(2)
    ]


    def row_loop(fn):
        @pl.loop(0, rows // 32)
        def _(k):
            fn(pl.ds(pl.multiple_of(k * 32, 32), 32))

    def tiles(emit, value):
        for k in range(width // TILE):
            emit(slice(k * TILE, (k + 1) * TILE), value[:, k * TILE : (k + 1) * TILE])

    def project(p, a, emit, halves):
        if not halves:
            tiles(emit, jnp.dot(a[...], held[p], preferred_element_type=F32))
            return

        @pl.loop(0, 2)
        def _(k):
            lanes = pl.ds(pl.multiple_of(k * half, 128), half)
            emit(lanes, jnp.dot(a[...], held[p, :, lanes], preferred_element_type=F32))

    def project_back(pieces, emit):
        @pl.loop(0, 2)
        def _(k):
            lanes = pl.ds(pl.multiple_of(k * half, 128), half)
            total = None
            for p, a in pieces:
                term = contract_cols(a[...], held[p, lanes, :])
                total = term if total is None else total + term
            emit(lanes, total)

    def weight_grad(p, a, g):
        @pl.loop(0, 2)
        def _(k):
            lanes = pl.ds(pl.multiple_of(k * half, 128), half)
            held[p, lanes] = contract_rows(a[:, lanes], g[...]).astype(BF16)

    def recip_of(value):
        return lax.rsqrt(jnp.mean(value * value, -1, keepdims=True) + NORM_EPS)

    def norm(src, row, dst):
        def part(r):
            value = src[r].astype(F32)
            dst[r] = (value * recip_of(value) * gain_rows[row : row + 1]).astype(BF16)

        row_loop(part)

    def put(ref):
        def emit(lanes, value):
            ref[:, lanes] = value.astype(ref.dtype)

        return emit

    def emit_query(lanes, value):
        qf[:, lanes] = value
        qb[:, lanes] = (value * gain_rows[2:3, lanes]).astype(BF16)

    def emit_up(lanes, value):
        up[:, lanes] = value
        hid[:, lanes] = (value / (1.0 + jnp.exp(-value))).astype(BF16)

    def emit_mid(lanes, value):
        mid[:, lanes] = hb[:, lanes].astype(F32) + value

    def emit_out(lanes, value):
        give[:, lanes] = (mid[:, lanes] + value).astype(BF16)

    def lane_mask(offset, span):
        lane = lax.broadcasted_iota(jnp.int32, (1, span), 1)
        return ((lane >= offset) & (lane < offset + HD)).astype(F32).astype(BF16)

    def attention(body):
        @pl.loop(0, 2 * rows // slots)
        def _(it):
            seq, g = it // 2, it % 2
            r = pl.ds(pl.multiple_of(seq * slots, slots), slots)

            def window(ref, start, span):
                return ref[r, pl.ds(pl.multiple_of(g * group + start, 128), span)]

            body(it, seq, r, g, window)

    def spread(total, start, span, value):
        for j in range(span // 128):
            k = start // 128 + j
            term = value[:, j * 128 : (j + 1) * 128]
            total[k] = term if total[k] is None else total[k] + term

    def attend(it, seq, r, g, window):
        allowed = causal_allowed(slots, lengths[seq])
        total = [None] * (group // 128)
        for k, start, offset, span in head_windows():
            only = lane_mask(offset, span)
            scores = contract_cols(window(qb, start, span) * only, window(kb, start, span))
            scores = jnp.where(allowed, scores, NEG_FILL)
            expd = jnp.exp(scores - jnp.max(scores, -1, keepdims=True))
            probs = expd / jnp.sum(expd, -1, keepdims=True)
            prob[it, k] = probs
            value = jnp.dot(probs.astype(BF16), window(vb, start, span) * only, preferred_element_type=F32)
            spread(total, start, span, value)
        for k, value in enumerate(total):
            ob[r, pl.ds(pl.multiple_of(g * group + k * 128, 128), 128)] = value.astype(BF16)

    def attend_back(it, seq, r, g, window):
        count = group // 128
        t_q, t_k, t_v = [None] * count, [None] * count, [None] * count
        for k, start, offset, span in head_windows():
            only = lane_mask(offset, span)
            d_o_part = window(dob, start, span) * only
            probs = prob[it, k]
            d_probs = contract_cols(d_o_part, window(vb, start, span))
            spread(t_v, start, span, contract_rows(probs.astype(BF16), d_o_part))
            d_scores = probs * (d_probs - jnp.sum(probs * d_probs, -1, keepdims=True))
            d_scores = d_scores.astype(BF16)
            spread(t_q, start, span, jnp.dot(d_scores, window(kb, start, span) * only, preferred_element_type=F32))
            spread(t_k, start, span, contract_rows(d_scores, window(qb, start, span) * only))
        for k in range(count):
            lanes = pl.ds(pl.multiple_of(g * group + k * 128, 128), 128)
            products = t_q[k] * qf[r, lanes]
            sums[2, :, lanes] += jnp.sum(products.reshape(slots // 8, 8, 128), 0)
            qb[r, lanes] = (t_q[k] * gain_rows[2:3, lanes]).astype(BF16)
            kb[r, lanes] = t_k[k].astype(BF16)
            vb[r, lanes] = t_v[k].astype(BF16)

    def emit_dup(lanes, value):
        u = up[:, lanes]
        sig = 1.0 / (1.0 + jnp.exp(-u))
        dup[:, lanes] = (value * sig * (1.0 + u * (1.0 - sig))).astype(BF16)

    def norm_grad(row, src, base, emit):
        def part(r):
            value, d_normed = src[r].astype(F32), up[r]
            recip = recip_of(value)
            sums[row] += jnp.sum((d_normed * value * recip).reshape(4, 8, width), 0)
            emit(r, base[r].astype(F32) + norm_back(value, recip, d_normed * gain_rows[row : row + 1]))

        row_loop(part)

    def emit_dmid(r, value):
        dmid[r] = value
        low[r] = value.astype(BF16)

    def emit_give(r, value):
        give[r] = value.astype(BF16)

    def window_of(k, size):
        start = min(size * k // 128 * 128, width - 256)
        return start, size * k - start

    def rolled(block, shift):
        return pltpu.roll(block, shift, 1) if shift else block

    def spread_gains():
        gain_rows[...] = jnp.zeros_like(gain_rows)
        none = jnp.zeros((8, 128), F32)
        for f in range(4 * NZ):
            start, shift = window_of(f, n)
            gain_rows[:, start : start + 256] += rolled(jnp.concatenate([gain_all[f], none], -1), shift)
        value = query_block[...]
        scale = (jnp.maximum(value, 0.0) + jnp.log1p(jnp.exp(-jnp.abs(value)))) * factor
        lane = lax.broadcasted_iota(jnp.int32, (8, 128), 1)
        row = lax.broadcasted_iota(jnp.int32, (8, 128), 0)
        scale = jnp.where((lane < HD) & (row == 2), scale, 0.0)
        for k in range(H):
            start, shift = window_of(k, HD)
            gain_rows[:, start : start + 256] += rolled(jnp.concatenate([scale, none], -1), shift)

    def finish_small(value):
        me = z * 4 + x * 2 + c
        own = jnp.zeros((8, 128), F32)
        for f in range(4 * NZ):
            start, shift = window_of(f, n)
            part = rolled(value[:, start : start + 256], (256 - shift) % 256)[:, :128]
            own = own + jnp.where(me == f, part, 0.0)
        heads = jnp.zeros((8, 128), F32)
        for k in range(H):
            start, shift = window_of(k, HD)
            heads = heads + rolled(value[:, start : start + 256], (256 - shift) % 256)[:, :128]
        gate = factor / (1.0 + jnp.exp(-query_block[...]))
        row = lax.broadcasted_iota(jnp.int32, (8, 128), 0)
        small_out[...] = jnp.where(row == 2, heads * gate, own)

    def forward_stage(p, halves):
        if p == 0:
            spread_gains()
            norm(hb, 0, a1)
            project(0, a1, emit_query, halves)
        elif p == 1:
            project(1, a1, put(kb), halves)
        elif p == 2:
            project(2, a1, put(vb), halves)
            attention(attend)
        elif p == 3:
            project(3, ob, emit_mid, halves)
            norm(mid, 1, a2)
        elif p == 4:
            project(4, a2, emit_up, halves)
        else:
            project(5, hid, emit_out, halves)


    def hand(k):
        r = pl.ds(k * slots, slots)
        return remote(give.at[r], hb.at[r], hand_s.at[k], hand_r.at[k], across_y)

    def back(k):
        r = pl.ds(k * slots, slots)
        return remote(give.at[r], grad.at[r], back_s.at[k], back_r.at[k], across_y)

    def end(which):
        dst, col = ((out_half, 0), (token_half, half))[which]
        return remote(give.at[:, col : col + half], dst, end_s.at[which], end_r.at[which], across_y)


    def load(act):
        for k in range(rows // slots):
            r = pl.ds(k * slots, slots)
            here = pltpu.make_async_copy(tokens.at[k], hb.at[r], load_sem.at[k])
            there = pltpu.make_async_copy(cotangent.at[k], grad.at[r], load_sem.at[k])
            pl.when(s == 0)(getattr(here, act))
            pl.when(s == 1)(getattr(there, act))
        for p in range(PIECES):
            cp = pltpu.make_async_copy(in_hbm(p, wq, (wo, wu, wd)), staged(p), load_sem.at[rows // slots + p])
            getattr(cp, act)()

    load("start")
    me = z * 4 + x * 2 + c
    gain_all[me] = jnp.zeros((8, 128), F32)
    gain_all[me, 0:2, 0:n] = norm_gains[...].astype(BF16).astype(F32)
    query_block[...] = jnp.zeros_like(query_block)
    query_block[:, 0:HD] = jnp.broadcast_to(query_gain[...], (8, HD))
    sums[...] = jnp.zeros_like(sums)
    neighbour_barrier(s, z, x, c)
    load("wait")
    mine = pl.ds(pl.multiple_of((z * 4 + x * 2 + c) * n, 16), n)
    for p in range(PIECES):
        held[p, mine] = staged(p)[...].astype(BF16)

    def forward(section):
        for step in GATHER_STEPS[section]:
            if step[0] == "stage":
                forward_stage(step[1], True)
            elif step[0] == "hand":
                for k in range(rows // slots):
                    hand(k).wait_recv()
            else:
                getattr(gathers[section], step[0])(*step[1:])

    def hand_start():
        for k in range(rows // slots):
            hand(k).start()

    @pl.when(s == 0)
    def _():
        forward(0)
        hand_start()
        gathers[0].drain()
        for k in range(rows // slots):
            hand(k).wait_send()
            back(k).wait_recv()

    @pl.when(s == 1)
    def _():
        forward(1)
        gathers[1].drain()
        end(0).start()
        out_half[...] = give[:, half:]
        for k in range(rows // slots):
            row = lax.broadcasted_iota(jnp.int32, (slots, 1), 0)
            live = (row < lengths[k]).astype(F32)
            part = pl.ds(k * slots, slots)
            grad[part] = (grad[part].astype(F32) * live).astype(BF16)

    grads = ((a1, qb), (a1, kb), (a1, vb), (ob, low), (a2, dup), (hid, grad))

    def exchange(k):
        partner = (
            device(s, z, x, 1 - c),
            device(s, z, 1 - x, c),
            device(s, z + 1 - 2 * (z % 2), x, c),
            device(s, (z + 2) % NZ, x, c),
        )[k]
        return remote(swap.at[k, 0], swap.at[k, 1], swap_s.at[k], swap_r.at[k], partner)

    def small(k):
        if k == 0:
            totals = [jnp.sum(sums[i], 0, keepdims=True) for i in range(3)]
            swap[0, 0] = jnp.concatenate(totals + [jnp.zeros((5, width), F32)], 0)
            exchange(0).start()
            return
        exchange(k - 1).wait_recv()
        value = swap[k - 1, 0] + swap[k - 1, 1]
        if k < 4:
            swap[k, 0] = value
            exchange(k).start()
        else:
            finish_small(value)

    def finish_input(section):
        if section == 1:
            end(0).wait_send()
        norm_grad(0, hb, dmid, emit_give)
        if section == 1:
            for k in range(rows // slots):
                back(k).start()
        else:
            end(1).start()
            token_half[...] = give[:, :half]

    compute = dict(
        hidden=lambda section: project_back([(5, grad)], emit_dup),
        normed_two=lambda section: project_back([(4, dup)], put(up)),
        middle=lambda section: norm_grad(1, mid, grad, emit_dmid),
        attended=lambda section: project_back([(3, low)], put(dob)),
        heads=lambda section: attention(attend_back),
        normed=lambda section: project_back([(0, qb), (1, kb), (2, vb)], put(up)),
        input=finish_input,
        weight=lambda section, p: weight_grad(p, *grads[p]),
        small=lambda section, k: small(k),
    )

    def backward(section):
        for step in BACKWARD_STEPS[section]:
            if step[0] in compute:
                compute[step[0]](section, *step[1:])
            else:
                getattr(scatters[section], step[0])(*step[1:])

    pl.when(s == 0)(lambda: backward(0))
    pl.when(s == 1)(lambda: backward(1))
    pl.when(s == 0)(scatters[0].drain)
    pl.when(s == 1)(scatters[1].drain)
    for p in range(PIECES):
        store_copy(p).wait()
    for k in range(4):
        exchange(k).wait_send()

    @pl.when(s == 0)
    def _():
        end(1).wait_send()
        end(0).wait_recv()

    @pl.when(s == 1)
    def _():
        for k in range(rows // slots):
            back(k).wait_send()
        end(1).wait_recv()


def finish_kernel(small, *refs):
    froms, tos, (d_gains, d_query), held, (in_sem, out_sem) = refs[:6], refs[6:12], refs[12:14], refs[14:20], refs[20:]
    ins = [pltpu.make_async_copy(a, h, in_sem.at[k]) for k, (a, h) in enumerate(zip(froms, held))]
    outs = [pltpu.make_async_copy(h, b, out_sem.at[k]) for k, (h, b) in enumerate(zip(held, tos))]
    for cp in ins:
        cp.start()
    d_gains[...] = small[0:2, : d_gains.shape[1]]
    d_query[...] = small[2:3, :HD]
    for came, goes in zip(ins, outs):
        came.wait()
        goes.start()
    for cp in outs:
        cp.wait()


def near_shards(
    tokens, cotangent, lengths, qkv_weight, out_weight, up_weight, down_weight, norm_gains, query_gain
):
    n, width = out_weight.shape
    count, slots, _ = tokens.shape
    rows = count * slots
    dma = pltpu.SemaphoreType.DMA
    whole = pl.BlockSpec(memory_space=pltpu.VMEM)
    far = pl.BlockSpec(memory_space=pl.ANY)
    block = (n, width)
    low_rows = pltpu.VMEM((rows, width), BF16)
    wide_rows = pltpu.VMEM((rows, width), F32)
    scratch = dict(
        held=pltpu.VMEM((PIECES, 4 * NZ * n, width), BF16),
        lent=pltpu.VMEM((2 * NZ,) + block, BF16),
        gain_all=pltpu.VMEM((4 * NZ, 8, 128), F32),
        gain_rows=pltpu.VMEM((8, width), F32),
        query_block=pltpu.VMEM((8, 128), F32),
        hb=low_rows,
        a1=low_rows,
        qf=wide_rows,
        qb=low_rows,
        kb=low_rows,
        vb=low_rows,
        prob=pltpu.VMEM((2 * count, 8, slots, slots), F32),
        ob=low_rows,
        mid=wide_rows,
        a2=low_rows,
        up=wide_rows,
        hid=low_rows,
        grad=low_rows,
        dup=low_rows,
        dmid=wide_rows,
        low=low_rows,
        dob=low_rows,
        give=low_rows,
        sums=pltpu.VMEM((3, 8, width), F32),
        swap=pltpu.VMEM((4, 2, 8, width), F32),
        got_core=pltpu.VMEM((PIECES, 2 * NZ) + block, BF16),
        got_x=pltpu.VMEM((PIECES * NZ + 1,) + block, BF16),
        got_z=pltpu.VMEM((PIECES, NZ + 1) + block, BF16),
        got_zz=pltpu.VMEM((2, NZ + 1) + block, BF16),
        got_home=pltpu.VMEM(block, BF16),
    )
    pieces = PIECES + 2
    semaphores = [
        dma((pieces, 2 * NZ, 4)),
        dma((pieces, 2 * NZ)),
        dma((pieces, 2 * NZ)),
        dma((pieces, 2 * NZ)),
        dma((PIECES, 2 * NZ)),
        dma((PIECES, 2 * NZ)),
        dma((PIECES + 1, NZ)),
        dma((PIECES + 1, NZ)),
        dma((PIECES + 1, 2, NZ)),
        dma((PIECES + 1, 2, NZ + 1)),
        dma((2 * NZ,)),
        dma((2 * NZ,)),
        dma((1,)),
        dma((1,)),
        dma((4,)),
        dma((4,)),
        dma((count,)),
        dma((count,)),
        dma((count,)),
        dma((count,)),
        dma((2,)),
        dma((2,)),
        dma((count + PIECES,)),
        dma((PIECES,)),
    ]
    half = jax.ShapeDtypeStruct((rows, width // 2), BF16)
    square = jax.ShapeDtypeStruct(block, F32)
    shapes = (half, half, jax.ShapeDtypeStruct((n, 3 * width), F32), square, square, square)
    *results, small = pl.pallas_call(
        lambda *refs: layers_kernel(n, *refs),
        out_shape=shapes + (jax.ShapeDtypeStruct((8, 128), F32),),
        in_specs=[far, far, pl.BlockSpec(memory_space=pltpu.SMEM), whole, whole] + [far] * 4,
        out_specs=(whole, whole) + (far,) * 4 + (whole,),
        scratch_shapes=list(scratch.values()) + semaphores,
        compiler_params=pltpu.CompilerParams(
            collective_id=1, has_side_effects=True, vmem_limit_bytes=63 << 20
        ),
        name="two_layers",
    )(tokens, cotangent, lengths, norm_gains.T, query_gain, qkv_weight, out_weight, up_weight, down_weight)
    out, d_tokens, d_q, d_o, d_u, d_d, d_gains, d_query = pl.pallas_call(
        finish_kernel,
        out_shape=shapes + (jax.ShapeDtypeStruct((2, n), F32), jax.ShapeDtypeStruct((1, HD), F32)),
        in_specs=[whole] + [far] * 6,
        out_specs=(far,) * 6 + (whole,) * 2,
        scratch_shapes=[pltpu.VMEM(item.shape, item.dtype) for item in shapes] + [dma((6,)), dma((6,))],
        compiler_params=pltpu.CompilerParams(vmem_limit_bytes=63 << 20),
        name="results",
    )(small, *results)
    shape = (count, slots, width // 2)
    return (
        out.reshape(shape),
        d_tokens.reshape(shape),
        d_q[None],
        d_o[None],
        d_u[None],
        d_d[None],
        d_gains.T[None],
        d_query,
    )


def swapped(value, axis, bit):
    return lax.ppermute(value, axis, [(i, i ^ 1 << bit) for i in range(lax.axis_size(axis))])


def causal_allowed(row_count, length):
    row_ids = lax.broadcasted_iota(jnp.int32, (row_count, row_count), 0)
    col_ids = lax.broadcasted_iota(jnp.int32, (row_count, row_count), 1)
    return (col_ids <= row_ids) & (col_ids < length)


def contract_rows(left, right):
    return lax.dot_general(
        left, right, (((0,), (0,)), ((), ())), preferred_element_type=jnp.float32
    )


def contract_cols(left, right):
    return lax.dot_general(
        left, right, (((1,), (1,)), ((), ())), preferred_element_type=jnp.float32
    )


def norm_back(source, recip, grad_flat):
    return recip * grad_flat - source * recip**3 * jnp.mean(grad_flat * source, -1, keepdims=True)


def layer_forward(layer_input, length, weights, query_scale):
    qkv_w, out_w, up_w, down_w, gain_pair = weights
    row_count, width = layer_input.shape
    gain_one = gain_pair[:, 0].astype(jnp.float32)
    gain_two = gain_pair[:, 1].astype(jnp.float32)
    recip_one = lax.rsqrt(jnp.mean(layer_input * layer_input, -1, keepdims=True) + NORM_EPS)
    normed = (layer_input * recip_one * gain_one).astype(jnp.bfloat16)
    proj = jnp.dot(normed, qkv_w, preferred_element_type=jnp.float32)
    query = proj[:, :width].reshape(row_count, H, HD)
    query_b = (query * query_scale).astype(jnp.bfloat16)
    keys_b = proj[:, width : 2 * width].astype(jnp.bfloat16).reshape(row_count, H, HD)
    values_b = proj[:, 2 * width :].astype(jnp.bfloat16).reshape(row_count, H, HD)
    scores = jnp.einsum("qhd,khd->hqk", query_b, keys_b, preferred_element_type=jnp.float32)
    scores = jnp.where(causal_allowed(row_count, length)[None], scores, NEG_FILL)
    row_peak = jnp.max(scores, -1, keepdims=True)
    expd = jnp.exp(scores - row_peak)
    row_total = jnp.sum(expd, -1, keepdims=True)
    probs = expd / row_total
    logsum = (row_peak + jnp.log(row_total))[..., 0]
    attended = (
        jnp.einsum(
            "hqk,khd->qhd", probs.astype(jnp.bfloat16), values_b, preferred_element_type=jnp.float32
        )
        .reshape(row_count, width)
        .astype(jnp.bfloat16)
    )
    middle = layer_input + jnp.dot(attended, out_w, preferred_element_type=jnp.float32)
    recip_two = lax.rsqrt(jnp.mean(middle * middle, -1, keepdims=True) + NORM_EPS)
    normed_two = (middle * recip_two * gain_two).astype(jnp.bfloat16)
    upper = jnp.dot(normed_two, up_w, preferred_element_type=jnp.float32)
    hidden = jax.nn.silu(upper).astype(jnp.bfloat16)
    layer_output = middle + jnp.dot(hidden, down_w, preferred_element_type=jnp.float32)
    saved = (
        layer_input,
        normed,
        query,
        query_b,
        keys_b,
        values_b,
        logsum,
        attended,
        middle,
        normed_two,
        upper,
        hidden,
        recip_one,
        recip_two,
    )
    return (layer_output, saved)


def layer_backward(saved, length, weights, query_scale, grad_output):
    qkv_w, out_w, up_w, down_w, gain_pair = weights
    (
        layer_input,
        normed,
        query,
        query_b,
        keys_b,
        values_b,
        logsum,
        attended,
        middle,
        normed_two,
        upper,
        hidden,
        recip_one,
        recip_two,
    ) = saved
    row_count, width = layer_input.shape
    gain_one = gain_pair[:, 0].astype(jnp.float32)
    gain_two = gain_pair[:, 1].astype(jnp.float32)
    grad_low = grad_output.astype(jnp.bfloat16)
    d_down = contract_rows(hidden, grad_low)
    d_hidden = contract_cols(grad_low, down_w)
    sigmoid_up = jax.nn.sigmoid(upper)
    d_upper = (d_hidden * sigmoid_up * (1.0 + upper * (1.0 - sigmoid_up))).astype(jnp.bfloat16)
    d_up = contract_rows(normed_two, d_upper)
    d_normed_two = contract_cols(d_upper, up_w)
    d_gain_two = jnp.sum(d_normed_two * middle * recip_two, 0)
    d_middle = grad_output + norm_back(middle, recip_two, d_normed_two * gain_two)
    middle_low = d_middle.astype(jnp.bfloat16)
    d_out = contract_rows(attended, middle_low)
    d_attended = contract_cols(middle_low, out_w).astype(jnp.bfloat16).reshape(row_count, H, HD)
    scores = jnp.einsum("qhd,khd->hqk", query_b, keys_b, preferred_element_type=jnp.float32)
    scores = jnp.where(causal_allowed(row_count, length)[None], scores, NEG_FILL)
    probs = jnp.exp(scores - logsum[..., None])
    d_probs = jnp.einsum("qhd,khd->hqk", d_attended, values_b, preferred_element_type=jnp.float32)
    d_values = jnp.einsum(
        "hqk,qhd->khd", probs.astype(jnp.bfloat16), d_attended, preferred_element_type=jnp.float32
    ).astype(jnp.bfloat16)
    d_scores = (probs * (d_probs - jnp.sum(probs * d_probs, -1, keepdims=True))).astype(
        jnp.bfloat16
    )
    d_query_s = jnp.einsum("hqk,khd->qhd", d_scores, keys_b, preferred_element_type=jnp.float32)
    d_keys = jnp.einsum(
        "hqk,qhd->khd", d_scores, query_b, preferred_element_type=jnp.float32
    ).astype(jnp.bfloat16)
    d_scale = jnp.sum(d_query_s * query, (0, 1))
    d_query = (d_query_s * query_scale).astype(jnp.bfloat16)
    d_proj = jnp.concatenate(
        [
            d_query.reshape(row_count, width),
            d_keys.reshape(row_count, width),
            d_values.reshape(row_count, width),
        ],
        -1,
    )
    d_qkv = contract_rows(normed, d_proj)
    d_normed = contract_cols(d_proj, qkv_w)
    d_gain_one = jnp.sum(d_normed * layer_input * recip_one, 0)
    d_input = d_middle + norm_back(layer_input, recip_one, d_normed * gain_one)
    d_gains = jnp.stack([d_gain_one, d_gain_two], -1)
    return (d_input, (d_qkv, d_out, d_up, d_down, d_gains), d_scale)


def shards(
    tokens,
    cotangent,
    lengths,
    qkv_weight,
    out_weight,
    up_weight,
    down_weight,
    norm_gains,
    query_gain,
):
    if lax.axis_size("fsdp") == 4 * NZ:
        return near_shards(
            tokens,
            cotangent,
            lengths,
            qkv_weight[0],
            out_weight[0],
            up_weight[0],
            down_weight[0],
            norm_gains[0],
            query_gain,
        )
    section_index = lax.axis_index("section")
    micro_count, slot_rows, width = tokens.shape
    half_width = width // 2
    scale_factor = LOG_BASE / math.sqrt(HD)
    query_scale = jax.nn.softplus(query_gain[0]) * scale_factor

    def gather_weights():
        pieces = (
            lax.all_gather(qkv_weight.astype(jnp.bfloat16), "fsdp", axis=1, tiled=True),
            lax.all_gather(out_weight.astype(jnp.bfloat16), "fsdp", axis=1, tiled=True),
            lax.all_gather(up_weight.astype(jnp.bfloat16), "fsdp", axis=1, tiled=True),
            lax.all_gather(down_weight.astype(jnp.bfloat16), "fsdp", axis=1, tiled=True),
            lax.all_gather(norm_gains.astype(jnp.bfloat16), "fsdp", axis=1, tiled=True),
        )
        return tuple((piece[0] for piece in pieces))

    def handoff(value):
        return swapped(value, "section", 0)

    weights = gather_weights()
    received = jnp.zeros((slot_rows, width), jnp.bfloat16)
    kept = []
    result_parts = []
    for tick_index in range(micro_count + 1):
        first_input = tokens[min(tick_index, micro_count - 1)].astype(jnp.float32)
        layer_input = jnp.where(section_index == 0, first_input, received.astype(jnp.float32))
        micro_index = jnp.clip(tick_index - section_index, 0, micro_count - 1)
        length = lengths[micro_index]
        layer_output, saved = layer_forward(layer_input, length, weights, query_scale)
        sent = layer_output.astype(jnp.bfloat16)
        received = handoff(sent)
        kept.append(saved)
        if tick_index >= 1:
            finished = jnp.where(section_index == 1, sent, received)
            result_parts.append(
                lax.dynamic_slice_in_dim(finished, section_index * half_width, half_width, 1)
            )
    output = jnp.stack(result_parts)
    weights = gather_weights()
    row_ids = lax.iota(jnp.int32, slot_rows)
    grad_received = jnp.zeros((slot_rows, width), jnp.bfloat16)
    grad_parts = []
    grad_totals = None
    scale_total = jnp.zeros((HD,), jnp.float32)
    for tick_index in range(micro_count + 1):
        offset = tick_index - 1 + section_index
        micro_index = jnp.clip(offset, 0, micro_count - 1)
        length = lengths[micro_index]
        live_tick = ((offset >= 0) & (offset < micro_count)).astype(jnp.float32)
        live_rows = (row_ids < length).astype(jnp.float32)[:, None]
        top_grad = cotangent[min(tick_index, micro_count - 1)].astype(jnp.float32) * live_rows
        grad_output = jnp.where(section_index == 1, top_grad, grad_received.astype(jnp.float32))
        saved = jax.tree.map(
            lambda early, late: jnp.where(section_index == 0, early, late),
            kept[max(tick_index - 1, 0)],
            kept[min(tick_index + 1, micro_count)],
        )
        d_input, weight_grads, scale_grad = layer_backward(
            saved, length, weights, query_scale, grad_output
        )
        weight_grads = tuple((item * live_tick for item in weight_grads))
        scale_total = scale_total + scale_grad * live_tick
        sent = d_input.astype(jnp.bfloat16)
        grad_received = handoff(sent)
        if tick_index >= 1:
            finished = jnp.where(section_index == 0, sent, grad_received)
            grad_parts.append(
                lax.dynamic_slice_in_dim(finished, section_index * half_width, half_width, 1)
            )
        if grad_totals is None:
            grad_totals = weight_grads
        else:
            grad_totals = tuple((total + piece for total, piece in zip(grad_totals, weight_grads)))
    d_tokens = jnp.stack(grad_parts)
    scattered = (
        lax.psum_scatter(grad_totals[0], "fsdp", scatter_dimension=0, tiled=True),
        lax.psum_scatter(grad_totals[1], "fsdp", scatter_dimension=0, tiled=True),
        lax.psum_scatter(grad_totals[2], "fsdp", scatter_dimension=0, tiled=True),
        lax.psum_scatter(grad_totals[3], "fsdp", scatter_dimension=0, tiled=True),
        lax.psum_scatter(grad_totals[4], "fsdp", scatter_dimension=0, tiled=True),
    )
    owned = tuple((item[None] for item in scattered))
    scale_sum = lax.psum(scale_total, "fsdp")
    d_query_gain = (scale_sum * jax.nn.sigmoid(query_gain[0]) * scale_factor)[None]
    return (output, d_tokens, owned[0], owned[1], owned[2], owned[3], owned[4], d_query_gain)


def solution(mesh):
    in_specs = (
        P("fsdp", None, None),
        P("fsdp", None, None),
        P("fsdp"),
        P("section", "fsdp", None),
        P("section", "fsdp", None),
        P("section", "fsdp", None),
        P("section", "fsdp", None),
        P("section", "fsdp", None),
        P("section", None),
    )
    out_specs = (
        P("fsdp", None, "section"),
        P("fsdp", None, "section"),
        P("section", "fsdp", None),
        P("section", "fsdp", None),
        P("section", "fsdp", None),
        P("section", "fsdp", None),
        P("section", "fsdp", None),
        P("section", None),
    )
    return jax.shard_map(shards, mesh=mesh, in_specs=in_specs, out_specs=out_specs, check_vma=False)
```

```python
import math

import jax
import jax.numpy as jnp
from jax import lax
from jax.experimental import pallas as pl
from jax.experimental.pallas import tpu as pltpu
from jax.sharding import PartitionSpec as P

H = 16
HD = 80


NORM_EPS = 1e-06
NEG_FILL = -1e30
LOG_BASE = 1.442695041


MESH_ID = pl.DeviceIdType.MESH
BF16 = jnp.bfloat16
F32 = jnp.float32
NZ = 4
TILE = 256
PIECES = 6
GAINS = 6
LENT = 7
LENT_IN = 5
TURN_IN = (4, 5)
LENT_OUT = 5
LENT_SUM = 6
TURN_OUT = (4, 4)


def place():
    s, f = lax.axis_index("section"), lax.axis_index("fsdp")
    return s, f // 4, (f // 2) % 2, f % 2


def device(s, z, x, c):
    return (s, z * 4 + x * 2 + c)


def inside(z):
    return (z >= 0) & (z < NZ)


def clipped(z):
    return jnp.clip(z, 0, NZ - 1)


def neighbour_barrier(s, z, x, c):
    barrier = pltpu.get_barrier_semaphore()

    def tell(target):
        pl.semaphore_signal(barrier, inc=1, device_id=target, device_id_type=MESH_ID)

    tell(device(s, z, x, 1 - c))
    tell(device(s, z, 1 - x, c))
    tell(device(1 - s, z, x, c))
    tell(device(s, (z + 2) % NZ, x, c))
    pl.when(z > 0)(lambda: tell(device(s, z - 1, x, c)))
    pl.when(z < NZ - 1)(lambda: tell(device(s, z + 1, x, c)))
    pl.semaphore_wait(barrier, 4 + (z > 0).astype(jnp.int32) + (z < NZ - 1).astype(jnp.int32))


def remote(src, dst, send_sem, recv_sem, target):
    return pltpu.make_async_remote_copy(
        src, dst, send_sem, recv_sem, device_id=target, device_id_type=MESH_ID
    )


GATHER_STEPS = (
    (
        ("own", 0),
        ("own", 2),
        ("own", 6),
        ("own", 4),
        ("own", 5),
        ("relay", 2, 1, (-1,)),
        ("own", 1),
        ("relay", 0, 1, (-1,)),
        ("relay", 0, 1, (1,)),
        ("relay", 0, 2, (-1,)),
        ("relay", 6, 1, (1,)),
        ("relay", 6, 1, (-1,)),
        ("relay", 2, 1, (1,)),
        ("relay", 6, 2, (1,)),
        ("relay", 1, 1, (-1,)),
        ("relay", 0, 2, (1,)),
        ("relay", 0, 3, (-1,)),
        ("relay", 6, 2, (-1,)),
        ("relay", 6, 3, (-1,)),
        ("relay", 1, 1, (1,)),
        ("relay", 1, 2, (-1,)),
        ("turn", 4),
        ("relay", 1, 2, (1,)),
        ("relay", 1, 3, (-1,)),
        ("relay", 0, 3, (1,)),
        ("across", 0, 0),
        ("relay", 6, 3, (1,)),
        ("across", 6, 0),
        ("across", 6, 1),
        ("relay", 2, 2, (-1,)),
        ("relay", 2, 2, (1,)),
        ("relay", 2, 3, (-1,)),
        ("across", 6, 2),
        ("across", 0, 1),
        ("across", 6, 3),
        ("own", 3),
        ("relay", 2, 3, (1,)),
        ("relay", 4, 1, (1,)),
        ("relay", 3, 1, (-1,)),
        ("home", 5, 0),
        ("home", 5, 1),
        ("relay", 1, 3, (1,)),
        ("across", 1, 0),
        ("across", 2, 0),
        ("home", 5, 2),
        ("across", 1, 1),
        ("relay", 4, 1, (-1,)),
        ("relay", 4, 2, (1,)),
        ("across", 1, 2),
        ("across", 2, 1),
        ("finish", 6),
        ("home", 5, 3),
        ("across", 2, 2),
        ("across", 2, 3),
        ("across", 1, 3),
        ("relay", 4, 2, (-1,)),
        ("across", 0, 2),
        ("across", 0, 3),
        ("finish", 0),
        ("stage", 0),
        ("relay", 3, 1, (1,)),
        ("finish", 5),
        ("relay", 3, 2, (-1,)),
        ("finish", 1),
        ("stage", 1),
        ("finish", 2),
        ("relay", 4, 3, (-1,)),
        ("relay", 4, 3, (1,)),
        ("finish", 4),
        ("relay", 3, 2, (1,)),
        ("relay", 3, 3, (-1,)),
        ("relay", 3, 3, (1,)),
        ("across", 3, 0),
        ("stage", 2),
        ("across", 3, 1),
        ("across", 3, 2),
        ("across", 3, 3),
        ("finish", 3),
        ("stage", 3),
        ("stage", 4),
        ("stage", 5),
    ),
    (
        ("own", 5),
        ("own", 0),
        ("own", 7),
        ("relay", 0, 1, (-1,)),
        ("relay", 7, 1, (-1,)),
        ("own", 6),
        ("own", 2),
        ("relay", 7, 1, (1,)),
        ("relay", 6, 1, (-1,)),
        ("relay", 7, 2, (-1,)),
        ("relay", 6, 1, (1,)),
        ("relay", 7, 2, (1,)),
        ("relay", 6, 2, (-1,)),
        ("relay", 7, 3, (-1,)),
        ("relay", 0, 1, (1,)),
        ("relay", 0, 2, (1,)),
        ("turn", 5),
        ("relay", 5, 1, (-1,)),
        ("relay", 6, 2, (1,)),
        ("own", 4),
        ("relay", 7, 3, (1,)),
        ("across", 7, 0),
        ("own", 3),
        ("own", 1),
        ("across", 7, 1),
        ("across", 7, 2),
        ("across", 7, 3),
        ("relay", 2, 1, (-1,)),
        ("relay", 1, 1, (1,)),
        ("relay", 6, 3, (1,)),
        ("relay", 0, 2, (-1,)),
        ("relay", 0, 3, (1,)),
        ("relay", 1, 1, (-1,)),
        ("relay", 0, 3, (-1,)),
        ("relay", 2, 1, (1,)),
        ("relay", 2, 2, (1,)),
        ("relay", 4, 1, (1,)),
        ("relay", 6, 3, (-1,)),
        ("across", 6, 0),
        ("across", 0, 0),
        ("relay", 1, 2, (1,)),
        ("across", 6, 1),
        ("relay", 1, 2, (-1,)),
        ("relay", 1, 3, (1,)),
        ("relay", 2, 2, (-1,)),
        ("relay", 2, 3, (1,)),
        ("relay", 1, 3, (-1,)),
        ("across", 6, 2),
        ("relay", 3, 1, (1,)),
        ("across", 0, 1),
        ("across", 0, 2),
        ("across", 0, 3),
        ("relay", 3, 1, (-1,)),
        ("relay", 5, 1, (1,)),
        ("relay", 3, 2, (-1,)),
        ("across", 1, 0),
        ("relay", 2, 3, (-1,)),
        ("relay", 3, 2, (1,)),
        ("relay", 3, 3, (-1,)),
        ("across", 1, 1),
        ("across", 1, 2),
        ("across", 2, 0),
        ("across", 2, 1),
        ("across", 2, 2),
        ("across", 2, 3),
        ("across", 1, 3),
        ("relay", 5, 2, (-1,)),
        ("relay", 4, 1, (-1,)),
        ("relay", 5, 2, (1,)),
        ("finish", 2),
        ("relay", 4, 2, (-1,)),
        ("finish", 1),
        ("relay", 3, 3, (1,)),
        ("finish", 0),
        ("across", 3, 0),
        ("across", 3, 1),
        ("relay", 5, 3, (1,)),
        ("across", 6, 3),
        ("relay", 5, 3, (-1,)),
        ("relay", 4, 2, (1,)),
        ("finish", 5),
        ("finish", 6),
        ("across", 3, 2),
        ("across", 3, 3),
        ("finish", 3),
        ("relay", 4, 3, (1,)),
        ("relay", 4, 3, (-1,)),
        ("across", 4, 0),
        ("across", 4, 1),
        ("hand",),
        ("stage", 0),
        ("stage", 1),
        ("stage", 2),
        ("across", 4, 2),
        ("across", 4, 3),
        ("stage", 3),
        ("finish", 4),
        ("stage", 4),
        ("stage", 5),
    ),
)
BACKWARD_STEPS = (
    (
        ("hidden",),
        ("normed_two",),
        ("weight", 4),
        ("core_send", 4),
        ("middle",),
        ("attended",),
        ("weight", 3),
        ("core_send", 3),
        ("core_add", 4),
        ("z_step", 4, 0),
        ("core_add", 3),
        ("weight", 5),
        ("core_send", 5),
        ("x_send", 3),
        ("z_step", 4, 1),
        ("heads",),
        ("normed",),
        ("weight", 0),
        ("z_step", 3, 0),
        ("core_send", 0),
        ("core_add", 0),
        ("x_send", 0),
        ("z_step", 4, 2),
        ("weight", 2),
        ("weight", 1),
        ("core_send", 1),
        ("core_add", 5),
        ("lend", 0),
        ("lend", 1),
        ("core_add", 1),
        ("input",),
        ("z_step", 0, 0),
        ("small", 0),
        ("small", 1),
        ("x_send", 1),
        ("z_step", 0, 1),
        ("z_step", 0, 2),
        ("core_send", 2),
        ("z_step", 1, 0),
        ("z_step", 3, 1),
        ("small", 2),
        ("core_add", 2),
        ("x_send", 2),
        ("close", 0),
        ("z_step", 1, 1),
        ("z_step", 1, 2),
        ("z_step", 2, 0),
        ("close", 1),
        ("z_step", 3, 2),
        ("z_step", 2, 1),
        ("turn", 4),
        ("z_step", 2, 2),
        ("small", 3),
        ("small", 4),
        ("close", 3),
        ("close", 4),
        ("close", 2),
        ("home",),
    ),
    (
        ("hidden",),
        ("normed_two",),
        ("middle",),
        ("attended",),
        ("weight", 5),
        ("core_send", 5),
        ("core_add", 5),
        ("x_send", 5),
        ("heads",),
        ("normed",),
        ("input",),
        ("weight", 3),
        ("core_send", 3),
        ("z_step", 5, 0),
        ("weight", 4),
        ("core_send", 4),
        ("core_add", 3),
        ("x_send", 3),
        ("weight", 0),
        ("core_send", 0),
        ("core_add", 4),
        ("z_step", 4, 0),
        ("core_add", 0),
        ("x_send", 0),
        ("weight", 2),
        ("core_send", 2),
        ("z_step", 5, 1),
        ("core_add", 2),
        ("x_send", 2),
        ("weight", 1),
        ("z_step", 4, 1),
        ("core_send", 1),
        ("small", 0),
        ("core_add", 1),
        ("z_step", 3, 0),
        ("z_step", 3, 1),
        ("z_step", 4, 2),
        ("small", 1),
        ("z_step", 0, 0),
        ("z_step", 5, 2),
        ("z_step", 2, 0),
        ("z_step", 2, 1),
        ("z_step", 2, 2),
        ("x_send", 1),
        ("z_step", 0, 1),
        ("x_send", 6, 0, 1),
        ("small", 2),
        ("z_step", 0, 2),
        ("close", 2),
        ("z_step", 3, 2),
        ("close", 0),
        ("z_step", 1, 0),
        ("x_send", 6, 1, 2),
        ("x_send", 6, 2, 3),
        ("z_step", 6, 0),
        ("z_step", 6, 1),
        ("z_step", 6, 2),
        ("x_send", 6, 3, 4),
        ("small", 3),
        ("z_step", 1, 1),
        ("close", 6),
        ("z_step", 1, 2),
        ("turn", 4),
        ("small", 4),
        ("close", 3),
        ("close", 5),
        ("close", 1),
        ("close", 4),
    ),
)


class Gather:
    def __init__(self, where, section, view, sems):
        self.where, self.section, self.view = where, section, view
        self.send_sem, self.recv_sem, self.core_send, self.core_recv = sems

    def ship(self, p, zz, xx, way, cond, wait):
        s, z, x, c = self.where
        i = zz * 2 + xx
        block = self.view(p, zz, xx, c)
        if way < 3:
            target = (
                device(s, clipped(z + 1), x, c),
                device(s, clipped(z - 1), x, c),
                device(s, z, 1 - x, c),
            )[way]
            cp = remote(block, block, self.send_sem.at[p, i, way], self.recv_sem.at[p, i], target)
        elif way == 3:
            cp = remote(block, block, self.core_send.at[p, i], self.core_recv.at[p, i], device(s, z, x, 1 - c))
        else:
            q = LENT if self.section == 0 else LENT_IN
            there = self.view(q, zz, xx, c)
            cp = remote(block, there, self.send_sem.at[p, i, 3], self.recv_sem.at[q, i], device(1 - s, z, x, c))
        act = cp.wait_send if wait else cp.start
        if cond is None:
            act()
        else:
            pl.when(cond)(act)

    def arrived(self, p, zz, xx):
        s, z, x, c = self.where
        block = self.view(p, zz, xx, c)
        i = zz * 2 + xx
        remote(block, block, self.send_sem.at[p, i, 0], self.recv_sem.at[p, i], device(s, z, 1 - x, c)).wait_recv()

    def own(self, p, wait=False):
        s, z, x, c = self.where
        ways = ((0, z < NZ - 1), (1, z > 0), (2, None), (3, None))
        if p == LENT:
            ways = ways[:3]
            if not wait:
                self.arrived(p, z, x)
        elif self.section == 0 and p == LENT_IN:
            ways = ((4, None), (3, None))
        for way, cond in ways:
            self.ship(p, z, x, way, cond, wait)

    def turn(self, p, wait=False):
        s, z, x, c = self.where
        if not wait:
            self.arrived(p, z, 1 - x)
        self.ship(p, z, 1 - x, 0, z < NZ - 1, wait)
        self.ship(p, z, 1 - x, 1, z > 0, wait)
        self.ship(p, z, 1 - x, 3, None, wait)

    def relay(self, p, d, signs=(-1, 1), wait=False):
        s, z, x, c = self.where
        turned = p == TURN_IN[self.section]
        for sign in signs:
            way = 0 if sign < 0 else 1
            zz = clipped(z + sign * d)
            here = inside(z + sign * d)
            for xx in (x, 1 - x) if turned else (x,):
                if not wait:
                    pl.when(here)(lambda zz=zz, xx=xx: self.arrived(p, zz, xx))
                self.ship(p, zz, xx, way, here & inside(z - sign), wait)
                if not turned:
                    self.ship(p, zz, xx, 2, here, wait)
                self.ship(p, zz, xx, 4 if p == LENT else 3, here, wait)

    def across(self, p, d, wait=False):
        s, z, x, c = self.where
        for sign in (-1, 1) if d else (1,):
            zz = clipped(z + sign * d)
            here = inside(z + sign * d)
            if not wait:
                pl.when(here)(lambda zz=zz: self.arrived(p, zz, 1 - x))
            self.ship(p, zz, 1 - x, 4 if p == LENT else 3, here, wait)

    def home(self, p, d, wait=False):
        s, z, x, c = self.where
        for sign in (-1, 1) if d else (1,):
            zz = clipped(z + sign * d)
            here = inside(z + sign * d)
            for xx in (x, 1 - x) if d else (1 - x,):
                if not wait:
                    pl.when(here)(lambda zz=zz, xx=xx: self.arrived(p, zz, xx))
                self.ship(p, zz, xx, 3, here, wait)

    def finish(self, p):
        s, z, x, c = self.where
        for zz in range(NZ):
            for xx in range(2):
                block = self.view(p, zz, xx, 1 - c)
                i = zz * 2 + xx
                remote(block, block, self.core_send.at[p, i], self.core_recv.at[p, i], device(s, z, x, 1 - c)).wait_recv()

    def drain(self, pieces):
        for step in GATHER_STEPS[self.section]:
            if step[0] not in ("finish", "stage", "hand") and step[1] in pieces:
                getattr(self, step[0])(*step[1:], wait=True)


def add_into(out, dst, terms):
    @pl.loop(0, dst.shape[0] // 16)
    def _(k):
        r = pl.ds(pl.multiple_of(k * 16, 16), 16)
        total = dst[r].astype(F32)
        for ref, cond in terms:
            value = ref[r].astype(F32)
            total = total + (value if cond is None else jnp.where(cond, value, 0.0))
        out[r] = total.astype(out.dtype)


def farthest_first(z, k):
    orders = ((3, 2, 1, 0), (3, 0, 2, 1), (0, 3, 1, 2), (0, 1, 2, 3))
    return jnp.where(
        z == 0, orders[0][k], jnp.where(z == 1, orders[1][k], jnp.where(z == 2, orders[2][k], orders[3][k]))
    )


class Scatter:
    def __init__(self, where, section, view, bufs, sems, store):
        self.where, self.section, self.view, self.store = where, section, view, store
        self.got_core, self.got_x, self.got_z, self.got_zz, self.got_home = bufs
        self.core_s, self.core_r, self.x_s, self.x_r, self.z_s, self.z_r, self.lend_s, self.lend_r, self.home_s, self.home_r = sems
        self.turned = TURN_OUT[section]
        left_out = (self.turned, LENT_OUT, LENT_SUM) if section == 0 else (self.turned,)
        self.straight = [p for p in range(PIECES + 1) if p not in left_out]

    def core_copy(self, p, i):
        s, z, x, c = self.where
        return remote(
            self.view(p, i // 2, i % 2, 1 - c),
            self.got_core.at[p, i],
            self.core_s.at[p, i],
            self.core_r.at[p, i],
            device(s, z, x, 1 - c),
        )

    def core_send(self, p):
        for i in range(2 * NZ):
            self.core_copy(p, i).start()

    def core_add(self, p):
        c = self.where[3]

        @pl.loop(0, 2 * NZ)
        def _(i):
            self.core_copy(p, i).wait_recv()
            dst = self.view(p, i // 2, i % 2, c)
            add_into(dst, dst, [(self.got_core.at[p, i], None)])

    def x_slot(self, p, zz):
        return self.got_x.at[PIECES * NZ if p == self.turned else self.straight.index(p) * NZ + zz]

    def x_copy(self, p, zz):
        s, z, x, c = self.where
        return remote(
            self.view(p, zz, 1 - x, c),
            self.x_slot(p, zz),
            self.x_s.at[p, zz],
            self.x_r.at[p, zz],
            device(s, z, 1 - x, c),
        )

    def lent_copy(self, zz, xx):
        s, z, x, c = self.where
        i = zz * 2 + xx
        dst = self.view(LENT_SUM, zz, xx, c)
        src = self.view(LENT_OUT, zz, xx, c) if self.section == 0 else dst
        return remote(src, dst, self.lend_s.at[i], self.lend_r.at[i], device(1 - s, z, x, c))

    def lend(self, side, wait=False):
        s, z, x, c = self.where
        xx = 1 - x if side == 0 else x

        for i in range(NZ):
            cp = self.lent_copy(farthest_first(z, i), xx)
            cp.wait_send() if wait else cp.start()

    def home_copy(self):
        s, z, x, c = self.where
        return remote(self.view(LENT_SUM, z, x, c), self.got_home, self.home_s.at[0], self.home_r.at[0], device(1 - s, z, x, c))

    def home(self):
        self.home_copy().wait_recv()
        self.store(LENT_OUT, self.got_home, [])

    def x_send(self, p, first=0, last=NZ):
        s, z, x, c = self.where
        for i in range(first, last):
            zz = farthest_first(z, i)
            if p == LENT_SUM:
                self.lent_copy(zz, 1 - x).wait_recv()
            self.x_copy(p, zz).start()

    def x_wait(self, p, zz):
        if p == LENT_SUM:
            self.lent_copy(zz, self.where[2]).wait_recv()
        self.x_copy(p, zz).wait_recv()
        return self.x_slot(p, zz), None

    def slot(self, p, k, xx):
        return self.got_zz.at[xx, k] if p == self.turned else self.got_z.at[self.straight.index(p), k]

    def z_copy(self, p, zz, xx, sign, k):
        s, z, x, c = self.where
        return remote(
            self.view(p, zz, xx, c),
            self.slot(p, k, xx),
            self.z_s.at[p, xx, zz],
            self.z_r.at[p, xx, k],
            device(s, clipped(z + sign), x, c),
        )

    def z_out(self, p, zz, xx, sign):
        k = jnp.where((sign < 0) & (self.where[1] + sign == zz), NZ, zz)
        return self.z_copy(p, zz, xx, sign, k)

    def cols(self, p):
        x = self.where[2]
        return (x, 1 - x) if p == self.turned else (x,)

    def z_wait(self, p, zz, xx, k, cond):
        pl.when(cond)(lambda: self.z_copy(p, zz, xx, 1, k).wait_recv())
        return self.slot(p, k, xx), cond

    def z_step(self, p, k):
        s, z, x, c = self.where
        zz = farthest_first(z, k)
        sign = jnp.where(zz > z, 1, -1)
        before = inside(z - sign)
        terms = [] if p == self.turned else [self.x_wait(p, zz)]
        for xx in self.cols(p):
            dst = self.view(p, zz, xx, c)
            add_into(dst, dst, terms + [self.z_wait(p, zz, xx, zz, before)])
            self.z_out(p, zz, xx, sign).start()

    def z_last(self, p, xx):
        z = self.where[1]
        return [self.z_wait(p, z, xx, z, z > 0), self.z_wait(p, z, xx, NZ, z < NZ - 1)]

    def turn(self, p):
        s, z, x, c = self.where
        dst = self.view(p, z, 1 - x, c)
        add_into(dst, dst, self.z_last(p, 1 - x))
        self.x_copy(p, z).start()

    def close(self, p):
        s, z, x, c = self.where
        dst = self.view(p, z, x, c)
        terms = [self.x_wait(p, z)] + self.z_last(p, x)
        if p == LENT_SUM:
            add_into(dst, dst, terms)
            self.home_copy().start()
        else:
            self.store(p, dst, terms)

    def drain(self):
        for p in range(PIECES):
            for i in range(2 * NZ):
                self.core_copy(p, i).wait_send()
        for p in self.straight + [self.turned]:
            self.drain_links(p)
        if self.section == 0:
            self.lend(0, True)
            self.lend(1, True)
        else:
            self.home_copy().wait_send()

    def drain_links(self, p):
        z = self.where[1]
        for i in range(NZ - 1):
            zz = farthest_first(z, i)
            if p != self.turned:
                self.x_copy(p, zz).wait_send()
            for xx in self.cols(p):
                self.z_out(p, zz, xx, jnp.where(zz > z, 1, -1)).wait_send()
        self.x_copy(p, z).wait_send()


def head_windows():
    for k in range(8):
        start = HD * k // 128 * 128
        offset = HD * k - start
        span = 128 if offset + HD <= 128 else 256
        yield k, start, offset, span


def layers_kernel(
    n,
    tokens,
    cotangent,
    lengths,
    norm_gains,
    query_gain,
    wq,
    wo,
    wu,
    wd,
    out_half,
    token_half,
    d_q,
    d_o,
    d_u,
    d_d,
    small_out,
    held,
    lent,
    gain_all,
    gain_rows,
    query_block,
    hb,
    a1,
    qf,
    qb,
    kb,
    vb,
    prob,
    ob,
    mid,
    a2,
    up,
    hid,
    grad,
    dup,
    dmid,
    low,
    dob,
    give,
    sums,
    swap,
    got_core,
    got_x,
    got_z,
    got_zz,
    got_home,
    *sems,
):
    where = s, z, x, c = place()
    rows, width = hb.shape
    slots = cotangent.shape[1]
    half = width // 2
    group = 8 * HD
    factor = LOG_BASE / math.sqrt(HD)
    g_sems, r_sems = sems[:4], sems[4:14]
    swap_s, swap_r, hand_s, hand_r, back_s, back_r, end_s, end_r, load_sem, out_sem = sems[14:]
    across_y = device(1 - s, z, x, c)

    def view(p, zz, xx, cc):
        if p == GAINS:
            return gain_all.at[zz * 4 + xx * 2 + cc]
        if p == LENT:
            return lent.at[zz * 2 + xx]
        return held.at[p, pl.ds(pl.multiple_of((zz * 4 + xx * 2 + cc) * n, 16), n)]

    def sum_view(p, zz, xx, cc):
        return view(LENT if p == LENT_SUM else p, zz, xx, cc)

    def staged(p):
        return (qf if p < 3 else mid).at[pl.ds(p % 3 * n, n)]

    def in_hbm(p, first, others):
        return first.at[:, pl.ds(p * width, width)] if p < 3 else others[p - 3]

    def store_copy(p):
        return pltpu.make_async_copy(staged(p), in_hbm(p, d_q, (d_o, d_u, d_d)), out_sem.at[p])

    def store(p, block, terms):
        add_into(staged(p), block, terms)
        store_copy(p).start()

    gathers = [Gather(where, k, view, g_sems) for k in range(2)]
    scatters = [
        Scatter(where, k, sum_view, (got_core, got_x, got_z, got_zz, got_home), r_sems, store) for k in range(2)
    ]


    def row_loop(fn):
        @pl.loop(0, rows // 32)
        def _(k):
            fn(pl.ds(pl.multiple_of(k * 32, 32), 32))

    def tiles(emit, value):
        for k in range(width // TILE):
            emit(slice(k * TILE, (k + 1) * TILE), value[:, k * TILE : (k + 1) * TILE])

    def project(p, a, emit, halves):
        if not halves:
            tiles(emit, jnp.dot(a[...], held[p], preferred_element_type=F32))
            return

        @pl.loop(0, 2)
        def _(k):
            lanes = pl.ds(pl.multiple_of(k * half, 128), half)
            emit(lanes, jnp.dot(a[...], held[p, :, lanes], preferred_element_type=F32))

    def project_back(pieces, emit):
        @pl.loop(0, 2)
        def _(k):
            lanes = pl.ds(pl.multiple_of(k * half, 128), half)
            total = None
            for p, a in pieces:
                term = contract_cols(a[...], held[p, lanes, :])
                total = term if total is None else total + term
            emit(lanes, total)

    def weight_grad(p, a, g):
        @pl.loop(0, 2)
        def _(k):
            lanes = pl.ds(pl.multiple_of(k * half, 128), half)
            held[p, lanes] = contract_rows(a[:, lanes], g[...]).astype(BF16)

    def recip_of(value):
        return lax.rsqrt(jnp.mean(value * value, -1, keepdims=True) + NORM_EPS)

    def norm(src, row, dst):
        def part(r):
            value = src[r].astype(F32)
            dst[r] = (value * recip_of(value) * gain_rows[row : row + 1]).astype(BF16)

        row_loop(part)

    def put(ref):
        def emit(lanes, value):
            ref[:, lanes] = value.astype(ref.dtype)

        return emit

    def emit_query(lanes, value):
        qf[:, lanes] = value
        qb[:, lanes] = (value * gain_rows[2:3, lanes]).astype(BF16)

    def emit_up(lanes, value):
        up[:, lanes] = value
        hid[:, lanes] = (value / (1.0 + jnp.exp(-value))).astype(BF16)

    def emit_mid(lanes, value):
        mid[:, lanes] = hb[:, lanes].astype(F32) + value

    def emit_out(lanes, value):
        give[:, lanes] = (mid[:, lanes] + value).astype(BF16)

    def lane_mask(offset, span):
        lane = lax.broadcasted_iota(jnp.int32, (1, span), 1)
        return ((lane >= offset) & (lane < offset + HD)).astype(F32).astype(BF16)

    def attention(body):
        @pl.loop(0, 2 * rows // slots)
        def _(it):
            seq, g = it // 2, it % 2
            r = pl.ds(pl.multiple_of(seq * slots, slots), slots)

            def window(ref, start, span):
                return ref[r, pl.ds(pl.multiple_of(g * group + start, 128), span)]

            body(it, seq, r, g, window)

    def spread(total, start, span, value):
        for j in range(span // 128):
            k = start // 128 + j
            term = value[:, j * 128 : (j + 1) * 128]
            total[k] = term if total[k] is None else total[k] + term

    def attend(it, seq, r, g, window):
        allowed = causal_allowed(slots, lengths[seq])
        total = [None] * (group // 128)
        for k, start, offset, span in head_windows():
            only = lane_mask(offset, span)
            scores = contract_cols(window(qb, start, span) * only, window(kb, start, span))
            scores = jnp.where(allowed, scores, NEG_FILL)
            expd = jnp.exp(scores - jnp.max(scores, -1, keepdims=True))
            probs = expd / jnp.sum(expd, -1, keepdims=True)
            prob[it, k] = probs
            value = jnp.dot(probs.astype(BF16), window(vb, start, span) * only, preferred_element_type=F32)
            spread(total, start, span, value)
        for k, value in enumerate(total):
            ob[r, pl.ds(pl.multiple_of(g * group + k * 128, 128), 128)] = value.astype(BF16)

    def attend_back(it, seq, r, g, window):
        count = group // 128
        t_q, t_k, t_v = [None] * count, [None] * count, [None] * count
        for k, start, offset, span in head_windows():
            only = lane_mask(offset, span)
            d_o_part = window(dob, start, span) * only
            probs = prob[it, k]
            d_probs = contract_cols(d_o_part, window(vb, start, span))
            spread(t_v, start, span, contract_rows(probs.astype(BF16), d_o_part))
            d_scores = probs * (d_probs - jnp.sum(probs * d_probs, -1, keepdims=True))
            d_scores = d_scores.astype(BF16)
            spread(t_q, start, span, jnp.dot(d_scores, window(kb, start, span) * only, preferred_element_type=F32))
            spread(t_k, start, span, contract_rows(d_scores, window(qb, start, span) * only))
        for k in range(count):
            lanes = pl.ds(pl.multiple_of(g * group + k * 128, 128), 128)
            products = t_q[k] * qf[r, lanes]
            sums[2, :, lanes] += jnp.sum(products.reshape(slots // 8, 8, 128), 0)
            qb[r, lanes] = (t_q[k] * gain_rows[2:3, lanes]).astype(BF16)
            kb[r, lanes] = t_k[k].astype(BF16)
            vb[r, lanes] = t_v[k].astype(BF16)

    def emit_dup(lanes, value):
        u = up[:, lanes]
        sig = 1.0 / (1.0 + jnp.exp(-u))
        dup[:, lanes] = (value * sig * (1.0 + u * (1.0 - sig))).astype(BF16)

    def norm_grad(row, src, base, emit):
        def part(r):
            value, d_normed = src[r].astype(F32), up[r]
            recip = recip_of(value)
            sums[row] += jnp.sum((d_normed * value * recip).reshape(4, 8, width), 0)
            emit(r, base[r].astype(F32) + norm_back(value, recip, d_normed * gain_rows[row : row + 1]))

        row_loop(part)

    def emit_dmid(r, value):
        dmid[r] = value
        low[r] = value.astype(BF16)

    def emit_give(r, value):
        give[r] = value.astype(BF16)

    def window_of(k, size):
        start = min(size * k // 128 * 128, width - 256)
        return start, size * k - start

    def rolled(block, shift):
        return pltpu.roll(block, shift, 1) if shift else block

    def spread_gains():
        gain_rows[...] = jnp.zeros_like(gain_rows)
        none = jnp.zeros((8, 128), F32)
        for f in range(4 * NZ):
            start, shift = window_of(f, n)
            gain_rows[:, start : start + 256] += rolled(jnp.concatenate([gain_all[f], none], -1), shift)
        value = query_block[...]
        scale = (jnp.maximum(value, 0.0) + jnp.log1p(jnp.exp(-jnp.abs(value)))) * factor
        lane = lax.broadcasted_iota(jnp.int32, (8, 128), 1)
        row = lax.broadcasted_iota(jnp.int32, (8, 128), 0)
        scale = jnp.where((lane < HD) & (row == 2), scale, 0.0)
        for k in range(H):
            start, shift = window_of(k, HD)
            gain_rows[:, start : start + 256] += rolled(jnp.concatenate([scale, none], -1), shift)

    def finish_small(value):
        me = z * 4 + x * 2 + c
        own = jnp.zeros((8, 128), F32)
        for f in range(4 * NZ):
            start, shift = window_of(f, n)
            part = rolled(value[:, start : start + 256], (256 - shift) % 256)[:, :128]
            own = own + jnp.where(me == f, part, 0.0)
        heads = jnp.zeros((8, 128), F32)
        for k in range(H):
            start, shift = window_of(k, HD)
            heads = heads + rolled(value[:, start : start + 256], (256 - shift) % 256)[:, :128]
        gate = factor / (1.0 + jnp.exp(-query_block[...]))
        row = lax.broadcasted_iota(jnp.int32, (8, 128), 0)
        small_out[...] = jnp.where(row == 2, heads * gate, own)

    def forward_stage(p, halves):
        if p == 0:
            spread_gains()
            norm(hb, 0, a1)
            project(0, a1, emit_query, halves)
        elif p == 1:
            project(1, a1, put(kb), halves)
        elif p == 2:
            project(2, a1, put(vb), halves)
            attention(attend)
        elif p == 3:
            project(3, ob, emit_mid, halves)
            norm(mid, 1, a2)
        elif p == 4:
            project(4, a2, emit_up, halves)
        else:
            project(5, hid, emit_out, halves)


    def hand(k):
        r = pl.ds(k * slots, slots)
        return remote(give.at[r], hb.at[r], hand_s.at[k], hand_r.at[k], across_y)

    def back(k):
        r = pl.ds(k * slots, slots)
        return remote(give.at[r], grad.at[r], back_s.at[k], back_r.at[k], across_y)

    def end(which):
        dst, col = ((out_half, 0), (token_half, half))[which]
        return remote(give.at[:, col : col + half], dst, end_s.at[which], end_r.at[which], across_y)


    def load(act):
        for k in range(rows // slots):
            r = pl.ds(k * slots, slots)
            here = pltpu.make_async_copy(tokens.at[k], hb.at[r], load_sem.at[k])
            there = pltpu.make_async_copy(cotangent.at[k], grad.at[r], load_sem.at[k])
            pl.when(s == 0)(getattr(here, act))
            pl.when(s == 1)(getattr(there, act))
        for p in range(PIECES):
            cp = pltpu.make_async_copy(in_hbm(p, wq, (wo, wu, wd)), staged(p), load_sem.at[rows // slots + p])
            getattr(cp, act)()

    load("start")
    me = z * 4 + x * 2 + c
    gain_all[me] = jnp.zeros((8, 128), F32)
    gain_all[me, 0:2, 0:n] = norm_gains[...].astype(BF16).astype(F32)
    query_block[...] = jnp.zeros_like(query_block)
    query_block[:, 0:HD] = jnp.broadcast_to(query_gain[...], (8, HD))
    sums[...] = jnp.zeros_like(sums)
    neighbour_barrier(s, z, x, c)
    load("wait")
    mine = pl.ds(pl.multiple_of((z * 4 + x * 2 + c) * n, 16), n)
    for p in range(PIECES):
        held[p, mine] = staged(p)[...].astype(BF16)

    def forward(section):
        for step in GATHER_STEPS[section]:
            if step[0] == "stage":
                forward_stage(step[1], True)
            elif step[0] == "hand":
                for k in range(rows // slots):
                    hand(k).wait_recv()
            else:
                getattr(gathers[section], step[0])(*step[1:])

    def hand_start():
        for k in range(rows // slots):
            hand(k).start()

    @pl.when(s == 0)
    def _():
        forward(0)
        hand_start()
        gathers[0].drain(range(LENT + 1))
        for k in range(rows // slots):
            hand(k).wait_send()
            back(k).wait_recv()

    @pl.when(s == 1)
    def _():
        forward(1)
        end(0).start()
        gathers[1].drain((LENT, 5))
        out_half[...] = give[:, half:]
        for k in range(rows // slots):
            row = lax.broadcasted_iota(jnp.int32, (slots, 1), 0)
            live = (row < lengths[k]).astype(F32)
            part = pl.ds(k * slots, slots)
            grad[part] = (grad[part].astype(F32) * live).astype(BF16)

    grads = ((a1, qb), (a1, kb), (a1, vb), (ob, low), (a2, dup), (hid, grad))

    def exchange(k):
        partner = (
            device(s, z, x, 1 - c),
            device(s, z, 1 - x, c),
            device(s, z + 1 - 2 * (z % 2), x, c),
            device(s, (z + 2) % NZ, x, c),
        )[k]
        return remote(swap.at[k, 0], swap.at[k, 1], swap_s.at[k], swap_r.at[k], partner)

    def small(k):
        if k == 0:
            totals = [jnp.sum(sums[i], 0, keepdims=True) for i in range(3)]
            swap[0, 0] = jnp.concatenate(totals + [jnp.zeros((5, width), F32)], 0)
            exchange(0).start()
            return
        exchange(k - 1).wait_recv()
        value = swap[k - 1, 0] + swap[k - 1, 1]
        if k < 4:
            swap[k, 0] = value
            exchange(k).start()
        else:
            finish_small(value)

    def finish_input(section):
        if section == 1:
            end(0).wait_send()
        norm_grad(0, hb, dmid, emit_give)
        if section == 1:
            for k in range(rows // slots):
                back(k).start()
            gathers[1].drain((0, 1, 2, 3, 4, GAINS))
        else:
            end(1).start()
            token_half[...] = give[:, :half]

    compute = dict(
        hidden=lambda section: project_back([(5, grad)], emit_dup),
        normed_two=lambda section: project_back([(4, dup)], put(up)),
        middle=lambda section: norm_grad(1, mid, grad, emit_dmid),
        attended=lambda section: project_back([(3, low)], put(dob)),
        heads=lambda section: attention(attend_back),
        normed=lambda section: project_back([(0, qb), (1, kb), (2, vb)], put(up)),
        input=finish_input,
        weight=lambda section, p: weight_grad(p, *grads[p]),
        small=lambda section, k: small(k),
    )

    def backward(section):
        for step in BACKWARD_STEPS[section]:
            if step[0] in compute:
                compute[step[0]](section, *step[1:])
            else:
                getattr(scatters[section], step[0])(*step[1:])

    pl.when(s == 0)(lambda: backward(0))
    pl.when(s == 1)(lambda: backward(1))
    pl.when(s == 0)(scatters[0].drain)
    pl.when(s == 1)(scatters[1].drain)
    for p in range(PIECES):
        store_copy(p).wait()
    for k in range(4):
        exchange(k).wait_send()

    @pl.when(s == 0)
    def _():
        end(1).wait_send()
        end(0).wait_recv()

    @pl.when(s == 1)
    def _():
        for k in range(rows // slots):
            back(k).wait_send()
        end(1).wait_recv()


def finish_kernel(small, *refs):
    froms, tos, (d_gains, d_query), held, (in_sem, out_sem) = refs[:6], refs[6:12], refs[12:14], refs[14:20], refs[20:]
    ins = [pltpu.make_async_copy(a, h, in_sem.at[k]) for k, (a, h) in enumerate(zip(froms, held))]
    outs = [pltpu.make_async_copy(h, b, out_sem.at[k]) for k, (h, b) in enumerate(zip(held, tos))]
    for cp in ins:
        cp.start()
    d_gains[...] = small[0:2, : d_gains.shape[1]]
    d_query[...] = small[2:3, :HD]
    for came, goes in zip(ins, outs):
        came.wait()
        goes.start()
    for cp in outs:
        cp.wait()


def near_shards(
    tokens, cotangent, lengths, qkv_weight, out_weight, up_weight, down_weight, norm_gains, query_gain
):
    n, width = out_weight.shape
    count, slots, _ = tokens.shape
    rows = count * slots
    dma = pltpu.SemaphoreType.DMA
    whole = pl.BlockSpec(memory_space=pltpu.VMEM)
    far = pl.BlockSpec(memory_space=pl.ANY)
    block = (n, width)
    low_rows = pltpu.VMEM((rows, width), BF16)
    wide_rows = pltpu.VMEM((rows, width), F32)
    scratch = dict(
        held=pltpu.VMEM((PIECES, 4 * NZ * n, width), BF16),
        lent=pltpu.VMEM((2 * NZ,) + block, BF16),
        gain_all=pltpu.VMEM((4 * NZ, 8, 128), F32),
        gain_rows=pltpu.VMEM((8, width), F32),
        query_block=pltpu.VMEM((8, 128), F32),
        hb=low_rows,
        a1=low_rows,
        qf=wide_rows,
        qb=low_rows,
        kb=low_rows,
        vb=low_rows,
        prob=pltpu.VMEM((2 * count, 8, slots, slots), F32),
        ob=low_rows,
        mid=wide_rows,
        a2=low_rows,
        up=wide_rows,
        hid=low_rows,
        grad=low_rows,
        dup=low_rows,
        dmid=wide_rows,
        low=low_rows,
        dob=low_rows,
        give=low_rows,
        sums=pltpu.VMEM((3, 8, width), F32),
        swap=pltpu.VMEM((4, 2, 8, width), F32),
        got_core=pltpu.VMEM((PIECES, 2 * NZ) + block, BF16),
        got_x=pltpu.VMEM((PIECES * NZ + 1,) + block, BF16),
        got_z=pltpu.VMEM((PIECES, NZ + 1) + block, BF16),
        got_zz=pltpu.VMEM((2, NZ + 1) + block, BF16),
        got_home=pltpu.VMEM(block, BF16),
    )
    pieces = PIECES + 2
    semaphores = [
        dma((pieces, 2 * NZ, 4)),
        dma((pieces, 2 * NZ)),
        dma((pieces, 2 * NZ)),
        dma((pieces, 2 * NZ)),
        dma((PIECES, 2 * NZ)),
        dma((PIECES, 2 * NZ)),
        dma((PIECES + 1, NZ)),
        dma((PIECES + 1, NZ)),
        dma((PIECES + 1, 2, NZ)),
        dma((PIECES + 1, 2, NZ + 1)),
        dma((2 * NZ,)),
        dma((2 * NZ,)),
        dma((1,)),
        dma((1,)),
        dma((4,)),
        dma((4,)),
        dma((count,)),
        dma((count,)),
        dma((count,)),
        dma((count,)),
        dma((2,)),
        dma((2,)),
        dma((count + PIECES,)),
        dma((PIECES,)),
    ]
    half = jax.ShapeDtypeStruct((rows, width // 2), BF16)
    square = jax.ShapeDtypeStruct(block, F32)
    shapes = (half, half, jax.ShapeDtypeStruct((n, 3 * width), F32), square, square, square)
    *results, small = pl.pallas_call(
        lambda *refs: layers_kernel(n, *refs),
        out_shape=shapes + (jax.ShapeDtypeStruct((8, 128), F32),),
        in_specs=[far, far, pl.BlockSpec(memory_space=pltpu.SMEM), whole, whole] + [far] * 4,
        out_specs=(whole, whole) + (far,) * 4 + (whole,),
        scratch_shapes=list(scratch.values()) + semaphores,
        compiler_params=pltpu.CompilerParams(
            collective_id=1, has_side_effects=True, vmem_limit_bytes=63 << 20
        ),
        name="two_layers",
    )(tokens, cotangent, lengths, norm_gains.T, query_gain, qkv_weight, out_weight, up_weight, down_weight)
    out, d_tokens, d_q, d_o, d_u, d_d, d_gains, d_query = pl.pallas_call(
        finish_kernel,
        out_shape=shapes + (jax.ShapeDtypeStruct((2, n), F32), jax.ShapeDtypeStruct((1, HD), F32)),
        in_specs=[whole] + [far] * 6,
        out_specs=(far,) * 6 + (whole,) * 2,
        scratch_shapes=[pltpu.VMEM(item.shape, item.dtype) for item in shapes] + [dma((6,)), dma((6,))],
        compiler_params=pltpu.CompilerParams(vmem_limit_bytes=63 << 20),
        name="results",
    )(small, *results)
    shape = (count, slots, width // 2)
    return (
        out.reshape(shape),
        d_tokens.reshape(shape),
        d_q[None],
        d_o[None],
        d_u[None],
        d_d[None],
        d_gains.T[None],
        d_query,
    )


def swapped(value, axis, bit):
    return lax.ppermute(value, axis, [(i, i ^ 1 << bit) for i in range(lax.axis_size(axis))])


def causal_allowed(row_count, length):
    row_ids = lax.broadcasted_iota(jnp.int32, (row_count, row_count), 0)
    col_ids = lax.broadcasted_iota(jnp.int32, (row_count, row_count), 1)
    return (col_ids <= row_ids) & (col_ids < length)


def contract_rows(left, right):
    return lax.dot_general(
        left, right, (((0,), (0,)), ((), ())), preferred_element_type=jnp.float32
    )


def contract_cols(left, right):
    return lax.dot_general(
        left, right, (((1,), (1,)), ((), ())), preferred_element_type=jnp.float32
    )


def norm_back(source, recip, grad_flat):
    return recip * grad_flat - source * recip**3 * jnp.mean(grad_flat * source, -1, keepdims=True)


def layer_forward(layer_input, length, weights, query_scale):
    qkv_w, out_w, up_w, down_w, gain_pair = weights
    row_count, width = layer_input.shape
    gain_one = gain_pair[:, 0].astype(jnp.float32)
    gain_two = gain_pair[:, 1].astype(jnp.float32)
    recip_one = lax.rsqrt(jnp.mean(layer_input * layer_input, -1, keepdims=True) + NORM_EPS)
    normed = (layer_input * recip_one * gain_one).astype(jnp.bfloat16)
    proj = jnp.dot(normed, qkv_w, preferred_element_type=jnp.float32)
    query = proj[:, :width].reshape(row_count, H, HD)
    query_b = (query * query_scale).astype(jnp.bfloat16)
    keys_b = proj[:, width : 2 * width].astype(jnp.bfloat16).reshape(row_count, H, HD)
    values_b = proj[:, 2 * width :].astype(jnp.bfloat16).reshape(row_count, H, HD)
    scores = jnp.einsum("qhd,khd->hqk", query_b, keys_b, preferred_element_type=jnp.float32)
    scores = jnp.where(causal_allowed(row_count, length)[None], scores, NEG_FILL)
    row_peak = jnp.max(scores, -1, keepdims=True)
    expd = jnp.exp(scores - row_peak)
    row_total = jnp.sum(expd, -1, keepdims=True)
    probs = expd / row_total
    logsum = (row_peak + jnp.log(row_total))[..., 0]
    attended = (
        jnp.einsum(
            "hqk,khd->qhd", probs.astype(jnp.bfloat16), values_b, preferred_element_type=jnp.float32
        )
        .reshape(row_count, width)
        .astype(jnp.bfloat16)
    )
    middle = layer_input + jnp.dot(attended, out_w, preferred_element_type=jnp.float32)
    recip_two = lax.rsqrt(jnp.mean(middle * middle, -1, keepdims=True) + NORM_EPS)
    normed_two = (middle * recip_two * gain_two).astype(jnp.bfloat16)
    upper = jnp.dot(normed_two, up_w, preferred_element_type=jnp.float32)
    hidden = jax.nn.silu(upper).astype(jnp.bfloat16)
    layer_output = middle + jnp.dot(hidden, down_w, preferred_element_type=jnp.float32)
    saved = (
        layer_input,
        normed,
        query,
        query_b,
        keys_b,
        values_b,
        logsum,
        attended,
        middle,
        normed_two,
        upper,
        hidden,
        recip_one,
        recip_two,
    )
    return (layer_output, saved)


def layer_backward(saved, length, weights, query_scale, grad_output):
    qkv_w, out_w, up_w, down_w, gain_pair = weights
    (
        layer_input,
        normed,
        query,
        query_b,
        keys_b,
        values_b,
        logsum,
        attended,
        middle,
        normed_two,
        upper,
        hidden,
        recip_one,
        recip_two,
    ) = saved
    row_count, width = layer_input.shape
    gain_one = gain_pair[:, 0].astype(jnp.float32)
    gain_two = gain_pair[:, 1].astype(jnp.float32)
    grad_low = grad_output.astype(jnp.bfloat16)
    d_down = contract_rows(hidden, grad_low)
    d_hidden = contract_cols(grad_low, down_w)
    sigmoid_up = jax.nn.sigmoid(upper)
    d_upper = (d_hidden * sigmoid_up * (1.0 + upper * (1.0 - sigmoid_up))).astype(jnp.bfloat16)
    d_up = contract_rows(normed_two, d_upper)
    d_normed_two = contract_cols(d_upper, up_w)
    d_gain_two = jnp.sum(d_normed_two * middle * recip_two, 0)
    d_middle = grad_output + norm_back(middle, recip_two, d_normed_two * gain_two)
    middle_low = d_middle.astype(jnp.bfloat16)
    d_out = contract_rows(attended, middle_low)
    d_attended = contract_cols(middle_low, out_w).astype(jnp.bfloat16).reshape(row_count, H, HD)
    scores = jnp.einsum("qhd,khd->hqk", query_b, keys_b, preferred_element_type=jnp.float32)
    scores = jnp.where(causal_allowed(row_count, length)[None], scores, NEG_FILL)
    probs = jnp.exp(scores - logsum[..., None])
    d_probs = jnp.einsum("qhd,khd->hqk", d_attended, values_b, preferred_element_type=jnp.float32)
    d_values = jnp.einsum(
        "hqk,qhd->khd", probs.astype(jnp.bfloat16), d_attended, preferred_element_type=jnp.float32
    ).astype(jnp.bfloat16)
    d_scores = (probs * (d_probs - jnp.sum(probs * d_probs, -1, keepdims=True))).astype(
        jnp.bfloat16
    )
    d_query_s = jnp.einsum("hqk,khd->qhd", d_scores, keys_b, preferred_element_type=jnp.float32)
    d_keys = jnp.einsum(
        "hqk,qhd->khd", d_scores, query_b, preferred_element_type=jnp.float32
    ).astype(jnp.bfloat16)
    d_scale = jnp.sum(d_query_s * query, (0, 1))
    d_query = (d_query_s * query_scale).astype(jnp.bfloat16)
    d_proj = jnp.concatenate(
        [
            d_query.reshape(row_count, width),
            d_keys.reshape(row_count, width),
            d_values.reshape(row_count, width),
        ],
        -1,
    )
    d_qkv = contract_rows(normed, d_proj)
    d_normed = contract_cols(d_proj, qkv_w)
    d_gain_one = jnp.sum(d_normed * layer_input * recip_one, 0)
    d_input = d_middle + norm_back(layer_input, recip_one, d_normed * gain_one)
    d_gains = jnp.stack([d_gain_one, d_gain_two], -1)
    return (d_input, (d_qkv, d_out, d_up, d_down, d_gains), d_scale)


def shards(
    tokens,
    cotangent,
    lengths,
    qkv_weight,
    out_weight,
    up_weight,
    down_weight,
    norm_gains,
    query_gain,
):
    if lax.axis_size("fsdp") == 4 * NZ:
        return near_shards(
            tokens,
            cotangent,
            lengths,
            qkv_weight[0],
            out_weight[0],
            up_weight[0],
            down_weight[0],
            norm_gains[0],
            query_gain,
        )
    section_index = lax.axis_index("section")
    micro_count, slot_rows, width = tokens.shape
    half_width = width // 2
    scale_factor = LOG_BASE / math.sqrt(HD)
    query_scale = jax.nn.softplus(query_gain[0]) * scale_factor

    def gather_weights():
        pieces = (
            lax.all_gather(qkv_weight.astype(jnp.bfloat16), "fsdp", axis=1, tiled=True),
            lax.all_gather(out_weight.astype(jnp.bfloat16), "fsdp", axis=1, tiled=True),
            lax.all_gather(up_weight.astype(jnp.bfloat16), "fsdp", axis=1, tiled=True),
            lax.all_gather(down_weight.astype(jnp.bfloat16), "fsdp", axis=1, tiled=True),
            lax.all_gather(norm_gains.astype(jnp.bfloat16), "fsdp", axis=1, tiled=True),
        )
        return tuple((piece[0] for piece in pieces))

    def handoff(value):
        return swapped(value, "section", 0)

    weights = gather_weights()
    received = jnp.zeros((slot_rows, width), jnp.bfloat16)
    kept = []
    result_parts = []
    for tick_index in range(micro_count + 1):
        first_input = tokens[min(tick_index, micro_count - 1)].astype(jnp.float32)
        layer_input = jnp.where(section_index == 0, first_input, received.astype(jnp.float32))
        micro_index = jnp.clip(tick_index - section_index, 0, micro_count - 1)
        length = lengths[micro_index]
        layer_output, saved = layer_forward(layer_input, length, weights, query_scale)
        sent = layer_output.astype(jnp.bfloat16)
        received = handoff(sent)
        kept.append(saved)
        if tick_index >= 1:
            finished = jnp.where(section_index == 1, sent, received)
            result_parts.append(
                lax.dynamic_slice_in_dim(finished, section_index * half_width, half_width, 1)
            )
    output = jnp.stack(result_parts)
    weights = gather_weights()
    row_ids = lax.iota(jnp.int32, slot_rows)
    grad_received = jnp.zeros((slot_rows, width), jnp.bfloat16)
    grad_parts = []
    grad_totals = None
    scale_total = jnp.zeros((HD,), jnp.float32)
    for tick_index in range(micro_count + 1):
        offset = tick_index - 1 + section_index
        micro_index = jnp.clip(offset, 0, micro_count - 1)
        length = lengths[micro_index]
        live_tick = ((offset >= 0) & (offset < micro_count)).astype(jnp.float32)
        live_rows = (row_ids < length).astype(jnp.float32)[:, None]
        top_grad = cotangent[min(tick_index, micro_count - 1)].astype(jnp.float32) * live_rows
        grad_output = jnp.where(section_index == 1, top_grad, grad_received.astype(jnp.float32))
        saved = jax.tree.map(
            lambda early, late: jnp.where(section_index == 0, early, late),
            kept[max(tick_index - 1, 0)],
            kept[min(tick_index + 1, micro_count)],
        )
        d_input, weight_grads, scale_grad = layer_backward(
            saved, length, weights, query_scale, grad_output
        )
        weight_grads = tuple((item * live_tick for item in weight_grads))
        scale_total = scale_total + scale_grad * live_tick
        sent = d_input.astype(jnp.bfloat16)
        grad_received = handoff(sent)
        if tick_index >= 1:
            finished = jnp.where(section_index == 0, sent, grad_received)
            grad_parts.append(
                lax.dynamic_slice_in_dim(finished, section_index * half_width, half_width, 1)
            )
        if grad_totals is None:
            grad_totals = weight_grads
        else:
            grad_totals = tuple((total + piece for total, piece in zip(grad_totals, weight_grads)))
    d_tokens = jnp.stack(grad_parts)
    scattered = (
        lax.psum_scatter(grad_totals[0], "fsdp", scatter_dimension=0, tiled=True),
        lax.psum_scatter(grad_totals[1], "fsdp", scatter_dimension=0, tiled=True),
        lax.psum_scatter(grad_totals[2], "fsdp", scatter_dimension=0, tiled=True),
        lax.psum_scatter(grad_totals[3], "fsdp", scatter_dimension=0, tiled=True),
        lax.psum_scatter(grad_totals[4], "fsdp", scatter_dimension=0, tiled=True),
    )
    owned = tuple((item[None] for item in scattered))
    scale_sum = lax.psum(scale_total, "fsdp")
    d_query_gain = (scale_sum * jax.nn.sigmoid(query_gain[0]) * scale_factor)[None]
    return (output, d_tokens, owned[0], owned[1], owned[2], owned[3], owned[4], d_query_gain)


def solution(mesh):
    in_specs = (
        P("fsdp", None, None),
        P("fsdp", None, None),
        P("fsdp"),
        P("section", "fsdp", None),
        P("section", "fsdp", None),
        P("section", "fsdp", None),
        P("section", "fsdp", None),
        P("section", "fsdp", None),
        P("section", None),
    )
    out_specs = (
        P("fsdp", None, "section"),
        P("fsdp", None, "section"),
        P("section", "fsdp", None),
        P("section", "fsdp", None),
        P("section", "fsdp", None),
        P("section", "fsdp", None),
        P("section", "fsdp", None),
        P("section", None),
    )
    return jax.shard_map(shards, mesh=mesh, in_specs=in_specs, out_specs=out_specs, check_vma=False)
```
